32 devices in a mesh: dp: 4 (over x, core), space: 8 (over z, y).
Axes of the slice: x: 2, y: 2, z: 4, core: 2. Of those that a mesh axis runs over, the one named last changes fastest.
Arguments:
- field: bfloat16 [4, 32, 32, 16, 128], P('dp', 'space'), may hold values from -6 to 6
- cotangent: bfloat16 [4, 32, 32, 16, 128], P('dp', 'space'), may hold values from -6 to 6
- weights: float32 [16, 128, 2, 128, 128], P('space', 'dp'), may hold values from -0.375 to 0.375
- first_moment: float32 [16, 128, 2, 128, 128], P('space', 'dp'), may hold values from -6 to 6
- second_moment: float32 [16, 128, 2, 128, 128], P('space', 'dp'), may hold values from 0.01 to 10
Outputs:
- field_grad: bfloat16 [4, 32, 32, 16, 128], P('dp', 'space')
- new_weights: float32 [16, 128, 2, 128, 128], P('space', 'dp')
- new_first: float32 [16, 128, 2, 128, 128], P('space', 'dp')
- new_second: float32 [16, 128, 2, 128, 128], P('space', 'dp')
The draws below stay inside these ranges and needn't reach their ends.
All inputs are finite; a program needn't handle non-finite values.
Results may differ from the reference program's by a relative error of at most 0.024.
Values may be sent and summed in bfloat16 or wider, within the bound.
No kernel may reach another device: no remote copies, remote signals or barrier semaphores. Data moves between devices by JAX's collectives and lax.ppermute only.
A program may use at most 128 MiB of HBM per device.

```python
import math
import jax
import jax.numpy as jnp
from jax import lax

C = 128
MX = 16
MY = 16
MZ = 8
NY = 32
NZ = 16
STEP = 100
MYZ = 128
NX = 32
BATCH = 4


def block_levels(rng, dims, split, low, high):
    level, own = 1.0, jax.random.fold_in(rng, 6)
    for dim, parts in split:
        draws = jnp.exp(jax.random.uniform(jax.random.fold_in(own, dim), (parts,), jnp.float32, low / len(split), high / len(split)))
        level = level * jnp.repeat(draws, dims[dim] // parts).reshape([-1 if axis == dim else 1 for axis in range(len(dims))])
    return level


def normal_values(own_key, dims, deviation, bound, split=(), kind=jnp.bfloat16):
    gain = block_levels(own_key, dims, split, -0.22, 0.18) if split else 1.0
    entries = jax.random.normal(own_key, dims, jnp.float32) * deviation * gain
    return jnp.minimum(jnp.maximum(entries, -bound), bound).astype(kind)


def setup_inputs(seed: int = 0) -> dict:
    key_list = jax.random.split(jax.random.key(seed), 6)
    return {
        "field": normal_values(key_list[0], (BATCH, NX, NY, NZ, C), 1.0, 6.0, ((0, 4), (1, 8))),
        "cotangent": normal_values(key_list[1], (BATCH, NX, NY, NZ, C), 1.0, 6.0, ((0, 4), (1, 8))),
        "weights": normal_values(key_list[2], (MX, MYZ, 2, C, C), (2 * C) ** -0.5, 0.375, ((0, 8), (1, 4)), jnp.float32),
        "first_moment": normal_values(key_list[3], (MX, MYZ, 2, C, C), 1.0, 6.0, ((0, 8), (1, 4)), jnp.float32),
        "second_moment": jnp.clip(jnp.exp(math.log(10.0) - 6.9077553 * jax.random.uniform(key_list[4], (MX, MYZ, 2, C, C), jnp.float32) ** block_levels(key_list[4], (MX, MYZ, 2, C, C), ((0, 8), (1, 4)), -0.2, 0.2)), 0.01, 10.0),
    }


decay_first = 0.9
decay_second = 0.999
learn_rate = 0.001
adam_floor = 1e-08

def round_half(values):
    return lax.optimization_barrier(values.astype(jnp.bfloat16))

def trig_tables(length, modes_kept, signed):
    points = jnp.arange(length, dtype=jnp.int32)
    frequency = jnp.arange(modes_kept, dtype=jnp.int32) - (modes_kept // 2 if signed else 0)
    phases = jnp.mod(points[:, None] * frequency[None, :], length).astype(jnp.float32)
    angles = phases * (2.0 * math.pi / length)
    factor = 1.0 / math.sqrt(length)
    return ((jnp.cos(angles) * factor).astype(jnp.bfloat16), (jnp.sin(angles) * factor).astype(jnp.bfloat16))

def forward_table(cosine, sine_part):
    real_row = jnp.stack([cosine, -sine_part], axis=-1)
    imag_row = jnp.stack([sine_part, cosine], axis=-1)
    return jnp.stack([real_row, imag_row], axis=1)

def inverse_table(cosine, sine_part):
    real_row = jnp.stack([cosine.T, sine_part.T], axis=-1)
    imag_row = jnp.stack([-sine_part.T, cosine.T], axis=-1)
    return jnp.stack([real_row, imag_row], axis=1)

def adam_update(weights, first_moment, second_moment, weight_grads):
    new_first = decay_first * first_moment + (1.0 - decay_first) * weight_grads
    new_second = decay_second * second_moment + (1.0 - decay_second) * weight_grads * weight_grads
    first_hat = new_first / (1.0 - decay_first ** STEP)
    second_hat = new_second / (1.0 - decay_second ** STEP)
    new_weights = weights - learn_rate * first_hat / (jnp.sqrt(second_hat) + adam_floor)
    return (new_weights, new_first, new_second)

def reference(field, cotangent, weights, first_moment, second_moment):
    f32 = jnp.float32
    cos_z, sin_z = trig_tables(NZ, MZ, False)
    cos_y, sin_y = trig_tables(NY, MY, True)
    cos_x, sin_x = trig_tables(NX, MX, True)
    table_z = jnp.stack([cos_z, -sin_z], axis=1).astype(f32)
    table_y = forward_table(cos_y, sin_y).astype(f32)
    table_x = forward_table(cos_x, sin_x).astype(f32)
    back_table_x = inverse_table(cos_x, sin_x).astype(f32)
    back_table_y = inverse_table(cos_y, sin_y).astype(f32)
    back_table_z = jnp.stack([cos_z.T, -sin_z.T], axis=0).astype(f32)

    def to_modes(sample):
        first_pass = round_half(jnp.einsum('xyzc,zpk->xypkc', sample.astype(f32), table_z))
        second = round_half(jnp.einsum('xypkc,ypmq->xmkqc', first_pass.astype(f32), table_y))
        second = second.reshape(NX, MY * MZ, 2, C)
        return round_half(jnp.einsum('xpjc,xjmq->mpqc', second.astype(f32), table_x))
    field_hat = lax.map(to_modes, field).astype(f32)
    cot_hat = lax.map(to_modes, cotangent).astype(f32)
    rotated = jnp.stack([cot_hat[..., 1, :], -cot_hat[..., 0, :]], axis=-2)
    grad_real = jnp.einsum('bmpjc,bmpjo->mpco', field_hat, cot_hat)
    grad_imag = jnp.einsum('bmpjc,bmpjo->mpco', field_hat, rotated)
    weight_grads = jnp.stack([grad_real, grad_imag], axis=2)
    half_weights = round_half(weights).astype(f32)
    back_real = jnp.einsum('mpjio,bmpjo->bmpi', half_weights, cot_hat)
    back_imag = jnp.einsum('mpjio,bmpjo->bmpi', half_weights, rotated)
    mode_grads = round_half(jnp.stack([back_real, back_imag], axis=3))

    def to_field(sample_modes):
        back_x = round_half(jnp.einsum('mpjc,mjxq->xpqc', sample_modes.astype(f32), back_table_x))
        back_x = back_x.reshape(NX, MY, MZ, 2, C)
        back_y = round_half(jnp.einsum('xmkjc,mjyq->xyqkc', back_x.astype(f32), back_table_y))
        return jnp.einsum('xyqkc,qkz->xyzc', back_y.astype(f32), back_table_z).astype(jnp.bfloat16)
    field_grad = lax.map(to_field, mode_grads)
    new_weights, new_first, new_second = adam_update(weights, first_moment, second_moment, weight_grads)
    return (field_grad, new_weights, new_first, new_second)
```

```python
import functools
import math

import jax
import jax.numpy as jnp
import ml_dtypes
import numpy as np
from jax import lax
from jax.experimental import pallas as pl
from jax.experimental.pallas import tpu as pltpu
from jax.sharding import PartitionSpec as P

C = 128
MX = 16
MY = 16
MZ = 8
NY = 32
NZ = 16
STEP = 100
MYZ = 128
QUAD = 4


decay_first = 0.9
decay_second = 0.999
learn_rate = 0.001
adam_floor = 1e-08

f32 = jnp.float32
half = jnp.bfloat16


def np_tables(length, modes_kept, signed):
    points = np.arange(length)
    frequency = np.arange(modes_kept) - (modes_kept // 2 if signed else 0)
    angles = np.mod(points[:, None] * frequency[None, :], length) * (2.0 * math.pi / length)
    factor = np.float32(1.0 / math.sqrt(length))
    cosine = (np.cos(angles).astype(np.float32) * factor).astype(ml_dtypes.bfloat16)
    sine = (np.sin(angles).astype(np.float32) * factor).astype(ml_dtypes.bfloat16)
    return cosine.astype(np.float64), sine.astype(np.float64)


def yz_table(dp_count):
    cos_z, sin_z = np_tables(NZ, MZ, False)
    cos_y, sin_y = np_tables(NY, MY, True)
    cy, sy = cos_y.T[:, None, :, None], sin_y.T[:, None, :, None]
    cz, sz = cos_z.T[None, :, None, :], sin_z.T[None, :, None, :]
    real = cy * cz - sy * sz
    imag = -(sy * cz + cy * sz)
    table = np.stack([real, imag], axis=2).reshape(MYZ, 2, NY * NZ)
    pencils = MYZ // dp_count // QUAD
    table = table.reshape(dp_count, QUAD, pencils, 2, NY * NZ).transpose(1, 0, 2, 3, 4)
    return table.reshape(QUAD, dp_count * pencils * 2, NY * NZ).astype(ml_dtypes.bfloat16)


def x_tables(total_x, halves, pencils):
    cos_x, sin_x = np_tables(total_x, MX, True)
    same = np.eye(pencils)
    span = total_x // halves
    forward, backward = [], []
    for part in range(halves):
        c, s = cos_x[part * span : (part + 1) * span], sin_x[part * span : (part + 1) * span]
        fwd = np.zeros((MX, pencils, 2, span, pencils, 2))
        fwd[:, :, 0, :, :, 0] = np.einsum("xm,pr->mpxr", c, same)
        fwd[:, :, 0, :, :, 1] = np.einsum("xm,pr->mpxr", s, same)
        fwd[:, :, 1, :, :, 0] = np.einsum("xm,pr->mpxr", -s, same)
        fwd[:, :, 1, :, :, 1] = np.einsum("xm,pr->mpxr", c, same)
        bwd = np.zeros((span, pencils, 2, MX, pencils, 2))
        bwd[:, :, 0, :, :, 0] = np.einsum("xm,pr->xpmr", c, same)
        bwd[:, :, 0, :, :, 1] = np.einsum("xm,pr->xpmr", -s, same)
        bwd[:, :, 1, :, :, 0] = np.einsum("xm,pr->xpmr", s, same)
        bwd[:, :, 1, :, :, 1] = np.einsum("xm,pr->xpmr", c, same)
        forward.append(fwd.reshape(MX * pencils * 2, span * pencils * 2))
        backward.append(bwd.reshape(span * pencils * 2, MX * pencils * 2))
    return np.stack(forward).astype(ml_dtypes.bfloat16), np.stack(backward).astype(ml_dtypes.bfloat16)


def gather_tables(batch, halves, modes, pencils):
    plain = np.zeros((modes, pencils, batch, 2, batch, halves, modes, pencils, 2))
    turned = np.zeros_like(plain)
    for m in range(modes):
        for p in range(pencils):
            for b in range(batch):
                plain[m, p, b, 0, b, :, m, p, 0] = 1.0
                plain[m, p, b, 1, b, :, m, p, 1] = 1.0
                turned[m, p, b, 0, b, :, m, p, 1] = 1.0
                turned[m, p, b, 1, b, :, m, p, 0] = -1.0
    rows = modes * pencils * batch * 2
    both = np.stack([plain.reshape(rows, -1), turned.reshape(rows, -1)])
    return both.astype(ml_dtypes.bfloat16)


def scatter_table(batch, modes, pencils):
    order = np.arange(modes * pencils * batch * 2).reshape(modes * pencils, batch, 2).transpose(1, 0, 2).reshape(-1)
    return np.eye(order.size)[order].astype(ml_dtypes.bfloat16)


def dot(a, b, dims=((1,), (0,))):
    return lax.dot_general(a, b, (dims, ((), ())), preferred_element_type=f32)


def yz_kernel(place, field, cotangent, table, *blocks):
    rows = table.shape[1]
    mixed = jnp.concatenate([table[place[0] ^ r] for r in range(QUAD)], axis=0)
    for which, source in enumerate((field, cotangent)):
        for x in range(0, source.shape[0], 2):
            pair = jnp.concatenate([source[x], source[x + 1]], axis=1)
            result = dot(mixed, pair).astype(half)
            for r in range(QUAD):
                piece = result[r * rows : (r + 1) * rows]
                blocks[r][which, x] = piece[:, :C]
                blocks[r][which, x + 1] = piece[:, C:]


def x_kernel(place, *refs):
    pieces, (table, out, held) = refs[:QUAD], refs[QUAD:]
    for r in range(QUAD):
        held[place[0] ^ r] = pieces[r][...]
    matrix = table[place[1]]
    fields, cells, rows = held.shape[1:4]
    height = matrix.shape[1] // QUAD // cells
    owners = rows // height
    spaces = out.shape[0] // owners
    for d in range(owners):
        columns = [
            jnp.concatenate(
                [held[q, f, x, d * height : (d + 1) * height, :] for q in range(QUAD) for x in range(cells)], axis=0
            )
            for f in range(fields)
        ]
        result = dot(matrix, jnp.concatenate(columns, axis=1)).astype(half)
        for f in range(fields):
            out[d * spaces : (d + 1) * spaces, f] = result[:, f * C : (f + 1) * C].reshape(spaces, -1, C)


def modes_kernel(arrived, weights, gather, scatter, sent, inputs, pairs):
    batch, halves, _, _, rows, _ = arrived.shape
    modes, _, pencils = weights.shape[:3]
    field = arrived[:, :, 0, 0].reshape(-1, C)
    cot = arrived[:, :, 0, 1].reshape(-1, C)
    both = dot(gather[0], jnp.concatenate([field, cot], axis=1))
    turned = dot(gather[1], cot)
    inputs[0] = both[:, :C].astype(half)
    pair = jnp.concatenate([both[:, C:], turned], axis=1).astype(half)
    pairs[0] = pair
    height = batch * 2
    results = []
    for m in range(modes):
        for p in range(0, pencils, 2):
            at = (m * pencils + p) * height
            columns = jnp.concatenate(
                [jnp.concatenate([weights[m, 0, p + k, 0], weights[m, 0, p + k, 1]], axis=1) for k in range(2)], axis=0
            ).astype(half)
            result = dot(pair[at : at + 2 * height], columns, ((1,), (1,)))
            results += [result[:height, :C], result[height:, C:]]
    grads = jnp.concatenate(results, axis=0).astype(half)
    spread = dot(scatter[...], grads).astype(half).reshape(batch, rows, C)
    for h in range(halves):
        sent[:, h, 0] = spread


def adam_kernel(inputs, pairs, weights, first, second, new_weights, new_first, new_second):
    count = weights.shape[0]
    height = inputs.shape[0] // count
    scale_first = learn_rate / (1.0 - decay_first**STEP)
    scale_second = 1.0 / (1.0 - decay_second**STEP)
    for k in range(count):
        u = inputs[k * height : (k + 1) * height, :]
        g = pairs[k * height : (k + 1) * height, :]
        grads = dot(u, g, ((0,), (0,)))
        for part in range(2):
            grad = grads[:, part * C : (part + 1) * C]
            m = decay_first * first[k, part] + (1.0 - decay_first) * grad
            v = decay_second * second[k, part] + (1.0 - decay_second) * grad * grad
            new_first[k, part] = m
            new_second[k, part] = v
            new_weights[k, part] = weights[k, part] - scale_first * m / (jnp.sqrt(v * scale_second) + adam_floor)


def back_x_kernel(place, arrived, table, *blocks):
    matrix = table[place[1]]
    cells, owners, height, _ = blocks[0].shape
    spaces = arrived.shape[0] // owners
    span = cells * height
    held = blocks[QUAD]
    for d in range(0, owners, 2):
        columns = jnp.concatenate(
            [arrived[k * spaces : (k + 1) * spaces].reshape(-1, C) for k in (d, d + 1)], axis=1
        )
        result = dot(matrix, columns).astype(half)
        for q in range(QUAD):
            piece = result[q * span : (q + 1) * span].reshape(cells, height, 2 * C)
            held[q, :, d] = piece[:, :, :C]
            held[q, :, d + 1] = piece[:, :, C:]
    for r in range(QUAD):
        blocks[r][...] = held[place[0] ^ r]


def back_yz_kernel(place, *refs):
    pieces, (table, out, held) = refs[:QUAD], refs[QUAD:]
    for r in range(QUAD):
        held[place[0] ^ r] = pieces[r][...]
    matrix = table[...]
    for x in range(0, out.shape[0], 2):
        columns = jnp.concatenate([held[:, k].reshape(-1, C) for k in (x, x + 1)], axis=1)
        result = dot(matrix, columns).astype(half)
        out[x] = result[:, :C]
        out[x + 1] = result[:, C:]


VMEM = pl.BlockSpec(memory_space=pltpu.VMEM)
SMEM = pl.BlockSpec(memory_space=pltpu.SMEM)
MIB = 1 << 20


def params(mib, **more):
    return pltpu.CompilerParams(vmem_limit_bytes=mib * MIB, **more)


def exchange(blocks, count):
    moved = [
        lax.ppermute(blocks[r], "space", [(s, s ^ r) for s in range(count)]) for r in range(1, QUAD)
    ]
    return [blocks[0]] + moved


def fast(field, cotangent, weights, first_moment, second_moment):
    spaces = lax.axis_size("space")
    owners = lax.axis_size("dp")
    cells = field.shape[1]
    total_x = cells * spaces
    halves = spaces // QUAD
    pencils = MYZ // owners // QUAD
    modes = MX // spaces
    height = pencils * 2
    s = lax.axis_index("space").astype(jnp.int32)
    place = jnp.stack([s % QUAD, s // QUAD])
    table_yz = yz_table(owners)
    table_x, back_table_x = x_tables(total_x, halves, pencils)
    back_table_yz = np.ascontiguousarray(table_yz.reshape(MYZ * 2, NY * NZ).T)
    gather = gather_tables(owners, halves, modes, pencils)
    scatter = scatter_table(owners, modes, pencils)

    blocks = pl.pallas_call(
        yz_kernel,
        out_shape=[jax.ShapeDtypeStruct((2, cells, owners * height, C), half)] * QUAD,
        in_specs=[SMEM, VMEM, VMEM, VMEM],
        out_specs=[VMEM] * QUAD,
        compiler_params=params(16),
        name="yz_modes",
    )(place, field.reshape(cells, NY * NZ, C), cotangent.reshape(cells, NY * NZ, C), jnp.asarray(table_yz))
    blocks = exchange(blocks, spaces)

    rows = modes * height
    partial = pl.pallas_call(
        x_kernel,
        out_shape=jax.ShapeDtypeStruct((owners * spaces, 2, rows, C), half),
        in_specs=[SMEM] + [VMEM] * (QUAD + 1),
        out_specs=VMEM,
        scratch_shapes=[pltpu.VMEM((QUAD, 2, cells, owners * height, C), half)],
        compiler_params=params(16),
        name="x_modes",
    )(place, *blocks, jnp.asarray(table_x))
    arrived = lax.all_to_all(partial, ("dp", "space"), 0, 0, tiled=True)
    arrived = arrived.reshape(owners, halves, QUAD, 2, rows, C)

    mode_rows = rows * owners
    whole = lambda *shape: pl.BlockSpec(shape, lambda q: (0,) * len(shape))
    sent, inputs, pairs = pl.pallas_call(
        modes_kernel,
        grid=(QUAD,),
        out_shape=[
            jax.ShapeDtypeStruct((owners, halves, QUAD, rows, C), half),
            jax.ShapeDtypeStruct((QUAD, mode_rows, C), half),
            jax.ShapeDtypeStruct((QUAD, mode_rows, 2 * C), half),
        ],
        in_specs=[
            pl.BlockSpec((owners, halves, 1, 2, rows, C), lambda q: (0, 0, q, 0, 0, 0)),
            pl.BlockSpec((modes, 1, pencils, 2, C, C), lambda q: (0, q, 0, 0, 0, 0)),
            whole(*gather.shape),
            whole(*scatter.shape),
        ],
        out_specs=[
            pl.BlockSpec((owners, halves, 1, rows, C), lambda q: (0, 0, q, 0, 0)),
            pl.BlockSpec((1, mode_rows, C), lambda q: (q, 0, 0)),
            pl.BlockSpec((1, mode_rows, 2 * C), lambda q: (q, 0, 0)),
        ],
        compiler_params=params(24),
        name="mode_grads",
    )(arrived, weights.reshape(modes, QUAD, pencils, 2, C, C), jnp.asarray(gather), jnp.asarray(scatter))

    returned = lax.all_to_all(
        sent.reshape(owners * spaces, rows, C), ("dp", "space"), 0, 0, tiled=True
    )

    chunk = pencils // 2
    steps = modes * QUAD * 2
    big = pl.BlockSpec((None, None, chunk, 2, C, C), lambda i: (i // (2 * QUAD), i // 2 % QUAD, i % 2, 0, 0, 0))
    per = chunk * owners * 2
    small = lambda width: pl.BlockSpec(
        (None, per, width), lambda i: (i // 2 % QUAD, i // (2 * QUAD) * 2 + i % 2, 0)
    )
    split = (modes, QUAD, pencils, 2, C, C)
    elements = weights.size
    new_weights, new_first, new_second = pl.pallas_call(
        adam_kernel,
        grid=(steps,),
        out_shape=[jax.ShapeDtypeStruct(split, f32)] * 3,
        in_specs=[small(C), small(2 * C), big, big, big],
        out_specs=[big] * 3,
        compiler_params=params(24),
        cost_estimate=pl.CostEstimate(
            flops=16 * elements, bytes_accessed=24 * elements, transcendentals=elements
        ),
        name="adam",
    )(inputs, pairs, weights.reshape(split), first_moment.reshape(split), second_moment.reshape(split))

    blocks = pl.pallas_call(
        back_x_kernel,
        out_shape=[jax.ShapeDtypeStruct((cells, owners, height, C), half)] * QUAD,
        in_specs=[SMEM, VMEM, VMEM],
        out_specs=[VMEM] * QUAD,
        scratch_shapes=[pltpu.VMEM((QUAD, cells, owners, height, C), half)],
        compiler_params=params(16),
        name="back_x",
    )(place, returned, jnp.asarray(back_table_x))
    blocks = exchange(blocks, spaces)
    field_grad = pl.pallas_call(
        back_yz_kernel,
        out_shape=jax.ShapeDtypeStruct((cells, NY * NZ, C), half),
        in_specs=[SMEM] + [VMEM] * (QUAD + 1),
        out_specs=VMEM,
        scratch_shapes=[pltpu.VMEM((QUAD, cells, owners, height, C), half)],
        compiler_params=params(16),
        name="back_yz",
    )(place, *blocks, jnp.asarray(back_table_yz))
    return (
        field_grad.reshape(field.shape),
        new_weights.reshape(weights.shape),
        new_first.reshape(weights.shape),
        new_second.reshape(weights.shape),
    )


def trig_tables(length, modes_kept, signed):
    cosine, sine_part = np_tables(length, modes_kept, signed)
    return jnp.asarray(cosine, half), jnp.asarray(sine_part, half)


def forward_table(cosine, sine_part):
    real_row = jnp.stack([cosine, -sine_part], axis=-1)
    imag_row = jnp.stack([sine_part, cosine], axis=-1)
    return jnp.stack([real_row, imag_row], axis=1)


def inverse_table(cosine, sine_part):
    real_row = jnp.stack([cosine.T, sine_part.T], axis=-1)
    imag_row = jnp.stack([-sine_part.T, cosine.T], axis=-1)
    return jnp.stack([real_row, imag_row], axis=1)


def adam_update(weights, first_moment, second_moment, weight_grads):
    new_first = decay_first * first_moment + (1.0 - decay_first) * weight_grads
    new_second = decay_second * second_moment + (1.0 - decay_second) * weight_grads * weight_grads
    first_hat = new_first / (1.0 - decay_first**STEP)
    second_hat = new_second / (1.0 - decay_second**STEP)
    new_weights = weights - learn_rate * first_hat / (jnp.sqrt(second_hat) + adam_floor)
    return (new_weights, new_first, new_second)


def general(field, cotangent, weights, first_moment, second_moment):
    slab_count = lax.axis_size("space")
    batch_local = field.shape[0]
    cells_x = field.shape[1]
    total_x = cells_x * slab_count
    cos_z, sin_z = trig_tables(NZ, MZ, False)
    cos_y, sin_y = trig_tables(NY, MY, True)
    cos_x, sin_x = trig_tables(total_x, MX, True)
    table_z = jnp.stack([cos_z, -sin_z], axis=1)
    table_y = forward_table(cos_y, sin_y)
    table_x = forward_table(cos_x, sin_x)
    back_table_x = inverse_table(cos_x, sin_x)
    back_table_y = inverse_table(cos_y, sin_y)
    back_table_z = jnp.stack([cos_z.T, -sin_z.T], axis=0)
    product = functools.partial(jnp.einsum, preferred_element_type=f32)

    def swap(values, axis, split, concat):
        return lax.all_to_all(values, axis, split_axis=split, concat_axis=concat, tiled=True)

    def to_modes(slab_field):
        first_pass = product("bxyzc,zpk->bxypkc", slab_field, table_z).astype(half)
        second = product("bxypkc,ypmq->bxmkqc", first_pass, table_y).astype(half)
        second = second.reshape(batch_local, cells_x, MYZ, 2, C)
        along = product("bxpjc,xjmq->bmpqc", swap(second, "space", 2, 1), table_x).astype(half)
        return swap(swap(along, "space", 1, 2), "dp", 2, 0)

    field_hat = to_modes(field)
    cot_hat = to_modes(cotangent)
    rotated = jnp.stack([cot_hat[:, :, :, 1], -cot_hat[:, :, :, 0]], axis=3)
    form_in = "bmpjc,bmpjo->mpco"
    weight_grads = jnp.stack([product(form_in, field_hat, cot_hat), product(form_in, field_hat, rotated)], axis=2)
    half_weights = weights.astype(half)
    form_back = "mpjio,bmpjo->bmpi"
    mode_grads = jnp.stack(
        [product(form_back, half_weights, cot_hat), product(form_back, half_weights, rotated)], axis=3
    ).astype(half)
    updated = adam_update(weights, first_moment, second_moment, weight_grads)
    pencils = swap(swap(mode_grads, "dp", 0, 2), "space", 2, 1)
    back_x = product("bmpjc,mjxq->bxpqc", pencils, back_table_x).astype(half)
    unpacked = swap(back_x, "space", 1, 2).reshape(batch_local, cells_x, MY, MZ, 2, C)
    back_y = product("bxmkjc,mjyq->bxyqkc", unpacked, back_table_y).astype(half)
    field_grad = product("bxyqkc,qkz->bxyzc", back_y, back_table_z).astype(half)
    return (field_grad, *updated)


def solution(mesh):
    owners, spaces = mesh.shape["dp"], mesh.shape["space"]
    grid = P("dp", "space", None, None, None)
    held = P("space", "dp", None, None, None)

    def on_device(field, *rest):
        fits = spaces % QUAD == 0 and MX % spaces == 0 and MYZ % (owners * QUAD * 8) == 0 and owners % 2 == 0
        fits = fits and field.shape[0] == 1 and field.shape[1] % 2 == 0
        return (fast if fits else general)(field, *rest)

    return jax.shard_map(
        on_device,
        mesh=mesh,
        in_specs=(grid, grid, held, held, held),
        out_specs=(grid, held, held, held),
        check_vma=False,
    )
```

```python
import functools
import math

import jax
import jax.numpy as jnp
import ml_dtypes
import numpy as np
from jax import lax
from jax.experimental import pallas as pl
from jax.experimental.pallas import tpu as pltpu
from jax.sharding import PartitionSpec as P

C = 128
MX = 16
MY = 16
MZ = 8
NY = 32
NZ = 16
STEP = 100
MYZ = 128
QUAD = 4


decay_first = 0.9
decay_second = 0.999
learn_rate = 0.001
adam_floor = 1e-08

f32 = jnp.float32
half = jnp.bfloat16


def np_tables(length, modes_kept, signed):
    points = np.arange(length)
    frequency = np.arange(modes_kept) - (modes_kept // 2 if signed else 0)
    angles = np.mod(points[:, None] * frequency[None, :], length) * (2.0 * math.pi / length)
    factor = np.float32(1.0 / math.sqrt(length))
    cosine = (np.cos(angles).astype(np.float32) * factor).astype(ml_dtypes.bfloat16)
    sine = (np.sin(angles).astype(np.float32) * factor).astype(ml_dtypes.bfloat16)
    return cosine.astype(np.float64), sine.astype(np.float64)


def yz_table(dp_count):
    cos_z, sin_z = np_tables(NZ, MZ, False)
    cos_y, sin_y = np_tables(NY, MY, True)
    cy, sy = cos_y.T[:, None, :, None], sin_y.T[:, None, :, None]
    cz, sz = cos_z.T[None, :, None, :], sin_z.T[None, :, None, :]
    real = cy * cz - sy * sz
    imag = -(sy * cz + cy * sz)
    table = np.stack([real, imag], axis=2).reshape(MYZ, 2, NY * NZ)
    pencils = MYZ // dp_count // QUAD
    table = table.reshape(dp_count, QUAD, pencils, 2, NY * NZ).transpose(1, 0, 2, 3, 4)
    return table.reshape(QUAD, dp_count * pencils * 2, NY * NZ).astype(ml_dtypes.bfloat16)


def x_tables(total_x, halves, pencils):
    cos_x, sin_x = np_tables(total_x, MX, True)
    same = np.eye(pencils)
    span = total_x // halves
    forward, backward = [], []
    for part in range(halves):
        c, s = cos_x[part * span : (part + 1) * span], sin_x[part * span : (part + 1) * span]
        fwd = np.zeros((MX, pencils, 2, span, pencils, 2))
        fwd[:, :, 0, :, :, 0] = np.einsum("xm,pr->mpxr", c, same)
        fwd[:, :, 0, :, :, 1] = np.einsum("xm,pr->mpxr", s, same)
        fwd[:, :, 1, :, :, 0] = np.einsum("xm,pr->mpxr", -s, same)
        fwd[:, :, 1, :, :, 1] = np.einsum("xm,pr->mpxr", c, same)
        bwd = np.zeros((span, pencils, 2, MX, pencils, 2))
        bwd[:, :, 0, :, :, 0] = np.einsum("xm,pr->xpmr", c, same)
        bwd[:, :, 0, :, :, 1] = np.einsum("xm,pr->xpmr", -s, same)
        bwd[:, :, 1, :, :, 0] = np.einsum("xm,pr->xpmr", s, same)
        bwd[:, :, 1, :, :, 1] = np.einsum("xm,pr->xpmr", c, same)
        forward.append(fwd.reshape(MX * pencils * 2, span * pencils * 2))
        backward.append(bwd.reshape(span * pencils * 2, MX * pencils * 2))
    return np.stack(forward).astype(ml_dtypes.bfloat16), np.stack(backward).astype(ml_dtypes.bfloat16)


def gather_tables(batch, halves, modes, pencils):
    plain = np.zeros((modes, pencils, batch, 2, batch, halves, modes, pencils, 2))
    turned = np.zeros_like(plain)
    for m in range(modes):
        for p in range(pencils):
            for b in range(batch):
                plain[m, p, b, 0, b, :, m, p, 0] = 1.0
                plain[m, p, b, 1, b, :, m, p, 1] = 1.0
                turned[m, p, b, 0, b, :, m, p, 1] = 1.0
                turned[m, p, b, 1, b, :, m, p, 0] = -1.0
    rows = modes * pencils * batch * 2
    both = np.stack([plain.reshape(rows, -1), turned.reshape(rows, -1)])
    return both.astype(ml_dtypes.bfloat16)


def scatter_table(batch, modes, pencils):
    order = np.arange(modes * pencils * batch * 2).reshape(modes * pencils, batch, 2).transpose(1, 0, 2).reshape(-1)
    return np.eye(order.size)[order].astype(ml_dtypes.bfloat16)


def dot(a, b, dims=((1,), (0,))):
    return lax.dot_general(a, b, (dims, ((), ())), preferred_element_type=f32)


def yz_kernel(place, field, cotangent, table, *refs):
    blocks, (mixed, cells_in, sems) = refs[:QUAD], refs[QUAD:]
    rows = table.shape[1]
    cells = field.shape[0]
    loads = [
        pltpu.make_async_copy(table.at[place[0] ^ r], mixed.at[pl.ds(r * rows, rows)], sems.at[r]) for r in range(QUAD)
    ]
    for which, source in enumerate((field, cotangent)):
        for x in range(0, cells, 2):
            loads.append(
                pltpu.make_async_copy(source.at[x : x + 2], cells_in.at[which, x : x + 2], sems.at[len(loads)])
            )
    for load in loads:
        load.start()
    for load in loads[:QUAD]:
        load.wait()
    matrix = mixed[...]
    at = QUAD
    for which in range(2):
        for x in range(0, cells, 2):
            loads[at].wait()
            at += 1
            pair = jnp.concatenate([cells_in[which, x], cells_in[which, x + 1]], axis=1)
            result = dot(matrix, pair).astype(half)
            for r in range(QUAD):
                piece = result[r * rows : (r + 1) * rows]
                blocks[r][which, x] = piece[:, :C]
                blocks[r][which, x + 1] = piece[:, C:]


def x_transform(place, which, pieces, table, held):
    for r in range(QUAD):
        held[place[0] ^ r] = pieces[r][which]
    matrix = table[place[1]]
    cells, rows = held.shape[1:3]
    height = matrix.shape[1] // QUAD // cells
    results = []
    for d in range(0, rows // height, 2):
        columns = [
            jnp.concatenate(
                [held[q, x, k * height : (k + 1) * height, :] for q in range(QUAD) for x in range(cells)], axis=0
            )
            for k in (d, d + 1)
        ]
        result = dot(matrix, jnp.concatenate(columns, axis=1)).astype(half)
        results += [result[:, :C], result[:, C:]]
    return results


def x_field_kernel(place, *refs):
    pieces, (table, own, other, held, split) = refs[:QUAD], refs[QUAD:]
    for d, result in enumerate(x_transform(place, 0, pieces, table, held)):
        split[:, d * QUAD : (d + 1) * QUAD] = result.reshape(split.shape[0], QUAD, -1, C)
    own[...] = split[place[1]]
    other[...] = split[1 - place[1]]


def x_cot_kernel(place, *refs):
    pieces, (table, _, out, held) = refs[:QUAD], refs[QUAD:]
    results = x_transform(place, 1, pieces, table, held)
    spaces = out.shape[0] // len(results)
    for d, result in enumerate(results):
        out[d * spaces : (d + 1) * spaces] = result.reshape(spaces, -1, C)


def join_kernel(cot_in, own, come, after, cot_out, summed):
    del cot_in, after, cot_out
    summed[...] = (own[...].astype(f32) + come[...].astype(f32)).astype(half)


def start_all(loads):
    for load in loads:
        load.start()


def stage_weights_kernel(after, weights, *refs):
    count = (len(refs) - 3) // 2
    sources, weights_held, held = refs[:count], refs[count], refs[count + 1 : 2 * count + 1]
    rounded, sems = refs[2 * count + 1 :]
    del after
    pieces = 8
    modes, pencils = weights.shape[:2]
    each = modes * pencils // pieces
    loads = []
    for k in range(pieces):
        m, p = k * each // pencils, k * each % pencils
        loads.append(
            pltpu.make_async_copy(weights.at[m, p : p + each], weights_held.at[m, p : p + each], sems.at[k])
        )
    for source, target in zip(sources, held):
        loads.append(pltpu.make_async_copy(source, target, sems.at[len(loads)]))
    start_all(loads)
    for k in range(pieces):
        loads[k].wait()
        m, p = k * each // pencils, k * each % pencils

        def body(i, carry):
            for part in range(2):
                rounded[m, p + i, :, part * C : (part + 1) * C] = weights_held[m, p + i, part].astype(half)
            return carry

        lax.fori_loop(0, each, body, 0)
    for load in loads[pieces:]:
        load.wait()


def stage_moments_kernel(after, first, second, first_held, second_held, sems):
    del after
    loads = []
    pencils = first.shape[1]
    each = pencils // 4
    for source, target in ((first, first_held), (second, second_held)):
        for m in range(target.shape[0]):
            for p in range(0, pencils, each):
                loads.append(
                    pltpu.make_async_copy(source.at[m, p : p + each], target.at[m, p : p + each], sems.at[len(loads)])
                )
    start_all(loads)
    for load in loads:
        load.wait()


def modes_kernel(arrived, field, weights, gather, scatter, sent, pairs):
    batch, halves, quad, rows, _ = arrived.shape
    modes, pencils = weights.shape[0], weights.shape[1] // quad
    height = batch * 2
    sent[:, :, 1] = field[...].reshape(batch, quad, rows, C)
    for q in range(quad):
        cot = arrived[:, :, q].reshape(-1, C)
        pair = jnp.concatenate([dot(gather[0], cot), dot(gather[1], cot)], axis=1).astype(half)
        pairs[q] = pair
        results = []
        for m in range(modes):
            for p in range(0, pencils, 2):
                at = (m * pencils + p) * height
                first = q * pencils + p
                columns = weights[m, first : first + 2].reshape(2 * C, 2 * C)
                result = dot(pair[at : at + 2 * height], columns, ((1,), (1,)))
                results += [result[:height, :C], result[height:, C:]]
        grads = jnp.concatenate(results, axis=0).astype(half)
        sent[:, q, 0] = dot(scatter[0], grads).astype(half).reshape(batch, rows, C)


def sort_kernel(arrived, gather, back, inputs):
    batch, quad = arrived.shape[:2]
    back[...] = arrived[:, :, 0].reshape(back.shape)
    for q in range(quad):
        inputs[q] = dot(gather[1], arrived[:, q, 1].reshape(-1, C)).astype(half)


def adam_kernel(mode, inputs, pairs, weights, first, second, *refs):
    new_weights, new_first, new_second, token, held, sems = refs[-6:]
    new = (new_weights, new_first, new_second)
    modes, pencils = weights.shape[:2]
    steps, count = held.shape[1:3]
    height = inputs.shape[1] // (modes * (pencils // QUAD))
    per_quad = steps // QUAD
    scale_first = learn_rate / (1.0 - decay_first**STEP)
    scale_second = 1.0 / (1.0 - decay_second**STEP)

    def copies(i):
        return [
            pltpu.make_async_copy(held.at[o, i], new[o].at[mode, pl.ds(i * count, count)], sems.at[i, o])
            for o in range(3)
        ]

    def body(i, carry):
        rows = count * height
        row = pl.multiple_of((mode * per_quad + i % per_quad) * rows, rows)
        us = inputs[i // per_quad, pl.ds(row, rows), :]
        gs = pairs[i // per_quad, pl.ds(row, rows), :]
        for k in range(count):
            u = us[k * height : (k + 1) * height]
            g = gs[k * height : (k + 1) * height]
            grads = dot(u, g, ((0,), (0,)))
            p = i * count + k
            for part in range(2):
                grad = grads[:, part * C : (part + 1) * C]
                m = decay_first * first[mode, p, part] + (1.0 - decay_first) * grad
                v = decay_second * second[mode, p, part] + ((1.0 - decay_second) * grad) * grad
                held[1, i, k, part] = m
                held[2, i, k, part] = v
                level = v * scale_second
                inverse = lax.rsqrt(level)
                floored = level * inverse + adam_floor
                inverse = inverse * (2.0 - floored * inverse)
                held[0, i, k, part] = weights[mode, p, part] - (scale_first * m) * inverse
        for copy in copies(i):
            copy.start()
        return carry

    def finish(i, carry):
        for copy in copies(i):
            copy.wait()
        return carry

    lax.fori_loop(0, steps, body, 0)
    lax.fori_loop(0, steps, finish, 0)
    token[...] = jnp.zeros_like(token)


def back_x_kernel(place, own, come, table, after, *refs):
    blocks, (arrived, held) = refs[:QUAD], refs[QUAD:]
    arrived[place[1]] = own[...]
    arrived[1 - place[1]] = come[...]
    matrix = table[place[1]]
    cells, owners, height, _ = blocks[0].shape
    halves = arrived.shape[0]
    span = cells * height
    for d in range(0, owners, 2):
        columns = [
            jnp.concatenate([arrived[h, k * QUAD : (k + 1) * QUAD].reshape(-1, C) for h in range(halves)], axis=0)
            for k in (d, d + 1)
        ]
        result = dot(matrix, jnp.concatenate(columns, axis=1)).astype(half)
        for q in range(QUAD):
            piece = result[q * span : (q + 1) * span].reshape(cells, height, 2 * C)
            held[q, :, d] = piece[:, :, :C]
            held[q, :, d + 1] = piece[:, :, C:]
    for r in range(QUAD):
        blocks[r][...] = held[place[0] ^ r]


def back_yz_kernel(place, *refs):
    pieces, (table, after, out, held) = refs[:QUAD], refs[QUAD:]
    for r in range(QUAD):
        held[place[0] ^ r] = pieces[r][...]
    matrix = table[...]
    for x in range(0, out.shape[0], 2):
        columns = jnp.concatenate([held[:, k].reshape(-1, C) for k in (x, x + 1)], axis=1)
        result = dot(matrix, columns).astype(half)
        out[x] = result[:, :C]
        out[x + 1] = result[:, C:]


VMEM = pl.BlockSpec(memory_space=pltpu.VMEM)
SMEM = pl.BlockSpec(memory_space=pltpu.SMEM)
HBM = pl.BlockSpec(memory_space=pltpu.HBM)
ANY = pl.BlockSpec(memory_space=pl.ANY)
MIB = 1 << 20


def params(mib, **more):
    return pltpu.CompilerParams(vmem_limit_bytes=mib * MIB, **more)


def cost(size):
    return pl.CostEstimate(flops=0, bytes_accessed=size, transcendentals=0)


def in_hbm(values):
    return pltpu.with_memory_space_constraint(values, pltpu.HBM)


def exchange(blocks):
    moved = [lax.ppermute(blocks[r], "quad", [(q, q ^ r) for q in range(QUAD)]) for r in range(1, QUAD)]
    return [blocks[0]] + moved


def swap_halves(values):
    return lax.ppermute(values, "half", [(0, 1), (1, 0)])


def fast(field, cotangent, weights, first_moment, second_moment):
    halves = lax.axis_size("half")
    spaces = halves * QUAD
    owners = lax.axis_size("dp")
    cells = field.shape[1]
    total_x = cells * spaces
    pencils = MYZ // owners // QUAD
    modes = MX // spaces
    height = pencils * 2
    place = jnp.stack([lax.axis_index("quad"), lax.axis_index("half")]).astype(jnp.int32)
    table_yz = yz_table(owners)
    table_x, back_table_x = x_tables(total_x, halves, pencils)
    back_table_yz = np.ascontiguousarray(table_yz.reshape(MYZ * 2, NY * NZ).T)
    gather = gather_tables(owners, halves, modes, pencils)
    scatter = scatter_table(owners, modes, pencils)
    scatter = np.stack([scatter, scatter.T])
    vmem = lambda values: pltpu.VMEM(values.shape, values.dtype)

    flat = (cells, NY * NZ, C)
    blocks = pl.pallas_call(
        yz_kernel,
        out_shape=[pltpu.VMEM((2, cells, owners * height, C), half)] * QUAD,
        in_specs=[SMEM] + [HBM] * 3,
        out_specs=[VMEM] * QUAD,
        scratch_shapes=[
            pltpu.VMEM((MYZ * 2, NY * NZ), half),
            pltpu.VMEM((2,) + flat, half),
            pltpu.SemaphoreType.DMA((QUAD + cells,)),
        ],
        compiler_params=params(8),
        name="yz_modes",
    )(place, in_hbm(field.reshape(flat)), in_hbm(cotangent.reshape(flat)), in_hbm(jnp.asarray(table_yz)))

    split = (modes, QUAD * pencils, 2, C, C)
    big, first, second = weights.reshape(split), first_moment.reshape(split), second_moment.reshape(split)
    staged = [jnp.asarray(t) for t in (table_x, gather, scatter, back_table_x, back_table_yz)]
    weights_held, table_x, gather, scatter, back_table_x, back_table_yz, rounded = pl.pallas_call(
        stage_weights_kernel,
        out_shape=[vmem(big)] + [vmem(t) for t in staged] + [pltpu.VMEM((modes, QUAD * pencils, C, 2 * C), half)],
        in_specs=[ANY] + [HBM] * (1 + len(staged)),
        out_specs=[VMEM] * (2 + len(staged)),
        scratch_shapes=[pltpu.SemaphoreType.DMA((8 + len(staged),))],
        compiler_params=params(8),
        cost_estimate=cost(weights.size * 8),
        name="stage_weights",
    )(blocks[0], in_hbm(big), *[in_hbm(t) for t in staged])
    blocks = exchange(blocks)

    rows = modes * height
    per_half = (owners * QUAD, rows, C)
    gathered = pltpu.VMEM((QUAD, cells, owners * height, C), half)
    field_own, field_other = pl.pallas_call(
        x_field_kernel,
        out_shape=[pltpu.VMEM(per_half, half)] * 2,
        in_specs=[SMEM] + [VMEM] * (QUAD + 1),
        out_specs=[VMEM] * 2,
        scratch_shapes=[gathered, pltpu.VMEM((halves,) + per_half, half)],
        compiler_params=params(8),
        name="x_modes_field",
    )(place, *blocks, table_x)
    field_come = swap_halves(field_other)
    cot_part = pl.pallas_call(
        x_cot_kernel,
        out_shape=pltpu.VMEM((owners * spaces, rows, C), half),
        in_specs=[SMEM] + [VMEM] * (QUAD + 1) + [ANY],
        out_specs=VMEM,
        scratch_shapes=[gathered],
        compiler_params=params(8),
        name="x_modes_cot",
    )(place, *blocks, table_x, field_other)
    first_held, second_held = pl.pallas_call(
        stage_moments_kernel,
        out_shape=[vmem(first), vmem(second)],
        in_specs=[ANY] + [HBM] * 2,
        out_specs=[VMEM] * 2,
        scratch_shapes=[pltpu.SemaphoreType.DMA((8 * modes,))],
        compiler_params=params(8),
        cost_estimate=cost(weights.size * 8),
        name="stage_moments",
    )(field_other, in_hbm(first), in_hbm(second))
    cot_part, field_sum = pl.pallas_call(
        join_kernel,
        out_shape=[pltpu.VMEM((owners * spaces, rows, C), half), pltpu.VMEM(per_half, half)],
        in_specs=[VMEM] * 3 + [ANY],
        out_specs=[VMEM] * 2,
        input_output_aliases={0: 0},
        compiler_params=params(8),
        name="join",
    )(cot_part, field_own, field_come, first_held)
    arrived = lax.all_to_all(cot_part, ("dp", "half", "quad"), 0, 0, tiled=True)

    mode_rows = rows * owners
    sent, pairs = pl.pallas_call(
        modes_kernel,
        out_shape=[
            pltpu.VMEM((owners, QUAD, 2, rows, C), half),
            pltpu.VMEM((QUAD, mode_rows, 2 * C), half),
        ],
        in_specs=[VMEM] * 5,
        out_specs=[VMEM] * 2,
        compiler_params=params(8),
        name="mode_grads",
    )(arrived.reshape(owners, halves, QUAD, rows, C), field_sum, rounded, gather, scatter)

    returned = lax.all_to_all(
        sent.reshape(owners * QUAD, 2, rows, C), ("dp", "quad"), 0, 0, tiled=True
    )
    back, inputs = pl.pallas_call(
        sort_kernel,
        out_shape=[pltpu.VMEM(per_half, half), pltpu.VMEM((QUAD, mode_rows, C), half)],
        in_specs=[VMEM] * 2,
        out_specs=[VMEM] * 2,
        compiler_params=params(8),
        name="sort_modes",
    )(returned.reshape(owners, QUAD, 2, rows, C), scatter)
    back_come = swap_halves(back)

    count = 4
    steps = QUAD * pencils // count

    def adam(mode, after, *before):
        return pl.pallas_call(
            functools.partial(adam_kernel, mode),
            out_shape=[pltpu.HBM(split, f32)] * 3 + [pltpu.VMEM((8, C), f32)],
            in_specs=[VMEM] * 5 + [ANY] + [HBM] * len(before),
            out_specs=[HBM] * 3 + [VMEM],
            scratch_shapes=[
                pltpu.VMEM((3, steps, count, 2, C, C), f32),
                pltpu.SemaphoreType.DMA((steps, 3)),
            ],
            input_output_aliases={6 + k: k for k in range(len(before))},
            compiler_params=params(16),
            cost_estimate=cost(8 * weights.size),
            name="adam",
        )(inputs, pairs, weights_held, first_held, second_held, after, *before)

    *updated, token = adam(0, back)
    blocks = pl.pallas_call(
        back_x_kernel,
        out_shape=[pltpu.VMEM((cells, owners, height, C), half)] * QUAD,
        in_specs=[SMEM] + [VMEM] * 3 + [ANY],
        out_specs=[VMEM] * QUAD,
        scratch_shapes=[
            pltpu.VMEM((halves,) + per_half, half),
            pltpu.VMEM((QUAD, cells, owners, height, C), half),
        ],
        compiler_params=params(8),
        name="back_x",
    )(place, back, back_come, back_table_x, token)
    *updated, token = adam(1, blocks[1], *updated)
    blocks = exchange(blocks)
    field_grad = pl.pallas_call(
        back_yz_kernel,
        out_shape=jax.ShapeDtypeStruct((cells, NY * NZ, C), half),
        in_specs=[SMEM] + [VMEM] * (QUAD + 1) + [ANY],
        out_specs=VMEM,
        scratch_shapes=[pltpu.VMEM((QUAD, cells, owners, height, C), half)],
        compiler_params=params(8),
        name="back_yz",
    )(place, *blocks, back_table_yz, token)
    return (field_grad.reshape(field.shape), *[values.reshape(weights.shape) for values in updated])


def trig_tables(length, modes_kept, signed):
    cosine, sine_part = np_tables(length, modes_kept, signed)
    return jnp.asarray(cosine, half), jnp.asarray(sine_part, half)


def forward_table(cosine, sine_part):
    real_row = jnp.stack([cosine, -sine_part], axis=-1)
    imag_row = jnp.stack([sine_part, cosine], axis=-1)
    return jnp.stack([real_row, imag_row], axis=1)


def inverse_table(cosine, sine_part):
    real_row = jnp.stack([cosine.T, sine_part.T], axis=-1)
    imag_row = jnp.stack([-sine_part.T, cosine.T], axis=-1)
    return jnp.stack([real_row, imag_row], axis=1)


def adam_update(weights, first_moment, second_moment, weight_grads):
    new_first = decay_first * first_moment + (1.0 - decay_first) * weight_grads
    new_second = decay_second * second_moment + (1.0 - decay_second) * weight_grads * weight_grads
    first_hat = new_first / (1.0 - decay_first**STEP)
    second_hat = new_second / (1.0 - decay_second**STEP)
    new_weights = weights - learn_rate * first_hat / (jnp.sqrt(second_hat) + adam_floor)
    return (new_weights, new_first, new_second)


def general(field, cotangent, weights, first_moment, second_moment):
    slab_count = lax.axis_size("space")
    batch_local = field.shape[0]
    cells_x = field.shape[1]
    total_x = cells_x * slab_count
    cos_z, sin_z = trig_tables(NZ, MZ, False)
    cos_y, sin_y = trig_tables(NY, MY, True)
    cos_x, sin_x = trig_tables(total_x, MX, True)
    table_z = jnp.stack([cos_z, -sin_z], axis=1)
    table_y = forward_table(cos_y, sin_y)
    table_x = forward_table(cos_x, sin_x)
    back_table_x = inverse_table(cos_x, sin_x)
    back_table_y = inverse_table(cos_y, sin_y)
    back_table_z = jnp.stack([cos_z.T, -sin_z.T], axis=0)
    product = functools.partial(jnp.einsum, preferred_element_type=f32)

    def swap(values, axis, split, concat):
        return lax.all_to_all(values, axis, split_axis=split, concat_axis=concat, tiled=True)

    def to_modes(slab_field):
        first_pass = product("bxyzc,zpk->bxypkc", slab_field, table_z).astype(half)
        second = product("bxypkc,ypmq->bxmkqc", first_pass, table_y).astype(half)
        second = second.reshape(batch_local, cells_x, MYZ, 2, C)
        along = product("bxpjc,xjmq->bmpqc", swap(second, "space", 2, 1), table_x).astype(half)
        return swap(swap(along, "space", 1, 2), "dp", 2, 0)

    field_hat = to_modes(field)
    cot_hat = to_modes(cotangent)
    rotated = jnp.stack([cot_hat[:, :, :, 1], -cot_hat[:, :, :, 0]], axis=3)
    form_in = "bmpjc,bmpjo->mpco"
    weight_grads = jnp.stack([product(form_in, field_hat, cot_hat), product(form_in, field_hat, rotated)], axis=2)
    half_weights = weights.astype(half)
    form_back = "mpjio,bmpjo->bmpi"
    mode_grads = jnp.stack(
        [product(form_back, half_weights, cot_hat), product(form_back, half_weights, rotated)], axis=3
    ).astype(half)
    updated = adam_update(weights, first_moment, second_moment, weight_grads)
    pencils = swap(swap(mode_grads, "dp", 0, 2), "space", 2, 1)
    back_x = product("bmpjc,mjxq->bxpqc", pencils, back_table_x).astype(half)
    unpacked = swap(back_x, "space", 1, 2).reshape(batch_local, cells_x, MY, MZ, 2, C)
    back_y = product("bxmkjc,mjyq->bxyqkc", unpacked, back_table_y).astype(half)
    field_grad = product("bxyqkc,qkz->bxyzc", back_y, back_table_z).astype(half)
    return (field_grad, *updated)


def solution(mesh):
    owners, spaces = mesh.shape["dp"], mesh.shape["space"]
    pencils = MYZ // (owners * QUAD)
    if spaces == 2 * QUAD and MX == 2 * spaces and MYZ % (owners * QUAD * 8) == 0 and pencils * owners % 2 == 0:
        mesh = jax.sharding.Mesh(mesh.devices.reshape(owners, 2, QUAD), ("dp", "half", "quad"))
        space, on_device = ("half", "quad"), fast
    else:
        space, on_device = "space", general
    grid = P("dp", space, None, None, None)
    held = P(space, "dp", None, None, None)
    return jax.shard_map(
        on_device,
        mesh=mesh,
        in_specs=(grid, grid, held, held, held),
        out_specs=(grid, held, held, held),
        check_vma=False,
    )
```

```python
import functools
import math

import jax
import jax.numpy as jnp
import ml_dtypes
import numpy as np
from jax import lax
from jax.experimental import pallas as pl
from jax.experimental.pallas import tpu as pltpu
from jax.sharding import PartitionSpec as P

C = 128
MX = 16
MY = 16
MZ = 8
NY = 32
NZ = 16
STEP = 100
MYZ = 128
QUAD = 4


decay_first = 0.9
decay_second = 0.999
learn_rate = 0.001
adam_floor = 1e-08

f32 = jnp.float32
half = jnp.bfloat16


def np_tables(length, modes_kept, signed):
    points = np.arange(length)
    frequency = np.arange(modes_kept) - (modes_kept // 2 if signed else 0)
    angles = np.mod(points[:, None] * frequency[None, :], length) * (2.0 * math.pi / length)
    factor = np.float32(1.0 / math.sqrt(length))
    cosine = (np.cos(angles).astype(np.float32) * factor).astype(ml_dtypes.bfloat16)
    sine = (np.sin(angles).astype(np.float32) * factor).astype(ml_dtypes.bfloat16)
    return cosine.astype(np.float64), sine.astype(np.float64)


def yz_table(dp_count):
    cos_z, sin_z = np_tables(NZ, MZ, False)
    cos_y, sin_y = np_tables(NY, MY, True)
    cy, sy = cos_y.T[:, None, :, None], sin_y.T[:, None, :, None]
    cz, sz = cos_z.T[None, :, None, :], sin_z.T[None, :, None, :]
    real = cy * cz - sy * sz
    imag = -(sy * cz + cy * sz)
    table = np.stack([real, imag], axis=2).reshape(MYZ, 2, NY * NZ)
    pencils = MYZ // dp_count // QUAD
    table = table.reshape(dp_count, QUAD, pencils, 2, NY * NZ).transpose(1, 0, 2, 3, 4)
    return table.reshape(QUAD, dp_count * pencils * 2, NY * NZ).astype(ml_dtypes.bfloat16)


def x_tables(total_x, halves, pencils):
    cos_x, sin_x = np_tables(total_x, MX, True)
    same = np.eye(pencils)
    span = total_x // halves
    forward, backward = [], []
    for part in range(halves):
        c, s = cos_x[part * span : (part + 1) * span], sin_x[part * span : (part + 1) * span]
        fwd = np.zeros((MX, pencils, 2, span, pencils, 2))
        fwd[:, :, 0, :, :, 0] = np.einsum("xm,pr->mpxr", c, same)
        fwd[:, :, 0, :, :, 1] = np.einsum("xm,pr->mpxr", s, same)
        fwd[:, :, 1, :, :, 0] = np.einsum("xm,pr->mpxr", -s, same)
        fwd[:, :, 1, :, :, 1] = np.einsum("xm,pr->mpxr", c, same)
        bwd = np.zeros((span, pencils, 2, MX, pencils, 2))
        bwd[:, :, 0, :, :, 0] = np.einsum("xm,pr->xpmr", c, same)
        bwd[:, :, 0, :, :, 1] = np.einsum("xm,pr->xpmr", -s, same)
        bwd[:, :, 1, :, :, 0] = np.einsum("xm,pr->xpmr", s, same)
        bwd[:, :, 1, :, :, 1] = np.einsum("xm,pr->xpmr", c, same)
        forward.append(fwd.reshape(MX * pencils * 2, span * pencils * 2))
        backward.append(bwd.reshape(span * pencils * 2, MX * pencils * 2))
    return np.stack(forward).astype(ml_dtypes.bfloat16), np.stack(backward).astype(ml_dtypes.bfloat16)


def gather_tables(batch, halves, modes, pencils):
    plain = np.zeros((modes, pencils, batch, 2, batch, halves, modes, pencils, 2))
    turned = np.zeros_like(plain)
    for m in range(modes):
        for p in range(pencils):
            for b in range(batch):
                plain[m, p, b, 0, b, :, m, p, 0] = 1.0
                plain[m, p, b, 1, b, :, m, p, 1] = 1.0
                turned[m, p, b, 0, b, :, m, p, 1] = 1.0
                turned[m, p, b, 1, b, :, m, p, 0] = -1.0
    rows = modes * pencils * batch * 2
    both = np.stack([plain.reshape(rows, -1), turned.reshape(rows, -1)])
    return both.astype(ml_dtypes.bfloat16)


def scatter_table(batch, modes, pencils):
    order = np.arange(modes * pencils * batch * 2).reshape(modes * pencils, batch, 2).transpose(1, 0, 2).reshape(-1)
    return np.eye(order.size)[order].astype(ml_dtypes.bfloat16)


def dot(a, b, dims=((1,), (0,))):
    return lax.dot_general(a, b, (dims, ((), ())), preferred_element_type=f32)


def yz_transform(source, mixed, blocks):
    rows = mixed.shape[0] // QUAD
    for x in range(0, source.shape[0], 2):
        pair = jnp.concatenate([source[x], source[x + 1]], axis=1)
        result = dot(mixed[...], pair).astype(half)
        for r in range(QUAD):
            piece = result[r * rows : (r + 1) * rows]
            blocks[r][x] = piece[:, :C]
            blocks[r][x + 1] = piece[:, C:]


def yz_field_kernel(field, cotangent, table, later, *refs):
    blocks, (mixed, cot_held, later_held, cells_in, sems) = refs[:QUAD], refs[QUAD:]
    rows = table.shape[1]
    loads = [
        pltpu.make_async_copy(table.at[lax.axis_index("quad") ^ r], mixed.at[pl.ds(r * rows, rows)], sems.at[r]) for r in range(QUAD)
    ]
    for source, target in ((field, cells_in), (cotangent, cot_held), (later, later_held)):
        loads.append(pltpu.make_async_copy(source, target, sems.at[len(loads)]))
    for load in loads:
        load.start()
    for load in loads[: QUAD + 1]:
        load.wait()
    yz_transform(cells_in, mixed, blocks)
    for load in loads[QUAD + 1 :]:
        load.wait()


def yz_cot_kernel(cot_held, mixed, *blocks):
    yz_transform(cot_held, mixed, blocks)


def x_transform(pieces, table, held):
    for r in range(QUAD):
        held[lax.axis_index("quad") ^ r] = pieces[r][...]
    matrix = table[lax.axis_index("half")]
    cells, rows = held.shape[1:3]
    height = matrix.shape[1] // QUAD // cells
    results = []
    for d in range(0, rows // height, 2):
        columns = [
            jnp.concatenate(
                [held[q, x, k * height : (k + 1) * height, :] for q in range(QUAD) for x in range(cells)], axis=0
            )
            for k in (d, d + 1)
        ]
        result = dot(matrix, jnp.concatenate(columns, axis=1)).astype(half)
        results += [result[:, :C], result[:, C:]]
    return results


def x_kernel(extra, *refs):
    pieces, table, (own, other, held, split) = refs[:QUAD], refs[QUAD], refs[QUAD + 1 + extra :]
    for d, result in enumerate(x_transform(pieces, table, held)):
        split[:, d * QUAD : (d + 1) * QUAD] = result.reshape(split.shape[0], QUAD, -1, C)
    own[...] = split[lax.axis_index("half")]
    other[...] = split[1 - lax.axis_index("half")]


def sum_kernel(field_own, field_come, cot_own, cot_come, *refs):
    out = refs[-1]
    for which, (own, come) in enumerate(((field_own, field_come), (cot_own, cot_come))):
        out[:, which] = (own[...].astype(f32) + come[...].astype(f32)).astype(half)


def start_all(loads):
    for load in loads:
        load.start()


def stage_kernel(after, weights, *refs):
    count = (len(refs) - 3) // 2
    sources, weights_held, held = refs[:count], refs[count], refs[count + 1 : 2 * count + 1]
    rounded, sems = refs[2 * count + 1 :]
    del after
    modes, pencils = weights.shape[:2]
    each = pencils // 4
    spans = [(m, p) for m in range(modes) for p in range(0, pencils, each)]
    loads = []

    def add(source, target):
        loads.append(pltpu.make_async_copy(source, target, sems.at[len(loads)]))

    for m, p in spans:
        add(weights.at[m, p : p + each], weights_held.at[m, p : p + each])
    for source, target in zip(sources, held):
        if len(source.shape) < 5:
            add(source, target)
        else:
            for m, p in spans:
                add(source.at[m, p : p + each], target.at[m, p : p + each])
    for load in loads:
        load.start()
    for k, (m, p) in enumerate(spans):
        loads[k].wait()

        def body(i, carry):
            for part in range(2):
                rounded[m, p + i, :, part * C : (part + 1) * C] = weights_held[m, p + i, part].astype(half)
            return carry

        lax.fori_loop(0, each, body, 0)
    for load in loads[len(spans) :]:
        load.wait()


def modes_kernel(arrived, weights, gather, scatter, sent, inputs, pairs):
    batch, quad, _, rows, _ = arrived.shape
    modes, pencils = weights.shape[0], weights.shape[1] // quad
    height = batch * 2
    for q in range(quad):
        field = arrived[:, q, 0].reshape(-1, C)
        cot = arrived[:, q, 1].reshape(-1, C)
        both = dot(gather[0], jnp.concatenate([field, cot], axis=1)).astype(half)
        inputs[q] = both[:, :C]
        pair = jnp.concatenate([both[:, C:], dot(gather[1], cot).astype(half)], axis=1)
        pairs[q] = pair
        results = []
        for m in range(modes):
            for p in range(0, pencils, 2):
                at = (m * pencils + p) * height
                first = q * pencils + p
                columns = weights[m, first : first + 2].reshape(2 * C, 2 * C)
                result = dot(pair[at : at + 2 * height], columns, ((1,), (1,)))
                results += [result[:height, :C], result[height:, C:]]
        grads = jnp.concatenate(results, axis=0).astype(half)
        sent[:, q] = dot(scatter[...], grads).astype(half).reshape(batch, rows, C)


def adam_kernel(begin, inputs, pairs, weights, first, second, *refs):
    new_weights, new_first, new_second, token, held, sems = refs[-6:]
    new = (new_weights, new_first, new_second)
    modes, pencils = weights.shape[:2]
    steps, count = held.shape[1:3]
    height = inputs.shape[1] // (modes * (pencils // QUAD))
    per_mode = pencils // count
    per_quad = per_mode // QUAD
    scale_first = learn_rate / (1.0 - decay_first**STEP)
    scale_second = 1.0 / (1.0 - decay_second**STEP)

    def copies(i):
        mode, at = (i + begin) // per_mode, (i + begin) % per_mode
        return [
            pltpu.make_async_copy(held.at[o, i], new[o].at[mode, pl.ds(at * count, count)], sems.at[i, o])
            for o in range(3)
        ]

    def body(i, carry):
        mode, at = (i + begin) // per_mode, (i + begin) % per_mode
        rows = count * height
        row = pl.multiple_of((mode * per_quad + at % per_quad) * rows, rows)
        us = inputs[at // per_quad, pl.ds(row, rows), :]
        gs = pairs[at // per_quad, pl.ds(row, rows), :]
        for k in range(count):
            u = us[k * height : (k + 1) * height]
            g = gs[k * height : (k + 1) * height]
            grads = dot(u, g, ((0,), (0,)))
            p = at * count + k
            for part in range(2):
                grad = grads[:, part * C : (part + 1) * C]
                m = decay_first * first[mode, p, part] + (1.0 - decay_first) * grad
                v = decay_second * second[mode, p, part] + ((1.0 - decay_second) * grad) * grad
                held[1, i, k, part] = m
                held[2, i, k, part] = v
                level = v * scale_second
                inverse = lax.rsqrt(level)
                floored = level * inverse + adam_floor
                inverse = inverse * (2.0 - floored * inverse)
                held[0, i, k, part] = weights[mode, p, part] - (scale_first * m) * inverse
        for copy in copies(i):
            copy.start()
        return carry

    def finish(i, carry):
        for copy in copies(i):
            copy.wait()
        return carry

    lax.fori_loop(0, steps, body, 0)
    lax.fori_loop(0, steps, finish, 0)
    token[...] = jnp.zeros_like(token)


def back_x_kernel(own, come, table, after, *refs):
    blocks, (arrived, held) = refs[:QUAD], refs[QUAD:]
    arrived[lax.axis_index("half")] = own[...]
    arrived[1 - lax.axis_index("half")] = come[...]
    matrix = table[lax.axis_index("half")]
    cells, owners, height, _ = blocks[0].shape
    halves = arrived.shape[0]
    span = cells * height
    for d in range(0, owners, 2):
        columns = [
            jnp.concatenate([arrived[h, k * QUAD : (k + 1) * QUAD].reshape(-1, C) for h in range(halves)], axis=0)
            for k in (d, d + 1)
        ]
        result = dot(matrix, jnp.concatenate(columns, axis=1)).astype(half)
        for q in range(QUAD):
            piece = result[q * span : (q + 1) * span].reshape(cells, height, 2 * C)
            held[q, :, d] = piece[:, :, :C]
            held[q, :, d + 1] = piece[:, :, C:]
    for r in range(QUAD):
        blocks[r][...] = held[lax.axis_index("quad") ^ r]


def back_yz_kernel(*refs):
    pieces, (table, after, out, held) = refs[:QUAD], refs[QUAD:]
    for r in range(QUAD):
        held[lax.axis_index("quad") ^ r] = pieces[r][...]
    matrix = table[...]
    for x in range(0, out.shape[0], 2):
        columns = jnp.concatenate([held[:, k].reshape(-1, C) for k in (x, x + 1)], axis=1)
        result = dot(matrix, columns).astype(half)
        out[x] = result[:, :C]
        out[x + 1] = result[:, C:]


VMEM = pl.BlockSpec(memory_space=pltpu.VMEM)
HBM = pl.BlockSpec(memory_space=pltpu.HBM)
ANY = pl.BlockSpec(memory_space=pl.ANY)
MIB = 1 << 20


def params(mib, **more):
    return pltpu.CompilerParams(vmem_limit_bytes=mib * MIB, **more)


def cost(size):
    return pl.CostEstimate(flops=0, bytes_accessed=size, transcendentals=0)


def in_hbm(values):
    return pltpu.with_memory_space_constraint(values, pltpu.HBM)


def exchange(blocks):
    moved = [lax.ppermute(blocks[r], "quad", [(q, q ^ r) for q in range(QUAD)]) for r in range(1, QUAD)]
    return [blocks[0]] + moved


def swap_halves(values):
    return lax.ppermute(values, "half", [(0, 1), (1, 0)])


def fast(field, cotangent, weights, first_moment, second_moment):
    halves = lax.axis_size("half")
    spaces = halves * QUAD
    owners = lax.axis_size("dp")
    cells = field.shape[1]
    total_x = cells * spaces
    pencils = MYZ // owners // QUAD
    modes = MX // spaces
    height = pencils * 2
    table_yz = yz_table(owners)
    table_x, back_table_x = x_tables(total_x, halves, pencils)
    back_table_yz = np.ascontiguousarray(table_yz.reshape(MYZ * 2, NY * NZ).T)
    gather = gather_tables(owners, 1, modes, pencils)
    scatter = scatter_table(owners, modes, pencils)
    vmem = lambda values: pltpu.VMEM(values.shape, values.dtype)

    flat = (cells, NY * NZ, C)
    block = pltpu.VMEM((cells, owners * height, C), half)
    *field_blocks, mixed, cot_held, table_x = pl.pallas_call(
        yz_field_kernel,
        out_shape=[block] * QUAD + [pltpu.VMEM((MYZ * 2, NY * NZ), half), pltpu.VMEM(flat, half), vmem(table_x)],
        in_specs=[HBM] * 4,
        out_specs=[VMEM] * (QUAD + 3),
        scratch_shapes=[pltpu.VMEM(flat, half), pltpu.SemaphoreType.DMA((QUAD + 3,))],
        compiler_params=params(8),
        name="yz_modes_field",
    )(
        in_hbm(field.reshape(flat)),
        in_hbm(cotangent.reshape(flat)),
        in_hbm(jnp.asarray(table_yz)),
        in_hbm(jnp.asarray(table_x)),
    )
    cot_blocks = pl.pallas_call(
        yz_cot_kernel,
        out_shape=[block] * QUAD,
        in_specs=[VMEM] * 2,
        out_specs=[VMEM] * QUAD,
        compiler_params=params(8),
        name="yz_modes_cot",
    )(cot_held, mixed)

    split = (modes, QUAD * pencils, 2, C, C)
    big, first, second = weights.reshape(split), first_moment.reshape(split), second_moment.reshape(split)
    field_blocks = exchange(field_blocks)
    cot_blocks = exchange(cot_blocks)

    rows = modes * height
    per_half = (owners * QUAD, rows, C)
    gathered = pltpu.VMEM((QUAD, cells, owners * height, C), half)

    def x_modes(pieces, *after):
        return pl.pallas_call(
            functools.partial(x_kernel, len(after)),
            out_shape=[pltpu.VMEM(per_half, half)] * 2,
            in_specs=[VMEM] * (QUAD + 1) + [ANY] * len(after),
            out_specs=[VMEM] * 2,
            scratch_shapes=[gathered, pltpu.VMEM((halves,) + per_half, half)],
            compiler_params=params(8),
            name="x_modes",
        )(*pieces, table_x, *after)

    field_own, field_other = x_modes(field_blocks)
    field_come = swap_halves(field_other)
    cot_own, cot_other = x_modes(cot_blocks, field_other)
    cot_come = swap_halves(cot_other)
    staged = [jnp.asarray(t) for t in (gather, scatter, back_table_x, back_table_yz)] + [first, second]
    weights_held, gather, scatter, back_table_x, back_table_yz, first_held, second_held, rounded = pl.pallas_call(
        stage_kernel,
        out_shape=[vmem(big)] + [vmem(t) for t in staged] + [pltpu.VMEM((modes, QUAD * pencils, C, 2 * C), half)],
        in_specs=[ANY] + [HBM] * (1 + len(staged)),
        out_specs=[VMEM] * (2 + len(staged)),
        scratch_shapes=[pltpu.SemaphoreType.DMA((12 * modes + len(staged) - 2,))],
        compiler_params=params(8),
        cost_estimate=cost(0),
        name="stage",
    )(cot_other, in_hbm(big), *[in_hbm(t) for t in staged])
    summed = pl.pallas_call(
        sum_kernel,
        out_shape=pltpu.VMEM((owners * QUAD, 2, rows, C), half),
        in_specs=[VMEM] * 4 + [ANY],
        out_specs=VMEM,
        compiler_params=params(8),
        name="sum_halves",
    )(field_own, field_come, cot_own, cot_come, first_held)
    arrived = lax.all_to_all(summed, ("dp", "quad"), 0, 0, tiled=True)

    mode_rows = rows * owners
    sent, inputs, pairs = pl.pallas_call(
        modes_kernel,
        out_shape=[
            pltpu.VMEM((owners, QUAD, rows, C), half),
            pltpu.VMEM((QUAD, mode_rows, C), half),
            pltpu.VMEM((QUAD, mode_rows, 2 * C), half),
        ],
        in_specs=[VMEM] * 4,
        out_specs=[VMEM] * 3,
        compiler_params=params(8),
        name="mode_grads",
    )(arrived.reshape(owners, QUAD, 2, rows, C), rounded, gather, scatter)
    back = lax.all_to_all(sent.reshape(per_half), ("dp", "quad"), 0, 0, tiled=True)
    back_come = swap_halves(back)

    count = 4
    total = modes * QUAD * pencils // count
    first_steps = total * 12 // 16

    def adam(begin, end, after, *before):
        steps = end - begin
        return pl.pallas_call(
            functools.partial(adam_kernel, begin),
            out_shape=[pltpu.HBM(split, f32)] * 3 + [pltpu.VMEM((8, C), f32)],
            in_specs=[VMEM] * 5 + [ANY] + [HBM] * len(before),
            out_specs=[HBM] * 3 + [VMEM],
            scratch_shapes=[
                pltpu.VMEM((3, steps, count, 2, C, C), f32),
                pltpu.SemaphoreType.DMA((steps, 3)),
            ],
            input_output_aliases={6 + k: k for k in range(len(before))},
            compiler_params=params(22),
            cost_estimate=cost(16 * weights.size * steps // total),
            name="adam",
        )(inputs, pairs, weights_held, first_held, second_held, after, *before)

    *updated, token = adam(0, first_steps, back)
    blocks = pl.pallas_call(
        back_x_kernel,
        out_shape=[pltpu.VMEM((cells, owners, height, C), half)] * QUAD,
        in_specs=[VMEM] * 3 + [ANY],
        out_specs=[VMEM] * QUAD,
        scratch_shapes=[
            pltpu.VMEM((halves,) + per_half, half),
            pltpu.VMEM((QUAD, cells, owners, height, C), half),
        ],
        compiler_params=params(8),
        name="back_x",
    )(back, back_come, back_table_x, token)
    *updated, token = adam(first_steps, total, blocks[1], *updated)
    blocks = exchange(blocks)
    field_grad = pl.pallas_call(
        back_yz_kernel,
        out_shape=jax.ShapeDtypeStruct((cells, NY * NZ, C), half),
        in_specs=[VMEM] * (QUAD + 1) + [ANY],
        out_specs=VMEM,
        scratch_shapes=[pltpu.VMEM((QUAD, cells, owners, height, C), half)],
        compiler_params=params(8),
        name="back_yz",
    )(*blocks, back_table_yz, token)
    return (field_grad.reshape(field.shape), *[values.reshape(weights.shape) for values in updated])


def trig_tables(length, modes_kept, signed):
    cosine, sine_part = np_tables(length, modes_kept, signed)
    return jnp.asarray(cosine, half), jnp.asarray(sine_part, half)


def forward_table(cosine, sine_part):
    real_row = jnp.stack([cosine, -sine_part], axis=-1)
    imag_row = jnp.stack([sine_part, cosine], axis=-1)
    return jnp.stack([real_row, imag_row], axis=1)


def inverse_table(cosine, sine_part):
    real_row = jnp.stack([cosine.T, sine_part.T], axis=-1)
    imag_row = jnp.stack([-sine_part.T, cosine.T], axis=-1)
    return jnp.stack([real_row, imag_row], axis=1)


def adam_update(weights, first_moment, second_moment, weight_grads):
    new_first = decay_first * first_moment + (1.0 - decay_first) * weight_grads
    new_second = decay_second * second_moment + (1.0 - decay_second) * weight_grads * weight_grads
    first_hat = new_first / (1.0 - decay_first**STEP)
    second_hat = new_second / (1.0 - decay_second**STEP)
    new_weights = weights - learn_rate * first_hat / (jnp.sqrt(second_hat) + adam_floor)
    return (new_weights, new_first, new_second)


def general(field, cotangent, weights, first_moment, second_moment):
    slab_count = lax.axis_size("space")
    batch_local = field.shape[0]
    cells_x = field.shape[1]
    total_x = cells_x * slab_count
    cos_z, sin_z = trig_tables(NZ, MZ, False)
    cos_y, sin_y = trig_tables(NY, MY, True)
    cos_x, sin_x = trig_tables(total_x, MX, True)
    table_z = jnp.stack([cos_z, -sin_z], axis=1)
    table_y = forward_table(cos_y, sin_y)
    table_x = forward_table(cos_x, sin_x)
    back_table_x = inverse_table(cos_x, sin_x)
    back_table_y = inverse_table(cos_y, sin_y)
    back_table_z = jnp.stack([cos_z.T, -sin_z.T], axis=0)
    product = functools.partial(jnp.einsum, preferred_element_type=f32)

    def swap(values, axis, split, concat):
        return lax.all_to_all(values, axis, split_axis=split, concat_axis=concat, tiled=True)

    def to_modes(slab_field):
        first_pass = product("bxyzc,zpk->bxypkc", slab_field, table_z).astype(half)
        second = product("bxypkc,ypmq->bxmkqc", first_pass, table_y).astype(half)
        second = second.reshape(batch_local, cells_x, MYZ, 2, C)
        along = product("bxpjc,xjmq->bmpqc", swap(second, "space", 2, 1), table_x).astype(half)
        return swap(swap(along, "space", 1, 2), "dp", 2, 0)

    field_hat = to_modes(field)
    cot_hat = to_modes(cotangent)
    rotated = jnp.stack([cot_hat[:, :, :, 1], -cot_hat[:, :, :, 0]], axis=3)
    form_in = "bmpjc,bmpjo->mpco"
    weight_grads = jnp.stack([product(form_in, field_hat, cot_hat), product(form_in, field_hat, rotated)], axis=2)
    half_weights = weights.astype(half)
    form_back = "mpjio,bmpjo->bmpi"
    mode_grads = jnp.stack(
        [product(form_back, half_weights, cot_hat), product(form_back, half_weights, rotated)], axis=3
    ).astype(half)
    updated = adam_update(weights, first_moment, second_moment, weight_grads)
    pencils = swap(swap(mode_grads, "dp", 0, 2), "space", 2, 1)
    back_x = product("bmpjc,mjxq->bxpqc", pencils, back_table_x).astype(half)
    unpacked = swap(back_x, "space", 1, 2).reshape(batch_local, cells_x, MY, MZ, 2, C)
    back_y = product("bxmkjc,mjyq->bxyqkc", unpacked, back_table_y).astype(half)
    field_grad = product("bxyqkc,qkz->bxyzc", back_y, back_table_z).astype(half)
    return (field_grad, *updated)


def solution(mesh):
    owners, spaces = mesh.shape["dp"], mesh.shape["space"]
    pencils = MYZ // (owners * QUAD)
    if spaces == 2 * QUAD and MX == 2 * spaces and MYZ % (owners * QUAD * 8) == 0 and pencils * owners % 2 == 0:
        mesh = jax.sharding.Mesh(mesh.devices.reshape(owners, 2, QUAD), ("dp", "half", "quad"))
        space, on_device = ("half", "quad"), fast
    else:
        space, on_device = "space", general
    grid = P("dp", space, None, None, None)
    held = P(space, "dp", None, None, None)
    return jax.shard_map(
        on_device,
        mesh=mesh,
        in_specs=(grid, grid, held, held, held),
        out_specs=(grid, held, held, held),
        check_vma=False,
    )
```

```python
import functools
import math

import jax
import jax.numpy as jnp
import ml_dtypes
import numpy as np
from jax import lax
from jax.experimental import pallas as pl
from jax.experimental.pallas import tpu as pltpu
from jax.sharding import PartitionSpec as P

C = 128
MX = 16
MY = 16
MZ = 8
NY = 32
NZ = 16
STEP = 100
MYZ = 128
QUAD = 4


decay_first = 0.9
decay_second = 0.999
learn_rate = 0.001
adam_floor = 1e-08

f32 = jnp.float32
half = jnp.bfloat16


def np_tables(length, modes_kept, signed):
    points = np.arange(length)
    frequency = np.arange(modes_kept) - (modes_kept // 2 if signed else 0)
    angles = np.mod(points[:, None] * frequency[None, :], length) * (2.0 * math.pi / length)
    factor = np.float32(1.0 / math.sqrt(length))
    cosine = (np.cos(angles).astype(np.float32) * factor).astype(ml_dtypes.bfloat16)
    sine = (np.sin(angles).astype(np.float32) * factor).astype(ml_dtypes.bfloat16)
    return cosine.astype(np.float64), sine.astype(np.float64)


def yz_table(dp_count):
    cos_z, sin_z = np_tables(NZ, MZ, False)
    cos_y, sin_y = np_tables(NY, MY, True)
    cy, sy = cos_y.T[:, None, :, None], sin_y.T[:, None, :, None]
    cz, sz = cos_z.T[None, :, None, :], sin_z.T[None, :, None, :]
    real = cy * cz - sy * sz
    imag = -(sy * cz + cy * sz)
    table = np.stack([real, imag], axis=2).reshape(MYZ, 2, NY * NZ)
    pencils = MYZ // dp_count // QUAD
    table = table.reshape(dp_count, QUAD, pencils, 2, NY * NZ).transpose(1, 0, 2, 3, 4)
    return table.reshape(QUAD, dp_count * pencils * 2, NY * NZ).astype(ml_dtypes.bfloat16)


def x_tables(total_x, halves, pencils):
    cos_x, sin_x = np_tables(total_x, MX, True)
    same = np.eye(pencils)
    span = total_x // halves
    forward, backward = [], []
    for part in range(halves):
        c, s = cos_x[part * span : (part + 1) * span], sin_x[part * span : (part + 1) * span]
        fwd = np.zeros((MX, pencils, 2, span, pencils, 2))
        fwd[:, :, 0, :, :, 0] = np.einsum("xm,pr->mpxr", c, same)
        fwd[:, :, 0, :, :, 1] = np.einsum("xm,pr->mpxr", s, same)
        fwd[:, :, 1, :, :, 0] = np.einsum("xm,pr->mpxr", -s, same)
        fwd[:, :, 1, :, :, 1] = np.einsum("xm,pr->mpxr", c, same)
        bwd = np.zeros((span, pencils, 2, MX, pencils, 2))
        bwd[:, :, 0, :, :, 0] = np.einsum("xm,pr->xpmr", c, same)
        bwd[:, :, 0, :, :, 1] = np.einsum("xm,pr->xpmr", -s, same)
        bwd[:, :, 1, :, :, 0] = np.einsum("xm,pr->xpmr", s, same)
        bwd[:, :, 1, :, :, 1] = np.einsum("xm,pr->xpmr", c, same)
        forward.append(fwd.reshape(MX * pencils * 2, span * pencils * 2))
        backward.append(bwd.reshape(span * pencils * 2, MX * pencils * 2))
    return np.stack(forward).astype(ml_dtypes.bfloat16), np.stack(backward).astype(ml_dtypes.bfloat16)


def gather_tables(batch, halves, modes, pencils):
    plain = np.zeros((modes, pencils, batch, 2, batch, halves, modes, pencils, 2))
    turned = np.zeros_like(plain)
    for m in range(modes):
        for p in range(pencils):
            for b in range(batch):
                plain[m, p, b, 0, b, :, m, p, 0] = 1.0
                plain[m, p, b, 1, b, :, m, p, 1] = 1.0
                turned[m, p, b, 0, b, :, m, p, 1] = 1.0
                turned[m, p, b, 1, b, :, m, p, 0] = -1.0
    rows = modes * pencils * batch * 2
    both = np.stack([plain.reshape(rows, -1), turned.reshape(rows, -1)])
    return both.astype(ml_dtypes.bfloat16)


def scatter_table(batch, modes, pencils):
    order = np.arange(modes * pencils * batch * 2).reshape(modes * pencils, batch, 2).transpose(1, 0, 2).reshape(-1)
    return np.eye(order.size)[order].astype(ml_dtypes.bfloat16)


def dot(a, b, dims=((1,), (0,))):
    return lax.dot_general(a, b, (dims, ((), ())), preferred_element_type=f32)


def yz_transform(source, mixed, blocks):
    rows = mixed.shape[0] // QUAD
    for x in range(0, source.shape[0], 2):
        pair = jnp.concatenate([source[x], source[x + 1]], axis=1)
        result = dot(mixed[...], pair).astype(half)
        for r in range(QUAD):
            piece = result[r * rows : (r + 1) * rows]
            blocks[r][x] = piece[:, :C]
            blocks[r][x + 1] = piece[:, C:]


def yz_field_kernel(field, cotangent, table, later, *refs):
    blocks, (mixed, cot_held, later_held, cells_in, sems) = refs[:QUAD], refs[QUAD:]
    rows = table.shape[1]
    loads = [
        pltpu.make_async_copy(table.at[lax.axis_index("quad") ^ r], mixed.at[pl.ds(r * rows, rows)], sems.at[r]) for r in range(QUAD)
    ]
    for source, target in ((field, cells_in), (cotangent, cot_held), (later, later_held)):
        loads.append(pltpu.make_async_copy(source, target, sems.at[len(loads)]))
    for load in loads:
        load.start()
    for load in loads[: QUAD + 1]:
        load.wait()
    yz_transform(cells_in, mixed, blocks)
    for load in loads[QUAD + 1 :]:
        load.wait()


def yz_cot_kernel(cot_held, mixed, *blocks):
    yz_transform(cot_held, mixed, blocks)


def x_transform(pieces, table, held):
    for r in range(QUAD):
        held[lax.axis_index("quad") ^ r] = pieces[r][...]
    matrix = table[lax.axis_index("half")]
    cells, rows = held.shape[1:3]
    height = matrix.shape[1] // QUAD // cells
    results = []
    for d in range(0, rows // height, 2):
        columns = [
            jnp.concatenate(
                [held[q, x, k * height : (k + 1) * height, :] for q in range(QUAD) for x in range(cells)], axis=0
            )
            for k in (d, d + 1)
        ]
        result = dot(matrix, jnp.concatenate(columns, axis=1)).astype(half)
        results += [result[:, :C], result[:, C:]]
    return results


def x_kernel(extra, *refs):
    pieces, table, (own, other, held, split) = refs[:QUAD], refs[QUAD], refs[QUAD + 1 + extra :]
    for d, result in enumerate(x_transform(pieces, table, held)):
        split[:, d * QUAD : (d + 1) * QUAD] = result.reshape(split.shape[0], QUAD, -1, C)
    own[...] = split[lax.axis_index("half")]
    other[...] = split[1 - lax.axis_index("half")]


def sum_kernel(field_own, field_come, cot_own, cot_come, *refs):
    out = refs[-1]
    for which, (own, come) in enumerate(((field_own, field_come), (cot_own, cot_come))):
        out[:, which] = (own[...].astype(f32) + come[...].astype(f32)).astype(half)


def start_all(loads):
    for load in loads:
        load.start()


def stage_kernel(after, weights, *refs):
    count = (len(refs) - 3) // 2
    sources, weights_held, held = refs[:count], refs[count], refs[count + 1 : 2 * count + 1]
    rounded, sems = refs[2 * count + 1 :]
    del after
    modes, pencils = weights.shape[:2]
    each = pencils // 4
    spans = [(m, p) for m in range(modes) for p in range(0, pencils, each)]
    loads = []

    def add(source, target):
        loads.append(pltpu.make_async_copy(source, target, sems.at[len(loads)]))

    for m, p in spans:
        add(weights.at[m, p : p + each], weights_held.at[m, p : p + each])
    for source, target in zip(sources, held):
        if len(source.shape) < 5:
            add(source, target)
        else:
            for m, p in spans:
                add(source.at[m, p : p + each], target.at[m, p : p + each])
    for load in loads:
        load.start()
    for k, (m, p) in enumerate(spans):
        loads[k].wait()

        def body(i, carry):
            for part in range(2):
                rounded[m, p + i, :, part * C : (part + 1) * C] = weights_held[m, p + i, part].astype(half)
            return carry

        lax.fori_loop(0, each, body, 0)
    for load in loads[len(spans) :]:
        load.wait()


def modes_kernel(arrived, weights, gather, scatter, sent, inputs, pairs):
    batch, quad, _, rows, _ = arrived.shape
    modes, pencils = weights.shape[0], weights.shape[1] // quad
    height = batch * 2
    for q in range(quad):
        field = arrived[:, q, 0].reshape(-1, C)
        cot = arrived[:, q, 1].reshape(-1, C)
        both = dot(gather[0], jnp.concatenate([field, cot], axis=1)).astype(half)
        inputs[q] = both[:, :C]
        pair = jnp.concatenate([both[:, C:], dot(gather[1], cot).astype(half)], axis=1)
        pairs[q] = pair
        results = []
        for m in range(modes):
            for p in range(0, pencils, 2):
                at = (m * pencils + p) * height
                first = q * pencils + p
                columns = weights[m, first : first + 2].reshape(2 * C, 2 * C)
                result = dot(pair[at : at + 2 * height], columns, ((1,), (1,)))
                results += [result[:height, :C], result[height:, C:]]
        grads = jnp.concatenate(results, axis=0).astype(half)
        sent[:, q] = dot(scatter[...], grads).astype(half).reshape(batch, rows, C)


def adam_kernel(begin, inputs, pairs, weights, first, second, *refs):
    new_weights, new_first, new_second, token, held, sems = refs[-6:]
    new = (new_weights, new_first, new_second)
    modes, pencils = weights.shape[:2]
    steps, count = held.shape[1:3]
    height = inputs.shape[1] // (modes * (pencils // QUAD))
    per_mode = pencils // count
    per_quad = per_mode // QUAD
    scale_first = learn_rate / (1.0 - decay_first**STEP)
    scale_second = 1.0 / (1.0 - decay_second**STEP)

    def copies(i):
        mode, at = (i + begin) // per_mode, (i + begin) % per_mode
        return [
            pltpu.make_async_copy(held.at[o, i], new[o].at[mode, pl.ds(at * count, count)], sems.at[i, o])
            for o in range(3)
        ]

    def body(i, carry):
        mode, at = (i + begin) // per_mode, (i + begin) % per_mode
        rows = count * height
        row = pl.multiple_of((mode * per_quad + at % per_quad) * rows, rows)
        us = inputs[at // per_quad, pl.ds(row, rows), :]
        gs = pairs[at // per_quad, pl.ds(row, rows), :]
        for k in range(count):
            u = us[k * height : (k + 1) * height]
            g = gs[k * height : (k + 1) * height]
            grads = dot(u, g, ((0,), (0,)))
            p = at * count + k
            for part in range(2):
                grad = grads[:, part * C : (part + 1) * C]
                m = decay_first * first[mode, p, part] + (1.0 - decay_first) * grad
                v = decay_second * second[mode, p, part] + ((1.0 - decay_second) * grad) * grad
                held[1, i, k, part] = m
                held[2, i, k, part] = v
                level = v * scale_second
                inverse = lax.rsqrt(level)
                floored = level * inverse + adam_floor
                inverse = inverse * (2.0 - floored * inverse)
                held[0, i, k, part] = weights[mode, p, part] - (scale_first * m) * inverse
        for copy in copies(i):
            copy.start()
        return carry

    def finish(i, carry):
        for copy in copies(i):
            copy.wait()
        return carry

    lax.fori_loop(0, steps, body, 0)
    lax.fori_loop(0, steps, finish, 0)
    token[...] = jnp.zeros_like(token)


def back_x_kernel(own, come, table, after, *refs):
    blocks, (arrived, held) = refs[:QUAD], refs[QUAD:]
    arrived[lax.axis_index("half")] = own[...]
    arrived[1 - lax.axis_index("half")] = come[...]
    matrix = table[lax.axis_index("half")]
    cells, owners, height, _ = blocks[0].shape
    halves = arrived.shape[0]
    span = cells * height
    for d in range(0, owners, 2):
        columns = [
            jnp.concatenate([arrived[h, k * QUAD : (k + 1) * QUAD].reshape(-1, C) for h in range(halves)], axis=0)
            for k in (d, d + 1)
        ]
        result = dot(matrix, jnp.concatenate(columns, axis=1)).astype(half)
        for q in range(QUAD):
            piece = result[q * span : (q + 1) * span].reshape(cells, height, 2 * C)
            held[q, :, d] = piece[:, :, :C]
            held[q, :, d + 1] = piece[:, :, C:]
    for r in range(QUAD):
        blocks[r][...] = held[lax.axis_index("quad") ^ r]


def back_yz_kernel(*refs):
    pieces, (table, after, out, held) = refs[:QUAD], refs[QUAD:]
    for r in range(QUAD):
        held[lax.axis_index("quad") ^ r] = pieces[r][...]
    matrix = table[...]
    for x in range(0, out.shape[0], 2):
        columns = jnp.concatenate([held[:, k].reshape(-1, C) for k in (x, x + 1)], axis=1)
        result = dot(matrix, columns).astype(half)
        out[x] = result[:, :C]
        out[x + 1] = result[:, C:]


VMEM = pl.BlockSpec(memory_space=pltpu.VMEM)
HBM = pl.BlockSpec(memory_space=pltpu.HBM)
ANY = pl.BlockSpec(memory_space=pl.ANY)
MIB = 1 << 20


def params(mib, **more):
    return pltpu.CompilerParams(vmem_limit_bytes=mib * MIB, **more)


def cost(size):
    return pl.CostEstimate(flops=0, bytes_accessed=size, transcendentals=0)


def in_hbm(values):
    return pltpu.with_memory_space_constraint(values, pltpu.HBM)


def exchange(blocks):
    moved = [lax.ppermute(blocks[r], "quad", [(q, q ^ r) for q in range(QUAD)]) for r in range(1, QUAD)]
    return [blocks[0]] + moved


def swap_halves(values):
    return lax.ppermute(values, "half", [(0, 1), (1, 0)])


def fast(field, cotangent, weights, first_moment, second_moment):
    halves = lax.axis_size("half")
    spaces = halves * QUAD
    owners = lax.axis_size("dp")
    cells = field.shape[1]
    total_x = cells * spaces
    pencils = MYZ // owners // QUAD
    modes = MX // spaces
    height = pencils * 2
    table_yz = yz_table(owners)
    table_x, back_table_x = x_tables(total_x, halves, pencils)
    back_table_yz = np.ascontiguousarray(table_yz.reshape(MYZ * 2, NY * NZ).T)
    gather = gather_tables(owners, 1, modes, pencils)
    scatter = scatter_table(owners, modes, pencils)
    vmem = lambda values: pltpu.VMEM(values.shape, values.dtype)

    flat = (cells, NY * NZ, C)
    block = pltpu.VMEM((cells, owners * height, C), half)
    *field_blocks, mixed, cot_held, table_x = pl.pallas_call(
        yz_field_kernel,
        out_shape=[block] * QUAD + [pltpu.VMEM((MYZ * 2, NY * NZ), half), pltpu.VMEM(flat, half), vmem(table_x)],
        in_specs=[HBM] * 4,
        out_specs=[VMEM] * (QUAD + 3),
        scratch_shapes=[pltpu.VMEM(flat, half), pltpu.SemaphoreType.DMA((QUAD + 3,))],
        compiler_params=params(8),
        name="yz_modes_field",
    )(
        in_hbm(field.reshape(flat)),
        in_hbm(cotangent.reshape(flat)),
        in_hbm(jnp.asarray(table_yz)),
        in_hbm(jnp.asarray(table_x)),
    )
    cot_blocks = pl.pallas_call(
        yz_cot_kernel,
        out_shape=[block] * QUAD,
        in_specs=[VMEM] * 2,
        out_specs=[VMEM] * QUAD,
        compiler_params=params(8),
        name="yz_modes_cot",
    )(cot_held, mixed)

    split = (modes, QUAD * pencils, 2, C, C)
    big, first, second = weights.reshape(split), first_moment.reshape(split), second_moment.reshape(split)
    field_blocks = exchange(field_blocks)
    cot_blocks = exchange(cot_blocks)

    rows = modes * height
    per_half = (owners * QUAD, rows, C)
    gathered = pltpu.VMEM((QUAD, cells, owners * height, C), half)

    def x_modes(pieces, *after):
        return pl.pallas_call(
            functools.partial(x_kernel, len(after)),
            out_shape=[pltpu.VMEM(per_half, half)] * 2,
            in_specs=[VMEM] * (QUAD + 1) + [ANY] * len(after),
            out_specs=[VMEM] * 2,
            scratch_shapes=[gathered, pltpu.VMEM((halves,) + per_half, half)],
            compiler_params=params(8),
            name="x_modes",
        )(*pieces, table_x, *after)

    field_own, field_other = x_modes(field_blocks)
    field_come = swap_halves(field_other)
    cot_own, cot_other = x_modes(cot_blocks, field_other)
    cot_come = swap_halves(cot_other)
    staged = [jnp.asarray(t) for t in (gather, scatter, back_table_x, back_table_yz)]
    weights_held, gather, scatter, back_table_x, back_table_yz, rounded = pl.pallas_call(
        stage_kernel,
        out_shape=[vmem(big)] + [vmem(t) for t in staged] + [pltpu.VMEM((modes, QUAD * pencils, C, 2 * C), half)],
        in_specs=[ANY] + [HBM] * (1 + len(staged)),
        out_specs=[VMEM] * (2 + len(staged)),
        scratch_shapes=[pltpu.SemaphoreType.DMA((12 * modes + len(staged) - 2,))],
        compiler_params=params(8),
        cost_estimate=cost(0),
        name="stage",
    )(cot_other, in_hbm(big), *[in_hbm(t) for t in staged])
    summed = pl.pallas_call(
        sum_kernel,
        out_shape=pltpu.VMEM((owners * QUAD, 2, rows, C), half),
        in_specs=[VMEM] * 4 + [ANY],
        out_specs=VMEM,
        compiler_params=params(8),
        name="sum_halves",
    )(field_own, field_come, cot_own, cot_come, rounded)
    arrived = lax.all_to_all(summed, ("dp", "quad"), 0, 0, tiled=True)

    mode_rows = rows * owners
    sent, inputs, pairs = pl.pallas_call(
        modes_kernel,
        out_shape=[
            pltpu.VMEM((owners, QUAD, rows, C), half),
            pltpu.VMEM((QUAD, mode_rows, C), half),
            pltpu.VMEM((QUAD, mode_rows, 2 * C), half),
        ],
        in_specs=[VMEM] * 4,
        out_specs=[VMEM] * 3,
        compiler_params=params(8),
        name="mode_grads",
    )(arrived.reshape(owners, QUAD, 2, rows, C), rounded, gather, scatter)
    back = lax.all_to_all(sent.reshape(per_half), ("dp", "quad"), 0, 0, tiled=True)
    back_come = swap_halves(back)

    count = 4
    total = modes * QUAD * pencils // count
    first_steps = total * 12 // 16

    def adam(begin, end, after, *before):
        steps = end - begin
        return pl.pallas_call(
            functools.partial(adam_kernel, begin),
            out_shape=[pltpu.HBM(split, f32)] * 3 + [pltpu.VMEM((8, C), f32)],
            in_specs=[VMEM] * 5 + [ANY] + [HBM] * len(before),
            out_specs=[HBM] * 3 + [VMEM],
            scratch_shapes=[
                pltpu.VMEM((3, steps, count, 2, C, C), f32),
                pltpu.SemaphoreType.DMA((steps, 3)),
            ],
            input_output_aliases={6 + k: k for k in range(len(before))},
            compiler_params=params(22),
            cost_estimate=cost(16 * weights.size * steps // total),
            name="adam",
        )(inputs, pairs, weights_held, first, second, after, *before)

    *updated, token = adam(0, first_steps, back)
    blocks = pl.pallas_call(
        back_x_kernel,
        out_shape=[pltpu.VMEM((cells, owners, height, C), half)] * QUAD,
        in_specs=[VMEM] * 3 + [ANY],
        out_specs=[VMEM] * QUAD,
        scratch_shapes=[
            pltpu.VMEM((halves,) + per_half, half),
            pltpu.VMEM((QUAD, cells, owners, height, C), half),
        ],
        compiler_params=params(8),
        name="back_x",
    )(back, back_come, back_table_x, token)
    *updated, token = adam(first_steps, total, blocks[1], *updated)
    blocks = exchange(blocks)
    field_grad = pl.pallas_call(
        back_yz_kernel,
        out_shape=jax.ShapeDtypeStruct((cells, NY * NZ, C), half),
        in_specs=[VMEM] * (QUAD + 1) + [ANY],
        out_specs=VMEM,
        scratch_shapes=[pltpu.VMEM((QUAD, cells, owners, height, C), half)],
        compiler_params=params(8),
        name="back_yz",
    )(*blocks, back_table_yz, token)
    return (field_grad.reshape(field.shape), *[values.reshape(weights.shape) for values in updated])


def trig_tables(length, modes_kept, signed):
    cosine, sine_part = np_tables(length, modes_kept, signed)
    return jnp.asarray(cosine, half), jnp.asarray(sine_part, half)


def forward_table(cosine, sine_part):
    real_row = jnp.stack([cosine, -sine_part], axis=-1)
    imag_row = jnp.stack([sine_part, cosine], axis=-1)
    return jnp.stack([real_row, imag_row], axis=1)


def inverse_table(cosine, sine_part):
    real_row = jnp.stack([cosine.T, sine_part.T], axis=-1)
    imag_row = jnp.stack([-sine_part.T, cosine.T], axis=-1)
    return jnp.stack([real_row, imag_row], axis=1)


def adam_update(weights, first_moment, second_moment, weight_grads):
    new_first = decay_first * first_moment + (1.0 - decay_first) * weight_grads
    new_second = decay_second * second_moment + (1.0 - decay_second) * weight_grads * weight_grads
    first_hat = new_first / (1.0 - decay_first**STEP)
    second_hat = new_second / (1.0 - decay_second**STEP)
    new_weights = weights - learn_rate * first_hat / (jnp.sqrt(second_hat) + adam_floor)
    return (new_weights, new_first, new_second)


def general(field, cotangent, weights, first_moment, second_moment):
    slab_count = lax.axis_size("space")
    batch_local = field.shape[0]
    cells_x = field.shape[1]
    total_x = cells_x * slab_count
    cos_z, sin_z = trig_tables(NZ, MZ, False)
    cos_y, sin_y = trig_tables(NY, MY, True)
    cos_x, sin_x = trig_tables(total_x, MX, True)
    table_z = jnp.stack([cos_z, -sin_z], axis=1)
    table_y = forward_table(cos_y, sin_y)
    table_x = forward_table(cos_x, sin_x)
    back_table_x = inverse_table(cos_x, sin_x)
    back_table_y = inverse_table(cos_y, sin_y)
    back_table_z = jnp.stack([cos_z.T, -sin_z.T], axis=0)
    product = functools.partial(jnp.einsum, preferred_element_type=f32)

    def swap(values, axis, split, concat):
        return lax.all_to_all(values, axis, split_axis=split, concat_axis=concat, tiled=True)

    def to_modes(slab_field):
        first_pass = product("bxyzc,zpk->bxypkc", slab_field, table_z).astype(half)
        second = product("bxypkc,ypmq->bxmkqc", first_pass, table_y).astype(half)
        second = second.reshape(batch_local, cells_x, MYZ, 2, C)
        along = product("bxpjc,xjmq->bmpqc", swap(second, "space", 2, 1), table_x).astype(half)
        return swap(swap(along, "space", 1, 2), "dp", 2, 0)

    field_hat = to_modes(field)
    cot_hat = to_modes(cotangent)
    rotated = jnp.stack([cot_hat[:, :, :, 1], -cot_hat[:, :, :, 0]], axis=3)
    form_in = "bmpjc,bmpjo->mpco"
    weight_grads = jnp.stack([product(form_in, field_hat, cot_hat), product(form_in, field_hat, rotated)], axis=2)
    half_weights = weights.astype(half)
    form_back = "mpjio,bmpjo->bmpi"
    mode_grads = jnp.stack(
        [product(form_back, half_weights, cot_hat), product(form_back, half_weights, rotated)], axis=3
    ).astype(half)
    updated = adam_update(weights, first_moment, second_moment, weight_grads)
    pencils = swap(swap(mode_grads, "dp", 0, 2), "space", 2, 1)
    back_x = product("bmpjc,mjxq->bxpqc", pencils, back_table_x).astype(half)
    unpacked = swap(back_x, "space", 1, 2).reshape(batch_local, cells_x, MY, MZ, 2, C)
    back_y = product("bxmkjc,mjyq->bxyqkc", unpacked, back_table_y).astype(half)
    field_grad = product("bxyqkc,qkz->bxyzc", back_y, back_table_z).astype(half)
    return (field_grad, *updated)


def solution(mesh):
    owners, spaces = mesh.shape["dp"], mesh.shape["space"]
    pencils = MYZ // (owners * QUAD)
    if spaces == 2 * QUAD and MX == 2 * spaces and MYZ % (owners * QUAD * 8) == 0 and pencils * owners % 2 == 0:
        mesh = jax.sharding.Mesh(mesh.devices.reshape(owners, 2, QUAD), ("dp", "half", "quad"))
        space, on_device = ("half", "quad"), fast
    else:
        space, on_device = "space", general
    grid = P("dp", space, None, None, None)
    held = P(space, "dp", None, None, None)
    return jax.shard_map(
        on_device,
        mesh=mesh,
        in_specs=(grid, grid, held, held, held),
        out_specs=(grid, held, held, held),
        check_vma=False,
    )
```

```python
import functools
import math

import jax
import jax.numpy as jnp
import ml_dtypes
import numpy as np
from jax import lax
from jax.experimental import pallas as pl
from jax.experimental.pallas import tpu as pltpu
from jax.sharding import PartitionSpec as P

C = 128
MX = 16
MY = 16
MZ = 8
NY = 32
NZ = 16
STEP = 100
MYZ = 128
QUAD = 4


decay_first = 0.9
decay_second = 0.999
learn_rate = 0.001
adam_floor = 1e-08

f32 = jnp.float32
half = jnp.bfloat16


def np_tables(length, modes_kept, signed):
    points = np.arange(length)
    frequency = np.arange(modes_kept) - (modes_kept // 2 if signed else 0)
    angles = np.mod(points[:, None] * frequency[None, :], length) * (2.0 * math.pi / length)
    factor = np.float32(1.0 / math.sqrt(length))
    cosine = (np.cos(angles).astype(np.float32) * factor).astype(ml_dtypes.bfloat16)
    sine = (np.sin(angles).astype(np.float32) * factor).astype(ml_dtypes.bfloat16)
    return cosine.astype(np.float64), sine.astype(np.float64)


def yz_table(dp_count):
    cos_z, sin_z = np_tables(NZ, MZ, False)
    cos_y, sin_y = np_tables(NY, MY, True)
    cy, sy = cos_y.T[:, None, :, None], sin_y.T[:, None, :, None]
    cz, sz = cos_z.T[None, :, None, :], sin_z.T[None, :, None, :]
    real = cy * cz - sy * sz
    imag = -(sy * cz + cy * sz)
    table = np.stack([real, imag], axis=2).reshape(MYZ, 2, NY * NZ)
    pencils = MYZ // dp_count // QUAD
    table = table.reshape(dp_count, QUAD, pencils, 2, NY * NZ).transpose(1, 0, 2, 3, 4)
    return table.reshape(QUAD, dp_count * pencils * 2, NY * NZ).astype(ml_dtypes.bfloat16)


def x_tables(total_x, halves, pencils):
    cos_x, sin_x = np_tables(total_x, MX, True)
    same = np.eye(pencils)
    span = total_x // halves
    forward, backward = [], []
    for part in range(halves):
        c, s = cos_x[part * span : (part + 1) * span], sin_x[part * span : (part + 1) * span]
        fwd = np.zeros((MX, pencils, 2, span, pencils, 2))
        fwd[:, :, 0, :, :, 0] = np.einsum("xm,pr->mpxr", c, same)
        fwd[:, :, 0, :, :, 1] = np.einsum("xm,pr->mpxr", s, same)
        fwd[:, :, 1, :, :, 0] = np.einsum("xm,pr->mpxr", -s, same)
        fwd[:, :, 1, :, :, 1] = np.einsum("xm,pr->mpxr", c, same)
        bwd = np.zeros((span, pencils, 2, MX, pencils, 2))
        bwd[:, :, 0, :, :, 0] = np.einsum("xm,pr->xpmr", c, same)
        bwd[:, :, 0, :, :, 1] = np.einsum("xm,pr->xpmr", -s, same)
        bwd[:, :, 1, :, :, 0] = np.einsum("xm,pr->xpmr", s, same)
        bwd[:, :, 1, :, :, 1] = np.einsum("xm,pr->xpmr", c, same)
        forward.append(fwd.reshape(MX * pencils * 2, span * pencils * 2))
        backward.append(bwd.reshape(span * pencils * 2, MX * pencils * 2))
    return np.stack(forward).astype(ml_dtypes.bfloat16), np.stack(backward).astype(ml_dtypes.bfloat16)


def gather_tables(batch, halves, modes, pencils):
    plain = np.zeros((modes, pencils, batch, 2, batch, halves, modes, pencils, 2))
    turned = np.zeros_like(plain)
    for m in range(modes):
        for p in range(pencils):
            for b in range(batch):
                plain[m, p, b, 0, b, :, m, p, 0] = 1.0
                plain[m, p, b, 1, b, :, m, p, 1] = 1.0
                turned[m, p, b, 0, b, :, m, p, 1] = 1.0
                turned[m, p, b, 1, b, :, m, p, 0] = -1.0
    rows = modes * pencils * batch * 2
    both = np.stack([plain.reshape(rows, -1), turned.reshape(rows, -1)])
    return both.astype(ml_dtypes.bfloat16)


def scatter_table(batch, modes, pencils):
    order = np.arange(modes * pencils * batch * 2).reshape(modes * pencils, batch, 2).transpose(1, 0, 2).reshape(-1)
    return np.eye(order.size)[order].astype(ml_dtypes.bfloat16)


def dot(a, b, dims=((1,), (0,))):
    return lax.dot_general(a, b, (dims, ((), ())), preferred_element_type=f32)


def yz_kernel(field, cotangent, table, *refs):
    blocks, (mixed, cells_in, sems) = refs[:QUAD], refs[QUAD:]
    rows = table.shape[1]
    cells = field.shape[0]
    loads = [
        pltpu.make_async_copy(table.at[lax.axis_index("quad") ^ r], mixed.at[pl.ds(r * rows, rows)], sems.at[r]) for r in range(QUAD)
    ]
    for which, source in enumerate((field, cotangent)):
        loads.append(pltpu.make_async_copy(source, cells_in.at[which], sems.at[len(loads)]))
    for load in loads:
        load.start()
    for load in loads:
        load.wait()
    for which in range(2):
        for x in range(0, cells, 2):
            pair = jnp.concatenate([cells_in[which, x], cells_in[which, x + 1]], axis=1)
            result = dot(mixed[...], pair).astype(half)
            for r in range(QUAD):
                piece = result[r * rows : (r + 1) * rows]
                blocks[r][which, x] = piece[:, :C]
                blocks[r][which, x + 1] = piece[:, C:]


def x_kernel(*refs):
    pieces, (table, out, held) = refs[:QUAD], refs[QUAD:]
    for r in range(QUAD):
        held[lax.axis_index("quad") ^ r] = pieces[r][...]
    matrix = table[lax.axis_index("half")]
    fields, cells, rows = held.shape[1:4]
    height = matrix.shape[1] // QUAD // cells
    spaces = out.shape[0] // (rows // height)
    for d in range(rows // height):
        columns = [
            jnp.concatenate(
                [held[q, f, x, d * height : (d + 1) * height, :] for q in range(QUAD) for x in range(cells)], axis=0
            )
            for f in range(fields)
        ]
        result = dot(matrix, jnp.concatenate(columns, axis=1)).astype(half)
        for f in range(fields):
            out[d * spaces : (d + 1) * spaces, f] = result[:, f * C : (f + 1) * C].reshape(spaces, -1, C)


def stage_kernel(after, weights, *refs):
    count = (len(refs) - 3) // 2
    sources, weights_held, held = refs[:count], refs[count], refs[count + 1 : 2 * count + 1]
    rounded, sems = refs[2 * count + 1 :]
    del after
    modes, pencils = weights.shape[:2]
    each = pencils // 4
    spans = [(m, p) for m in range(modes) for p in range(0, pencils, each)]
    loads = []

    def add(source, target):
        loads.append(pltpu.make_async_copy(source, target, sems.at[len(loads)]))

    for m, p in spans:
        add(weights.at[m, p : p + each], weights_held.at[m, p : p + each])
    for source, target in zip(sources, held):
        if len(source.shape) < 5:
            add(source, target)
        else:
            for m, p in spans:
                add(source.at[m, p : p + each], target.at[m, p : p + each])
    for load in loads:
        load.start()
    for k, (m, p) in enumerate(spans):
        loads[k].wait()

        def body(i, carry):
            for part in range(2):
                rounded[m, p + i, :, part * C : (part + 1) * C] = weights_held[m, p + i, part].astype(half)
            return carry

        lax.fori_loop(0, each, body, 0)
    for load in loads[len(spans) :]:
        load.wait()


def modes_kernel(arrived, weights, gather, scatter, sent, inputs, pairs):
    batch, halves, quad, _, rows, _ = arrived.shape
    modes, pencils = weights.shape[0], weights.shape[1] // quad
    height = batch * 2
    for q in range(quad):
        field = arrived[:, :, q, 0].reshape(-1, C)
        cot = arrived[:, :, q, 1].reshape(-1, C)
        both = dot(gather[0], jnp.concatenate([field, cot], axis=1)).astype(half)
        inputs[q] = both[:, :C]
        pair = jnp.concatenate([both[:, C:], dot(gather[1], cot).astype(half)], axis=1)
        pairs[q] = pair
        results = []
        for m in range(modes):
            for p in range(0, pencils, 2):
                at = (m * pencils + p) * height
                first = q * pencils + p
                columns = weights[m, first : first + 2].reshape(2 * C, 2 * C)
                result = dot(pair[at : at + 2 * height], columns, ((1,), (1,)))
                results += [result[:height, :C], result[height:, C:]]
        grads = jnp.concatenate(results, axis=0).astype(half)
        sent[:, q] = dot(scatter[...], grads).astype(half).reshape(batch, rows, C)


def adam_kernel(begin, inputs, pairs, weights, first, second, *refs):
    new_weights, new_first, new_second, token, held, sems = refs[-6:]
    new = (new_weights, new_first, new_second)
    modes, pencils = weights.shape[:2]
    steps, count = held.shape[1:3]
    height = inputs.shape[1] // (modes * (pencils // QUAD))
    per_mode = pencils // count
    per_quad = per_mode // QUAD
    scale_first = learn_rate / (1.0 - decay_first**STEP)
    scale_second = 1.0 / (1.0 - decay_second**STEP)

    def copies(i):
        mode, at = (i + begin) // per_mode, (i + begin) % per_mode
        return [
            pltpu.make_async_copy(held.at[o, i], new[o].at[mode, pl.ds(at * count, count)], sems.at[i, o])
            for o in range(3)
        ]

    def body(i, carry):
        mode, at = (i + begin) // per_mode, (i + begin) % per_mode
        rows = count * height
        row = pl.multiple_of((mode * per_quad + at % per_quad) * rows, rows)
        us = inputs[at // per_quad, pl.ds(row, rows), :]
        gs = pairs[at // per_quad, pl.ds(row, rows), :]
        for k in range(count):
            u = us[k * height : (k + 1) * height]
            g = gs[k * height : (k + 1) * height]
            grads = dot(u, g, ((0,), (0,)))
            p = at * count + k
            for part in range(2):
                grad = grads[:, part * C : (part + 1) * C]
                m = decay_first * first[mode, p, part] + (1.0 - decay_first) * grad
                v = decay_second * second[mode, p, part] + ((1.0 - decay_second) * grad) * grad
                held[1, i, k, part] = m
                held[2, i, k, part] = v
                level = v * scale_second
                inverse = lax.rsqrt(level)
                floored = level * inverse + adam_floor
                inverse = inverse * (2.0 - floored * inverse)
                held[0, i, k, part] = weights[mode, p, part] - (scale_first * m) * inverse
        for copy in copies(i):
            copy.start()
        return carry

    def finish(i, carry):
        for copy in copies(i):
            copy.wait()
        return carry

    lax.fori_loop(0, steps, body, 0)
    lax.fori_loop(0, steps, finish, 0)
    token[...] = jnp.zeros_like(token)


def back_x_kernel(own, come, table, after, *refs):
    blocks, (arrived, held) = refs[:QUAD], refs[QUAD:]
    arrived[lax.axis_index("half")] = own[...]
    arrived[1 - lax.axis_index("half")] = come[...]
    matrix = table[lax.axis_index("half")]
    cells, owners, height, _ = blocks[0].shape
    halves = arrived.shape[0]
    span = cells * height
    for d in range(0, owners, 2):
        columns = [
            jnp.concatenate([arrived[h, k * QUAD : (k + 1) * QUAD].reshape(-1, C) for h in range(halves)], axis=0)
            for k in (d, d + 1)
        ]
        result = dot(matrix, jnp.concatenate(columns, axis=1)).astype(half)
        for q in range(QUAD):
            piece = result[q * span : (q + 1) * span].reshape(cells, height, 2 * C)
            held[q, :, d] = piece[:, :, :C]
            held[q, :, d + 1] = piece[:, :, C:]
    for r in range(QUAD):
        blocks[r][...] = held[lax.axis_index("quad") ^ r]


def back_yz_kernel(*refs):
    pieces, (table, after, out, held) = refs[:QUAD], refs[QUAD:]
    for r in range(QUAD):
        held[lax.axis_index("quad") ^ r] = pieces[r][...]
    matrix = table[...]
    for x in range(0, out.shape[0], 2):
        columns = jnp.concatenate([held[:, k].reshape(-1, C) for k in (x, x + 1)], axis=1)
        result = dot(matrix, columns).astype(half)
        out[x] = result[:, :C]
        out[x + 1] = result[:, C:]


VMEM = pl.BlockSpec(memory_space=pltpu.VMEM)
HBM = pl.BlockSpec(memory_space=pltpu.HBM)
ANY = pl.BlockSpec(memory_space=pl.ANY)
MIB = 1 << 20


def params(mib, **more):
    return pltpu.CompilerParams(vmem_limit_bytes=mib * MIB, **more)


def cost(size):
    return pl.CostEstimate(flops=0, bytes_accessed=size, transcendentals=0)


def in_hbm(values):
    return pltpu.with_memory_space_constraint(values, pltpu.HBM)


def exchange(blocks):
    moved = [lax.ppermute(blocks[r], "quad", [(q, q ^ r) for q in range(QUAD)]) for r in range(1, QUAD)]
    return [blocks[0]] + moved


def swap_halves(values):
    return lax.ppermute(values, "half", [(0, 1), (1, 0)])


def fast(field, cotangent, weights, first_moment, second_moment):
    halves = lax.axis_size("half")
    spaces = halves * QUAD
    owners = lax.axis_size("dp")
    cells = field.shape[1]
    total_x = cells * spaces
    pencils = MYZ // owners // QUAD
    modes = MX // spaces
    height = pencils * 2
    table_yz = yz_table(owners)
    table_x, back_table_x = x_tables(total_x, halves, pencils)
    back_table_yz = np.ascontiguousarray(table_yz.reshape(MYZ * 2, NY * NZ).T)
    gather = gather_tables(owners, halves, modes, pencils)
    scatter = scatter_table(owners, modes, pencils)
    vmem = lambda values: pltpu.VMEM(values.shape, values.dtype)

    flat = (cells, NY * NZ, C)
    blocks = pl.pallas_call(
        yz_kernel,
        out_shape=[pltpu.VMEM((2, cells, owners * height, C), half)] * QUAD,
        in_specs=[HBM] * 3,
        out_specs=[VMEM] * QUAD,
        scratch_shapes=[
            pltpu.VMEM((MYZ * 2, NY * NZ), half),
            pltpu.VMEM((2,) + flat, half),
            pltpu.SemaphoreType.DMA((QUAD + 2,)),
        ],
        compiler_params=params(8),
        name="yz_modes",
    )(in_hbm(field.reshape(flat)), in_hbm(cotangent.reshape(flat)), in_hbm(jnp.asarray(table_yz)))

    split = (modes, QUAD * pencils, 2, C, C)
    big, first, second = weights.reshape(split), first_moment.reshape(split), second_moment.reshape(split)
    staged = [jnp.asarray(t) for t in (table_x, gather, scatter, back_table_x, back_table_yz)]
    weights_held, table_x, gather, scatter, back_table_x, back_table_yz, rounded = pl.pallas_call(
        stage_kernel,
        out_shape=[vmem(big)] + [vmem(t) for t in staged] + [pltpu.VMEM((modes, QUAD * pencils, C, 2 * C), half)],
        in_specs=[ANY] + [HBM] * (1 + len(staged)),
        out_specs=[VMEM] * (2 + len(staged)),
        scratch_shapes=[pltpu.SemaphoreType.DMA((4 * modes + len(staged),))],
        compiler_params=params(8),
        cost_estimate=cost(0),
        name="stage",
    )(blocks[0], in_hbm(big), *[in_hbm(t) for t in staged])
    blocks = exchange(blocks)

    rows = modes * height
    per_half = (owners * QUAD, rows, C)
    partial = pl.pallas_call(
        x_kernel,
        out_shape=pltpu.VMEM((owners * spaces, 2, rows, C), half),
        in_specs=[VMEM] * (QUAD + 1),
        out_specs=VMEM,
        scratch_shapes=[pltpu.VMEM((QUAD, 2, cells, owners * height, C), half)],
        compiler_params=params(8),
        name="x_modes",
    )(*blocks, table_x)
    arrived = lax.all_to_all(partial, ("dp", "half", "quad"), 0, 0, tiled=True)

    mode_rows = rows * owners
    sent, inputs, pairs = pl.pallas_call(
        modes_kernel,
        out_shape=[
            pltpu.VMEM((owners, QUAD, rows, C), half),
            pltpu.VMEM((QUAD, mode_rows, C), half),
            pltpu.VMEM((QUAD, mode_rows, 2 * C), half),
        ],
        in_specs=[VMEM] * 4,
        out_specs=[VMEM] * 3,
        compiler_params=params(8),
        name="mode_grads",
    )(arrived.reshape(owners, halves, QUAD, 2, rows, C), rounded, gather, scatter)
    back = lax.all_to_all(sent.reshape(per_half), ("dp", "quad"), 0, 0, tiled=True)
    back_come = swap_halves(back)

    count = 4
    total = modes * QUAD * pencils // count
    first_steps = total * 12 // 16

    def adam(begin, end, after, *before):
        steps = end - begin
        return pl.pallas_call(
            functools.partial(adam_kernel, begin),
            out_shape=[pltpu.HBM(split, f32)] * 3 + [pltpu.VMEM((8, C), f32)],
            in_specs=[VMEM] * 5 + [ANY] + [HBM] * len(before),
            out_specs=[HBM] * 3 + [VMEM],
            scratch_shapes=[
                pltpu.VMEM((3, steps, count, 2, C, C), f32),
                pltpu.SemaphoreType.DMA((steps, 3)),
            ],
            input_output_aliases={6 + k: k for k in range(len(before))},
            compiler_params=params(22),
            cost_estimate=cost(16 * weights.size * steps // total),
            name="adam",
        )(inputs, pairs, weights_held, first, second, after, *before)

    *updated, token = adam(0, first_steps, back)
    blocks = pl.pallas_call(
        back_x_kernel,
        out_shape=[pltpu.VMEM((cells, owners, height, C), half)] * QUAD,
        in_specs=[VMEM] * 3 + [ANY],
        out_specs=[VMEM] * QUAD,
        scratch_shapes=[
            pltpu.VMEM((halves,) + per_half, half),
            pltpu.VMEM((QUAD, cells, owners, height, C), half),
        ],
        compiler_params=params(8),
        name="back_x",
    )(back, back_come, back_table_x, token)
    *updated, token = adam(first_steps, total, blocks[1], *updated)
    blocks = exchange(blocks)
    field_grad = pl.pallas_call(
        back_yz_kernel,
        out_shape=jax.ShapeDtypeStruct((cells, NY * NZ, C), half),
        in_specs=[VMEM] * (QUAD + 1) + [ANY],
        out_specs=VMEM,
        scratch_shapes=[pltpu.VMEM((QUAD, cells, owners, height, C), half)],
        compiler_params=params(8),
        name="back_yz",
    )(*blocks, back_table_yz, token)
    return (field_grad.reshape(field.shape), *[values.reshape(weights.shape) for values in updated])


def trig_tables(length, modes_kept, signed):
    cosine, sine_part = np_tables(length, modes_kept, signed)
    return jnp.asarray(cosine, half), jnp.asarray(sine_part, half)


def forward_table(cosine, sine_part):
    real_row = jnp.stack([cosine, -sine_part], axis=-1)
    imag_row = jnp.stack([sine_part, cosine], axis=-1)
    return jnp.stack([real_row, imag_row], axis=1)


def inverse_table(cosine, sine_part):
    real_row = jnp.stack([cosine.T, sine_part.T], axis=-1)
    imag_row = jnp.stack([-sine_part.T, cosine.T], axis=-1)
    return jnp.stack([real_row, imag_row], axis=1)


def adam_update(weights, first_moment, second_moment, weight_grads):
    new_first = decay_first * first_moment + (1.0 - decay_first) * weight_grads
    new_second = decay_second * second_moment + (1.0 - decay_second) * weight_grads * weight_grads
    first_hat = new_first / (1.0 - decay_first**STEP)
    second_hat = new_second / (1.0 - decay_second**STEP)
    new_weights = weights - learn_rate * first_hat / (jnp.sqrt(second_hat) + adam_floor)
    return (new_weights, new_first, new_second)


def general(field, cotangent, weights, first_moment, second_moment):
    slab_count = lax.axis_size("space")
    batch_local = field.shape[0]
    cells_x = field.shape[1]
    total_x = cells_x * slab_count
    cos_z, sin_z = trig_tables(NZ, MZ, False)
    cos_y, sin_y = trig_tables(NY, MY, True)
    cos_x, sin_x = trig_tables(total_x, MX, True)
    table_z = jnp.stack([cos_z, -sin_z], axis=1)
    table_y = forward_table(cos_y, sin_y)
    table_x = forward_table(cos_x, sin_x)
    back_table_x = inverse_table(cos_x, sin_x)
    back_table_y = inverse_table(cos_y, sin_y)
    back_table_z = jnp.stack([cos_z.T, -sin_z.T], axis=0)
    product = functools.partial(jnp.einsum, preferred_element_type=f32)

    def swap(values, axis, split, concat):
        return lax.all_to_all(values, axis, split_axis=split, concat_axis=concat, tiled=True)

    def to_modes(slab_field):
        first_pass = product("bxyzc,zpk->bxypkc", slab_field, table_z).astype(half)
        second = product("bxypkc,ypmq->bxmkqc", first_pass, table_y).astype(half)
        second = second.reshape(batch_local, cells_x, MYZ, 2, C)
        along = product("bxpjc,xjmq->bmpqc", swap(second, "space", 2, 1), table_x).astype(half)
        return swap(swap(along, "space", 1, 2), "dp", 2, 0)

    field_hat = to_modes(field)
    cot_hat = to_modes(cotangent)
    rotated = jnp.stack([cot_hat[:, :, :, 1], -cot_hat[:, :, :, 0]], axis=3)
    form_in = "bmpjc,bmpjo->mpco"
    weight_grads = jnp.stack([product(form_in, field_hat, cot_hat), product(form_in, field_hat, rotated)], axis=2)
    half_weights = weights.astype(half)
    form_back = "mpjio,bmpjo->bmpi"
    mode_grads = jnp.stack(
        [product(form_back, half_weights, cot_hat), product(form_back, half_weights, rotated)], axis=3
    ).astype(half)
    updated = adam_update(weights, first_moment, second_moment, weight_grads)
    pencils = swap(swap(mode_grads, "dp", 0, 2), "space", 2, 1)
    back_x = product("bmpjc,mjxq->bxpqc", pencils, back_table_x).astype(half)
    unpacked = swap(back_x, "space", 1, 2).reshape(batch_local, cells_x, MY, MZ, 2, C)
    back_y = product("bxmkjc,mjyq->bxyqkc", unpacked, back_table_y).astype(half)
    field_grad = product("bxyqkc,qkz->bxyzc", back_y, back_table_z).astype(half)
    return (field_grad, *updated)


def solution(mesh):
    owners, spaces = mesh.shape["dp"], mesh.shape["space"]
    pencils = MYZ // (owners * QUAD)
    if spaces == 2 * QUAD and MX == 2 * spaces and MYZ % (owners * QUAD * 8) == 0 and pencils * owners % 2 == 0:
        mesh = jax.sharding.Mesh(mesh.devices.reshape(owners, 2, QUAD), ("dp", "half", "quad"))
        space, on_device = ("half", "quad"), fast
    else:
        space, on_device = "space", general
    grid = P("dp", space, None, None, None)
    held = P(space, "dp", None, None, None)
    return jax.shard_map(
        on_device,
        mesh=mesh,
        in_specs=(grid, grid, held, held, held),
        out_specs=(grid, held, held, held),
        check_vma=False,
    )
```

```python
import functools
import math

import jax
import jax.numpy as jnp
import ml_dtypes
import numpy as np
from jax import lax
from jax.experimental import pallas as pl
from jax.experimental.pallas import tpu as pltpu
from jax.sharding import PartitionSpec as P

C = 128
MX = 16
MY = 16
MZ = 8
NY = 32
NZ = 16
STEP = 100
MYZ = 128
QUAD = 4


decay_first = 0.9
decay_second = 0.999
learn_rate = 0.001
adam_floor = 1e-08

f32 = jnp.float32
half = jnp.bfloat16


def np_tables(length, modes_kept, signed):
    points = np.arange(length)
    frequency = np.arange(modes_kept) - (modes_kept // 2 if signed else 0)
    angles = np.mod(points[:, None] * frequency[None, :], length) * (2.0 * math.pi / length)
    factor = np.float32(1.0 / math.sqrt(length))
    cosine = (np.cos(angles).astype(np.float32) * factor).astype(ml_dtypes.bfloat16)
    sine = (np.sin(angles).astype(np.float32) * factor).astype(ml_dtypes.bfloat16)
    return cosine.astype(np.float64), sine.astype(np.float64)


def yz_table(dp_count):
    cos_z, sin_z = np_tables(NZ, MZ, False)
    cos_y, sin_y = np_tables(NY, MY, True)
    cy, sy = cos_y.T[:, None, :, None], sin_y.T[:, None, :, None]
    cz, sz = cos_z.T[None, :, None, :], sin_z.T[None, :, None, :]
    real = cy * cz - sy * sz
    imag = -(sy * cz + cy * sz)
    table = np.stack([real, imag], axis=2).reshape(MYZ, 2, NY * NZ)
    pencils = MYZ // dp_count // QUAD
    table = table.reshape(dp_count, QUAD, pencils, 2, NY * NZ).transpose(1, 0, 2, 3, 4)
    return table.reshape(QUAD, dp_count * pencils * 2, NY * NZ).astype(ml_dtypes.bfloat16)


def x_tables(total_x, halves, pencils):
    cos_x, sin_x = np_tables(total_x, MX, True)
    same = np.eye(pencils)
    span = total_x // halves
    forward, backward = [], []
    for part in range(halves):
        c, s = cos_x[part * span : (part + 1) * span], sin_x[part * span : (part + 1) * span]
        fwd = np.zeros((MX, pencils, 2, span, pencils, 2))
        fwd[:, :, 0, :, :, 0] = np.einsum("xm,pr->mpxr", c, same)
        fwd[:, :, 0, :, :, 1] = np.einsum("xm,pr->mpxr", s, same)
        fwd[:, :, 1, :, :, 0] = np.einsum("xm,pr->mpxr", -s, same)
        fwd[:, :, 1, :, :, 1] = np.einsum("xm,pr->mpxr", c, same)
        bwd = np.zeros((span, pencils, 2, MX, pencils, 2))
        bwd[:, :, 0, :, :, 0] = np.einsum("xm,pr->xpmr", c, same)
        bwd[:, :, 0, :, :, 1] = np.einsum("xm,pr->xpmr", -s, same)
        bwd[:, :, 1, :, :, 0] = np.einsum("xm,pr->xpmr", s, same)
        bwd[:, :, 1, :, :, 1] = np.einsum("xm,pr->xpmr", c, same)
        forward.append(fwd.reshape(MX * pencils * 2, span * pencils * 2))
        backward.append(bwd.reshape(span * pencils * 2, MX * pencils * 2))
    return np.stack(forward).astype(ml_dtypes.bfloat16), np.stack(backward).astype(ml_dtypes.bfloat16)


def gather_tables(batch, halves, modes, pencils):
    plain = np.zeros((modes, pencils, batch, 2, batch, halves, modes, pencils, 2))
    turned = np.zeros_like(plain)
    for m in range(modes):
        for p in range(pencils):
            for b in range(batch):
                plain[m, p, b, 0, b, :, m, p, 0] = 1.0
                plain[m, p, b, 1, b, :, m, p, 1] = 1.0
                turned[m, p, b, 0, b, :, m, p, 1] = 1.0
                turned[m, p, b, 1, b, :, m, p, 0] = -1.0
    rows = modes * pencils * batch * 2
    both = np.concatenate([plain.reshape(rows, -1), turned.reshape(rows, -1)])
    return both.astype(ml_dtypes.bfloat16)


def scatter_table(batch, modes, pencils):
    order = np.arange(modes * pencils * batch * 2).reshape(modes * pencils, batch, 2).transpose(1, 0, 2).reshape(-1)
    return np.eye(order.size)[order].astype(ml_dtypes.bfloat16)


def dot(a, b, dims=((1,), (0,))):
    return lax.dot_general(a, b, (dims, ((), ())), preferred_element_type=f32)


def yz_kernel(field, cotangent, table, *refs):
    blocks, (mixed, cells_in, sems) = refs[:QUAD], refs[QUAD:]
    rows = table.shape[1]
    cells = field.shape[0]
    loads = [
        pltpu.make_async_copy(table.at[lax.axis_index("quad") ^ r], mixed.at[pl.ds(r * rows, rows)], sems.at[r]) for r in range(QUAD)
    ]
    for which, source in enumerate((field, cotangent)):
        loads.append(pltpu.make_async_copy(source, cells_in.at[which], sems.at[len(loads)]))
    for load in loads:
        load.start()
    for load in loads:
        load.wait()
    for which in range(2):
        for x in range(0, cells, 2):
            pair = jnp.concatenate([cells_in[which, x], cells_in[which, x + 1]], axis=1)
            result = dot(mixed[...], pair).astype(half)
            for r in range(QUAD):
                piece = result[r * rows : (r + 1) * rows]
                blocks[r][which, x] = piece[:, :C]
                blocks[r][which, x + 1] = piece[:, C:]


def x_kernel(*refs):
    pieces, (table, out, held) = refs[:QUAD], refs[QUAD:]
    for r in range(QUAD):
        held[lax.axis_index("quad") ^ r] = pieces[r][...]
    matrix = table[lax.axis_index("half")]
    fields, cells, rows = held.shape[1:4]
    height = matrix.shape[1] // QUAD // cells
    spaces = out.shape[0] // (rows // height)
    for d in range(rows // height):
        columns = [
            jnp.concatenate(
                [held[q, f, x, d * height : (d + 1) * height, :] for q in range(QUAD) for x in range(cells)], axis=0
            )
            for f in range(fields)
        ]
        result = dot(matrix, jnp.concatenate(columns, axis=1)).astype(half)
        for f in range(fields):
            out[d * spaces : (d + 1) * spaces, f] = result[:, f * C : (f + 1) * C].reshape(spaces, -1, C)


def stage_kernel(after, weights, *refs):
    count = (len(refs) - 3) // 2
    sources, weights_held, held = refs[:count], refs[count], refs[count + 1 : 2 * count + 1]
    rounded, sems = refs[2 * count + 1 :]
    del after
    modes, pencils = weights.shape[:2]
    each = pencils // 4
    spans = [(m, p) for m in range(modes) for p in range(0, pencils, each)]
    loads = []

    def add(source, target):
        loads.append(pltpu.make_async_copy(source, target, sems.at[len(loads)]))

    for m, p in spans:
        add(weights.at[m, p : p + each], weights_held.at[m, p : p + each])
    for source, target in zip(sources, held):
        if len(source.shape) < 5:
            add(source, target)
        else:
            for m, p in spans:
                add(source.at[m, p : p + each], target.at[m, p : p + each])
    for load in loads:
        load.start()
    for k, (m, p) in enumerate(spans):
        loads[k].wait()

        def body(i, carry):
            for part in range(2):
                rounded[m, p + i, :, part * C : (part + 1) * C] = weights_held[m, p + i, part].astype(half)
            return carry

        lax.fori_loop(0, each, body, 0)
    for load in loads[len(spans) :]:
        load.wait()


def modes_kernel(arrived, weights, gather, scatter, sent, inputs, pairs):
    batch, halves, quad, _, rows, _ = arrived.shape
    modes, pencils = weights.shape[0], weights.shape[1] // quad
    height = batch * 2
    columns_out = []
    all_pairs = []
    for q in range(quad):
        field = arrived[:, :, q, 0].reshape(-1, C)
        cot = arrived[:, :, q, 1].reshape(-1, C)
        both = dot(gather[...], jnp.concatenate([field, cot], axis=1)).astype(half)
        count = both.shape[0] // 2
        inputs[q] = both[:count, :C]
        pair = jnp.concatenate([both[:count, C:], both[count:, C:]], axis=1)
        pairs[q] = pair
        all_pairs.append(pair)
    for q in range(quad):
        pair = all_pairs[q]
        results = []
        for m in range(modes):
            for p in range(0, pencils, 2):
                at = (m * pencils + p) * height
                first = q * pencils + p
                columns = weights[m, first : first + 2].reshape(2 * C, 2 * C)
                result = dot(pair[at : at + 2 * height], columns, ((1,), (1,)))
                results += [result[:height, :C], result[height:, C:]]
        columns_out.append(jnp.concatenate(results, axis=0).astype(half))
    spread = dot(scatter[...], jnp.concatenate(columns_out, axis=1)).astype(half)
    for q in range(quad):
        sent[:, q] = spread[:, q * C : (q + 1) * C].reshape(batch, rows, C)


def adam_kernel(begin, inputs, pairs, weights, first, second, *refs):
    new_weights, new_first, new_second, token, held, sems = refs[-6:]
    new = (new_weights, new_first, new_second)
    modes, pencils = weights.shape[:2]
    steps, count = held.shape[1:3]
    height = inputs.shape[1] // (modes * (pencils // QUAD))
    per_mode = pencils // count
    per_quad = per_mode // QUAD
    scale_first = learn_rate / (1.0 - decay_first**STEP)
    scale_second = 1.0 / (1.0 - decay_second**STEP)

    def copies(i):
        mode, at = (i + begin) // per_mode, (i + begin) % per_mode
        return [
            pltpu.make_async_copy(held.at[o, i], new[o].at[mode, pl.ds(at * count, count)], sems.at[i, o])
            for o in range(3)
        ]

    def body(i, carry):
        mode, at = (i + begin) // per_mode, (i + begin) % per_mode
        rows = count * height
        row = pl.multiple_of((mode * per_quad + at % per_quad) * rows, rows)
        us = inputs[at // per_quad, pl.ds(row, rows), :]
        gs = pairs[at // per_quad, pl.ds(row, rows), :]
        for k in range(count):
            u = us[k * height : (k + 1) * height]
            g = gs[k * height : (k + 1) * height]
            grads = dot(u, g, ((0,), (0,)))
            p = at * count + k
            for part in range(2):
                grad = grads[:, part * C : (part + 1) * C]
                m = decay_first * first[mode, p, part] + (1.0 - decay_first) * grad
                v = decay_second * second[mode, p, part] + ((1.0 - decay_second) * grad) * grad
                held[1, i, k, part] = m
                held[2, i, k, part] = v
                level = v * scale_second
                inverse = lax.rsqrt(level)
                floored = level * inverse + adam_floor
                inverse = inverse * (2.0 - floored * inverse)
                held[0, i, k, part] = weights[mode, p, part] - (scale_first * m) * inverse
        for copy in copies(i):
            copy.start()
        return carry

    def finish(i, carry):
        for copy in copies(i):
            copy.wait()
        return carry

    lax.fori_loop(0, steps, body, 0)
    lax.fori_loop(0, steps, finish, 0)
    token[...] = jnp.zeros_like(token)


def back_x_kernel(own, come, table, after, *refs):
    blocks, (arrived, held) = refs[:QUAD], refs[QUAD:]
    arrived[lax.axis_index("half")] = own[...]
    arrived[1 - lax.axis_index("half")] = come[...]
    matrix = table[lax.axis_index("half")]
    cells, owners, height, _ = blocks[0].shape
    halves = arrived.shape[0]
    span = cells * height
    for d in range(0, owners, 2):
        columns = [
            jnp.concatenate([arrived[h, k * QUAD : (k + 1) * QUAD].reshape(-1, C) for h in range(halves)], axis=0)
            for k in (d, d + 1)
        ]
        result = dot(matrix, jnp.concatenate(columns, axis=1)).astype(half)
        for q in range(QUAD):
            piece = result[q * span : (q + 1) * span].reshape(cells, height, 2 * C)
            held[q, :, d] = piece[:, :, :C]
            held[q, :, d + 1] = piece[:, :, C:]
    for r in range(QUAD):
        blocks[r][...] = held[lax.axis_index("quad") ^ r]


def back_yz_kernel(*refs):
    pieces, (table, after, out, held) = refs[:QUAD], refs[QUAD:]
    for r in range(QUAD):
        held[lax.axis_index("quad") ^ r] = pieces[r][...]
    matrix = table[...]
    for x in range(0, out.shape[0], 2):
        columns = jnp.concatenate([held[:, k].reshape(-1, C) for k in (x, x + 1)], axis=1)
        result = dot(matrix, columns).astype(half)
        out[x] = result[:, :C]
        out[x + 1] = result[:, C:]


VMEM = pl.BlockSpec(memory_space=pltpu.VMEM)
HBM = pl.BlockSpec(memory_space=pltpu.HBM)
ANY = pl.BlockSpec(memory_space=pl.ANY)
MIB = 1 << 20


def params(mib, **more):
    return pltpu.CompilerParams(vmem_limit_bytes=mib * MIB, **more)


def cost(size):
    return pl.CostEstimate(flops=0, bytes_accessed=size, transcendentals=0)


def in_hbm(values):
    return pltpu.with_memory_space_constraint(values, pltpu.HBM)


def exchange(blocks):
    moved = [lax.ppermute(blocks[r], "quad", [(q, q ^ r) for q in range(QUAD)]) for r in range(1, QUAD)]
    return [blocks[0]] + moved


def swap_halves(values):
    return lax.ppermute(values, "half", [(0, 1), (1, 0)])


def fast(field, cotangent, weights, first_moment, second_moment):
    halves = lax.axis_size("half")
    spaces = halves * QUAD
    owners = lax.axis_size("dp")
    cells = field.shape[1]
    total_x = cells * spaces
    pencils = MYZ // owners // QUAD
    modes = MX // spaces
    height = pencils * 2
    table_yz = yz_table(owners)
    table_x, back_table_x = x_tables(total_x, halves, pencils)
    back_table_yz = np.ascontiguousarray(table_yz.reshape(MYZ * 2, NY * NZ).T)
    gather = gather_tables(owners, halves, modes, pencils)
    scatter = scatter_table(owners, modes, pencils)
    vmem = lambda values: pltpu.VMEM(values.shape, values.dtype)

    flat = (cells, NY * NZ, C)
    blocks = pl.pallas_call(
        yz_kernel,
        out_shape=[pltpu.VMEM((2, cells, owners * height, C), half)] * QUAD,
        in_specs=[HBM] * 3,
        out_specs=[VMEM] * QUAD,
        scratch_shapes=[
            pltpu.VMEM((MYZ * 2, NY * NZ), half),
            pltpu.VMEM((2,) + flat, half),
            pltpu.SemaphoreType.DMA((QUAD + 2,)),
        ],
        compiler_params=params(8),
        name="yz_modes",
    )(in_hbm(field.reshape(flat)), in_hbm(cotangent.reshape(flat)), in_hbm(jnp.asarray(table_yz)))

    split = (modes, QUAD * pencils, 2, C, C)
    big, first, second = weights.reshape(split), first_moment.reshape(split), second_moment.reshape(split)
    staged = [jnp.asarray(t) for t in (table_x, gather, scatter, back_table_x, back_table_yz)]
    weights_held, table_x, gather, scatter, back_table_x, back_table_yz, rounded = pl.pallas_call(
        stage_kernel,
        out_shape=[vmem(big)] + [vmem(t) for t in staged] + [pltpu.VMEM((modes, QUAD * pencils, C, 2 * C), half)],
        in_specs=[ANY] + [HBM] * (1 + len(staged)),
        out_specs=[VMEM] * (2 + len(staged)),
        scratch_shapes=[pltpu.SemaphoreType.DMA((4 * modes + len(staged),))],
        compiler_params=params(8),
        cost_estimate=cost(0),
        name="stage",
    )(blocks[0], in_hbm(big), *[in_hbm(t) for t in staged])
    blocks = exchange(blocks)

    rows = modes * height
    per_half = (owners * QUAD, rows, C)
    partial = pl.pallas_call(
        x_kernel,
        out_shape=pltpu.VMEM((owners * spaces, 2, rows, C), half),
        in_specs=[VMEM] * (QUAD + 1),
        out_specs=VMEM,
        scratch_shapes=[pltpu.VMEM((QUAD, 2, cells, owners * height, C), half)],
        compiler_params=params(8),
        name="x_modes",
    )(*blocks, table_x)
    arrived = lax.all_to_all(partial, ("dp", "half", "quad"), 0, 0, tiled=True)

    mode_rows = rows * owners
    sent, inputs, pairs = pl.pallas_call(
        modes_kernel,
        out_shape=[
            pltpu.VMEM((owners, QUAD, rows, C), half),
            pltpu.VMEM((QUAD, mode_rows, C), half),
            pltpu.VMEM((QUAD, mode_rows, 2 * C), half),
        ],
        in_specs=[VMEM] * 4,
        out_specs=[VMEM] * 3,
        compiler_params=params(8),
        name="mode_grads",
    )(arrived.reshape(owners, halves, QUAD, 2, rows, C), rounded, gather, scatter)
    back = lax.all_to_all(sent.reshape(per_half), ("dp", "quad"), 0, 0, tiled=True)
    back_come = swap_halves(back)

    count = 4
    total = modes * QUAD * pencils // count
    first_steps = total * 12 // 16

    def adam(begin, end, after, *before):
        steps = end - begin
        return pl.pallas_call(
            functools.partial(adam_kernel, begin),
            out_shape=[pltpu.HBM(split, f32)] * 3 + [pltpu.VMEM((8, C), f32)],
            in_specs=[VMEM] * 5 + [ANY] + [HBM] * len(before),
            out_specs=[HBM] * 3 + [VMEM],
            scratch_shapes=[
                pltpu.VMEM((3, steps, count, 2, C, C), f32),
                pltpu.SemaphoreType.DMA((steps, 3)),
            ],
            input_output_aliases={6 + k: k for k in range(len(before))},
            compiler_params=params(22),
            cost_estimate=cost(16 * weights.size * steps // total),
            name="adam",
        )(inputs, pairs, weights_held, first, second, after, *before)

    *updated, token = adam(0, first_steps, back)
    blocks = pl.pallas_call(
        back_x_kernel,
        out_shape=[pltpu.VMEM((cells, owners, height, C), half)] * QUAD,
        in_specs=[VMEM] * 3 + [ANY],
        out_specs=[VMEM] * QUAD,
        scratch_shapes=[
            pltpu.VMEM((halves,) + per_half, half),
            pltpu.VMEM((QUAD, cells, owners, height, C), half),
        ],
        compiler_params=params(8),
        name="back_x",
    )(back, back_come, back_table_x, token)
    *updated, token = adam(first_steps, total, blocks[1], *updated)
    blocks = exchange(blocks)
    field_grad = pl.pallas_call(
        back_yz_kernel,
        out_shape=jax.ShapeDtypeStruct((cells, NY * NZ, C), half),
        in_specs=[VMEM] * (QUAD + 1) + [ANY],
        out_specs=VMEM,
        scratch_shapes=[pltpu.VMEM((QUAD, cells, owners, height, C), half)],
        compiler_params=params(8),
        name="back_yz",
    )(*blocks, back_table_yz, token)
    return (field_grad.reshape(field.shape), *[values.reshape(weights.shape) for values in updated])


def trig_tables(length, modes_kept, signed):
    cosine, sine_part = np_tables(length, modes_kept, signed)
    return jnp.asarray(cosine, half), jnp.asarray(sine_part, half)


def forward_table(cosine, sine_part):
    real_row = jnp.stack([cosine, -sine_part], axis=-1)
    imag_row = jnp.stack([sine_part, cosine], axis=-1)
    return jnp.stack([real_row, imag_row], axis=1)


def inverse_table(cosine, sine_part):
    real_row = jnp.stack([cosine.T, sine_part.T], axis=-1)
    imag_row = jnp.stack([-sine_part.T, cosine.T], axis=-1)
    return jnp.stack([real_row, imag_row], axis=1)


def adam_update(weights, first_moment, second_moment, weight_grads):
    new_first = decay_first * first_moment + (1.0 - decay_first) * weight_grads
    new_second = decay_second * second_moment + (1.0 - decay_second) * weight_grads * weight_grads
    first_hat = new_first / (1.0 - decay_first**STEP)
    second_hat = new_second / (1.0 - decay_second**STEP)
    new_weights = weights - learn_rate * first_hat / (jnp.sqrt(second_hat) + adam_floor)
    return (new_weights, new_first, new_second)


def general(field, cotangent, weights, first_moment, second_moment):
    slab_count = lax.axis_size("space")
    batch_local = field.shape[0]
    cells_x = field.shape[1]
    total_x = cells_x * slab_count
    cos_z, sin_z = trig_tables(NZ, MZ, False)
    cos_y, sin_y = trig_tables(NY, MY, True)
    cos_x, sin_x = trig_tables(total_x, MX, True)
    table_z = jnp.stack([cos_z, -sin_z], axis=1)
    table_y = forward_table(cos_y, sin_y)
    table_x = forward_table(cos_x, sin_x)
    back_table_x = inverse_table(cos_x, sin_x)
    back_table_y = inverse_table(cos_y, sin_y)
    back_table_z = jnp.stack([cos_z.T, -sin_z.T], axis=0)
    product = functools.partial(jnp.einsum, preferred_element_type=f32)

    def swap(values, axis, split, concat):
        return lax.all_to_all(values, axis, split_axis=split, concat_axis=concat, tiled=True)

    def to_modes(slab_field):
        first_pass = product("bxyzc,zpk->bxypkc", slab_field, table_z).astype(half)
        second = product("bxypkc,ypmq->bxmkqc", first_pass, table_y).astype(half)
        second = second.reshape(batch_local, cells_x, MYZ, 2, C)
        along = product("bxpjc,xjmq->bmpqc", swap(second, "space", 2, 1), table_x).astype(half)
        return swap(swap(along, "space", 1, 2), "dp", 2, 0)

    field_hat = to_modes(field)
    cot_hat = to_modes(cotangent)
    rotated = jnp.stack([cot_hat[:, :, :, 1], -cot_hat[:, :, :, 0]], axis=3)
    form_in = "bmpjc,bmpjo->mpco"
    weight_grads = jnp.stack([product(form_in, field_hat, cot_hat), product(form_in, field_hat, rotated)], axis=2)
    half_weights = weights.astype(half)
    form_back = "mpjio,bmpjo->bmpi"
    mode_grads = jnp.stack(
        [product(form_back, half_weights, cot_hat), product(form_back, half_weights, rotated)], axis=3
    ).astype(half)
    updated = adam_update(weights, first_moment, second_moment, weight_grads)
    pencils = swap(swap(mode_grads, "dp", 0, 2), "space", 2, 1)
    back_x = product("bmpjc,mjxq->bxpqc", pencils, back_table_x).astype(half)
    unpacked = swap(back_x, "space", 1, 2).reshape(batch_local, cells_x, MY, MZ, 2, C)
    back_y = product("bxmkjc,mjyq->bxyqkc", unpacked, back_table_y).astype(half)
    field_grad = product("bxyqkc,qkz->bxyzc", back_y, back_table_z).astype(half)
    return (field_grad, *updated)


def solution(mesh):
    owners, spaces = mesh.shape["dp"], mesh.shape["space"]
    pencils = MYZ // (owners * QUAD)
    if spaces == 2 * QUAD and MX == 2 * spaces and MYZ % (owners * QUAD * 8) == 0 and pencils * owners % 2 == 0:
        mesh = jax.sharding.Mesh(mesh.devices.reshape(owners, 2, QUAD), ("dp", "half", "quad"))
        space, on_device = ("half", "quad"), fast
    else:
        space, on_device = "space", general
    grid = P("dp", space, None, None, None)
    held = P(space, "dp", None, None, None)
    return jax.shard_map(
        on_device,
        mesh=mesh,
        in_specs=(grid, grid, held, held, held),
        out_specs=(grid, held, held, held),
        check_vma=False,
    )
```

```python
import functools
import math

import jax
import jax.numpy as jnp
import ml_dtypes
import numpy as np
from jax import lax
from jax.experimental import pallas as pl
from jax.experimental.pallas import tpu as pltpu
from jax.sharding import PartitionSpec as P

C = 128
MX = 16
MY = 16
MZ = 8
NY = 32
NZ = 16
STEP = 100
MYZ = 128
QUAD = 4
PARTNERS = (0, 3, 1, 2)


decay_first = 0.9
decay_second = 0.999
learn_rate = 0.001
adam_floor = 1e-08

f32 = jnp.float32
half = jnp.bfloat16


def np_tables(length, modes_kept, signed):
    points = np.arange(length)
    frequency = np.arange(modes_kept) - (modes_kept // 2 if signed else 0)
    angles = np.mod(points[:, None] * frequency[None, :], length) * (2.0 * math.pi / length)
    factor = np.float32(1.0 / math.sqrt(length))
    cosine = (np.cos(angles).astype(np.float32) * factor).astype(ml_dtypes.bfloat16)
    sine = (np.sin(angles).astype(np.float32) * factor).astype(ml_dtypes.bfloat16)
    return cosine.astype(np.float64), sine.astype(np.float64)


def yz_table(dp_count):
    cos_z, sin_z = np_tables(NZ, MZ, False)
    cos_y, sin_y = np_tables(NY, MY, True)
    cy, sy = cos_y.T[:, None, :, None], sin_y.T[:, None, :, None]
    cz, sz = cos_z.T[None, :, None, :], sin_z.T[None, :, None, :]
    real = cy * cz - sy * sz
    imag = -(sy * cz + cy * sz)
    table = np.stack([real, imag], axis=2).reshape(MYZ, 2, NY * NZ)
    pencils = MYZ // dp_count // QUAD
    table = table.reshape(dp_count, QUAD, pencils, 2, NY * NZ).transpose(1, 0, 2, 3, 4)
    return table.reshape(QUAD, dp_count * pencils * 2, NY * NZ).astype(ml_dtypes.bfloat16)


def x_tables(total_x, halves, pencils):
    cos_x, sin_x = np_tables(total_x, MX, True)
    same = np.eye(pencils)
    span = total_x // halves
    forward, backward = [], []
    for part in range(halves):
        c, s = cos_x[part * span : (part + 1) * span], sin_x[part * span : (part + 1) * span]
        fwd = np.zeros((MX, pencils, 2, span, pencils, 2))
        fwd[:, :, 0, :, :, 0] = np.einsum("xm,pr->mpxr", c, same)
        fwd[:, :, 0, :, :, 1] = np.einsum("xm,pr->mpxr", s, same)
        fwd[:, :, 1, :, :, 0] = np.einsum("xm,pr->mpxr", -s, same)
        fwd[:, :, 1, :, :, 1] = np.einsum("xm,pr->mpxr", c, same)
        bwd = np.zeros((span, pencils, 2, MX, pencils, 2))
        bwd[:, :, 0, :, :, 0] = np.einsum("xm,pr->xpmr", c, same)
        bwd[:, :, 0, :, :, 1] = np.einsum("xm,pr->xpmr", -s, same)
        bwd[:, :, 1, :, :, 0] = np.einsum("xm,pr->xpmr", s, same)
        bwd[:, :, 1, :, :, 1] = np.einsum("xm,pr->xpmr", c, same)
        forward.append(fwd.reshape(MX * pencils * 2, span * pencils * 2))
        backward.append(bwd.reshape(span * pencils * 2, MX * pencils * 2))
    return np.stack(forward).astype(ml_dtypes.bfloat16), np.stack(backward).astype(ml_dtypes.bfloat16)


def gather_tables(batch, halves, modes, pencils):
    plain = np.zeros((modes, pencils, batch, 2, batch, halves, modes, pencils, 2))
    turned = np.zeros_like(plain)
    for m in range(modes):
        for p in range(pencils):
            for b in range(batch):
                plain[m, p, b, 0, b, :, m, p, 0] = 1.0
                plain[m, p, b, 1, b, :, m, p, 1] = 1.0
                turned[m, p, b, 0, b, :, m, p, 1] = 1.0
                turned[m, p, b, 1, b, :, m, p, 0] = -1.0
    rows = modes * pencils * batch * 2
    both = np.concatenate([plain.reshape(rows, -1), turned.reshape(rows, -1)])
    return both.astype(ml_dtypes.bfloat16)


def scatter_table(batch, modes, pencils):
    order = np.arange(modes * pencils * batch * 2).reshape(modes * pencils, batch, 2).transpose(1, 0, 2).reshape(-1)
    return np.eye(order.size)[order].astype(ml_dtypes.bfloat16)


def dot(a, b, dims=((1,), (0,))):
    return lax.dot_general(a, b, (dims, ((), ())), preferred_element_type=f32)


def yz_kernel(field, cotangent, table, *refs):
    blocks, (table_in, cells_in, sems) = refs[:QUAD], refs[QUAD:]
    rows = table.shape[1]
    cells = field.shape[0]
    loads = [
        pltpu.make_async_copy(table, table_in, sems.at[0]),
        pltpu.make_async_copy(field, cells_in.at[0], sems.at[1]),
        pltpu.make_async_copy(cotangent, cells_in.at[1], sems.at[2]),
    ]
    for load in loads:
        load.start()
    for load in loads:
        load.wait()
    matrix = jnp.concatenate([table_in[lax.axis_index("quad") ^ r] for r in range(QUAD)], axis=0)
    for which in range(2):
        for x in range(0, cells, 2):
            pair = jnp.concatenate([cells_in[which, x], cells_in[which, x + 1]], axis=1)
            result = dot(matrix, pair).astype(half)
            for r in range(QUAD):
                piece = result[r * rows : (r + 1) * rows]
                blocks[r][which, x] = piece[:, :C]
                blocks[r][which, x + 1] = piece[:, C:]


def x_kernel(*refs):
    pieces, (table, out, held) = refs[:QUAD], refs[QUAD:]
    for r, piece in zip(PARTNERS, pieces):
        held[lax.axis_index("quad") ^ r] = piece[...]
    matrix = table[lax.axis_index("half")]
    fields, cells, rows = held.shape[1:4]
    height = matrix.shape[1] // QUAD // cells
    spaces = out.shape[0] // (rows // height)
    for d in range(rows // height):
        columns = [
            jnp.concatenate(
                [held[q, f, x, d * height : (d + 1) * height, :] for q in range(QUAD) for x in range(cells)], axis=0
            )
            for f in range(fields)
        ]
        result = dot(matrix, jnp.concatenate(columns, axis=1)).astype(half)
        for f in range(fields):
            out[d * spaces : (d + 1) * spaces, f] = result[:, f * C : (f + 1) * C].reshape(spaces, -1, C)


def stage_kernel(after, weights, *refs):
    count = (len(refs) - 3) // 2
    sources, weights_held, held = refs[:count], refs[count], refs[count + 1 : 2 * count + 1]
    rounded, sems = refs[2 * count + 1 :]
    del after
    modes, pencils = weights.shape[:2]
    each = pencils // 4
    spans = [(m, p) for m in range(modes) for p in range(0, pencils, each)]
    loads = []

    def add(source, target):
        loads.append(pltpu.make_async_copy(source, target, sems.at[len(loads)]))

    for m, p in spans:
        add(weights.at[m, p : p + each], weights_held.at[m, p : p + each])
    for source, target in zip(sources, held):
        if len(source.shape) < 5:
            add(source, target)
        else:
            for m, p in spans:
                add(source.at[m, p : p + each], target.at[m, p : p + each])
    for load in loads:
        load.start()
    for k, (m, p) in enumerate(spans):
        loads[k].wait()

        def body(i, carry):
            for part in range(2):
                rounded[m, p + i, :, part * C : (part + 1) * C] = weights_held[m, p + i, part].astype(half)
            return carry

        lax.fori_loop(0, each, body, 0)
    for load in loads[len(spans) :]:
        load.wait()


def modes_kernel(arrived, weights, gather, scatter, sent, inputs, pairs):
    batch, halves, quad, _, rows, _ = arrived.shape
    modes, pencils = weights.shape[0], weights.shape[1] // quad
    height = batch * 2
    columns_out = []
    all_pairs = []
    for q in range(quad):
        field = arrived[:, :, q, 0].reshape(-1, C)
        cot = arrived[:, :, q, 1].reshape(-1, C)
        both = dot(gather[...], jnp.concatenate([field, cot], axis=1)).astype(half)
        count = both.shape[0] // 2
        inputs[q] = both[:count, :C]
        pair = jnp.concatenate([both[:count, C:], both[count:, C:]], axis=1)
        pairs[q] = pair
        all_pairs.append(pair)
    for q in range(quad):
        pair = all_pairs[q]
        results = []
        for m in range(modes):
            for p in range(0, pencils, 2):
                at = (m * pencils + p) * height
                first = q * pencils + p
                columns = weights[m, first : first + 2].reshape(2 * C, 2 * C)
                result = dot(pair[at : at + 2 * height], columns, ((1,), (1,)))
                results += [result[:height, :C], result[height:, C:]]
        columns_out.append(jnp.concatenate(results, axis=0).astype(half))
    spread = dot(scatter[...], jnp.concatenate(columns_out, axis=1)).astype(half)
    for q in range(quad):
        sent[:, q] = spread[:, q * C : (q + 1) * C].reshape(batch, rows, C)


def adam_kernel(begin, inputs, pairs, weights, first, second, *refs):
    new_weights, new_first, new_second, token, held, sems = refs[-6:]
    new = (new_weights, new_first, new_second)
    modes, pencils = weights.shape[:2]
    steps, count = held.shape[1:3]
    height = inputs.shape[1] // (modes * (pencils // QUAD))
    per_mode = pencils // count
    per_quad = per_mode // QUAD
    scale_first = learn_rate / (1.0 - decay_first**STEP)
    scale_second = 1.0 / (1.0 - decay_second**STEP)

    def copies(i):
        mode, at = (i + begin) // per_mode, (i + begin) % per_mode
        return [
            pltpu.make_async_copy(held.at[o, i], new[o].at[mode, pl.ds(at * count, count)], sems.at[i, o])
            for o in range(3)
        ]

    def body(i, carry):
        mode, at = (i + begin) // per_mode, (i + begin) % per_mode
        rows = count * height
        row = pl.multiple_of((mode * per_quad + at % per_quad) * rows, rows)
        us = inputs[at // per_quad, pl.ds(row, rows), :]
        gs = pairs[at // per_quad, pl.ds(row, rows), :]
        for k in range(count):
            u = us[k * height : (k + 1) * height]
            g = gs[k * height : (k + 1) * height]
            grads = dot(u, g, ((0,), (0,)))
            p = at * count + k
            for part in range(2):
                grad = grads[:, part * C : (part + 1) * C]
                m = decay_first * first[mode, p, part] + (1.0 - decay_first) * grad
                v = decay_second * second[mode, p, part] + ((1.0 - decay_second) * grad) * grad
                held[1, i, k, part] = m
                held[2, i, k, part] = v
                level = v * scale_second
                inverse = lax.rsqrt(level)
                floored = level * inverse + adam_floor
                inverse = inverse * (2.0 - floored * inverse)
                held[0, i, k, part] = weights[mode, p, part] - (scale_first * m) * inverse
        for copy in copies(i):
            copy.start()
        return carry

    def finish(i, carry):
        for copy in copies(i):
            copy.wait()
        return carry

    lax.fori_loop(0, steps, body, 0)
    lax.fori_loop(0, steps, finish, 0)
    token[...] = jnp.zeros_like(token)


def back_x_kernel(own, come, table, after, *refs):
    blocks, (arrived, held) = refs[:QUAD], refs[QUAD:]
    arrived[lax.axis_index("half")] = own[...]
    arrived[1 - lax.axis_index("half")] = come[...]
    matrix = table[lax.axis_index("half")]
    cells, owners, height, _ = blocks[0].shape
    halves = arrived.shape[0]
    span = cells * height
    for d in range(0, owners, 2):
        columns = [
            jnp.concatenate([arrived[h, k * QUAD : (k + 1) * QUAD].reshape(-1, C) for h in range(halves)], axis=0)
            for k in (d, d + 1)
        ]
        result = dot(matrix, jnp.concatenate(columns, axis=1)).astype(half)
        for q in range(QUAD):
            piece = result[q * span : (q + 1) * span].reshape(cells, height, 2 * C)
            held[q, :, d] = piece[:, :, :C]
            held[q, :, d + 1] = piece[:, :, C:]
    for r in range(QUAD):
        blocks[r][...] = held[lax.axis_index("quad") ^ r]


def back_yz_kernel(*refs):
    pieces, (table, after, out, held) = refs[:QUAD], refs[QUAD:]
    for r, piece in zip(PARTNERS, pieces):
        held[lax.axis_index("quad") ^ r] = piece[...]
    matrix = table[...]
    for x in range(0, out.shape[0], 2):
        columns = jnp.concatenate([held[:, k].reshape(-1, C) for k in (x, x + 1)], axis=1)
        result = dot(matrix, columns).astype(half)
        out[x] = result[:, :C]
        out[x + 1] = result[:, C:]


VMEM = pl.BlockSpec(memory_space=pltpu.VMEM)
HBM = pl.BlockSpec(memory_space=pltpu.HBM)
ANY = pl.BlockSpec(memory_space=pl.ANY)
MIB = 1 << 20


def params(mib, **more):
    return pltpu.CompilerParams(vmem_limit_bytes=mib * MIB, **more)


def cost(size):
    return pl.CostEstimate(flops=0, bytes_accessed=size, transcendentals=0)


def in_hbm(values):
    return pltpu.with_memory_space_constraint(values, pltpu.HBM)


def exchange(blocks):
    moved = [lax.ppermute(blocks[r], "quad", [(q, q ^ r) for q in range(QUAD)]) for r in PARTNERS[1:]]
    return [blocks[0]] + moved


def swap_halves(values):
    return lax.ppermute(values, "half", [(0, 1), (1, 0)])


def fast(field, cotangent, weights, first_moment, second_moment):
    halves = lax.axis_size("half")
    spaces = halves * QUAD
    owners = lax.axis_size("dp")
    cells = field.shape[1]
    total_x = cells * spaces
    pencils = MYZ // owners // QUAD
    modes = MX // spaces
    height = pencils * 2
    table_yz = yz_table(owners)
    table_x, back_table_x = x_tables(total_x, halves, pencils)
    back_table_yz = np.ascontiguousarray(table_yz.reshape(MYZ * 2, NY * NZ).T)
    gather = gather_tables(owners, halves, modes, pencils)
    scatter = scatter_table(owners, modes, pencils)
    vmem = lambda values: pltpu.VMEM(values.shape, values.dtype)

    flat = (cells, NY * NZ, C)
    blocks = pl.pallas_call(
        yz_kernel,
        out_shape=[pltpu.VMEM((2, cells, owners * height, C), half)] * QUAD,
        in_specs=[HBM] * 3,
        out_specs=[VMEM] * QUAD,
        scratch_shapes=[
            pltpu.VMEM(table_yz.shape, half),
            pltpu.VMEM((2,) + flat, half),
            pltpu.SemaphoreType.DMA((3,)),
        ],
        compiler_params=params(8),
        name="yz_modes",
    )(in_hbm(field.reshape(flat)), in_hbm(cotangent.reshape(flat)), in_hbm(jnp.asarray(table_yz)))

    split = (modes, QUAD * pencils, 2, C, C)
    big, first, second = weights.reshape(split), first_moment.reshape(split), second_moment.reshape(split)
    staged = [jnp.asarray(t) for t in (table_x, gather, scatter, back_table_x, back_table_yz)]
    weights_held, table_x, gather, scatter, back_table_x, back_table_yz, rounded = pl.pallas_call(
        stage_kernel,
        out_shape=[vmem(big)] + [vmem(t) for t in staged] + [pltpu.VMEM((modes, QUAD * pencils, C, 2 * C), half)],
        in_specs=[ANY] + [HBM] * (1 + len(staged)),
        out_specs=[VMEM] * (2 + len(staged)),
        scratch_shapes=[pltpu.SemaphoreType.DMA((4 * modes + len(staged),))],
        compiler_params=params(8),
        cost_estimate=cost(0),
        name="stage",
    )(blocks[0], in_hbm(big), *[in_hbm(t) for t in staged])
    blocks = exchange(blocks)

    rows = modes * height
    per_half = (owners * QUAD, rows, C)
    partial = pl.pallas_call(
        x_kernel,
        out_shape=pltpu.VMEM((owners * spaces, 2, rows, C), half),
        in_specs=[VMEM] * (QUAD + 1),
        out_specs=VMEM,
        scratch_shapes=[pltpu.VMEM((QUAD, 2, cells, owners * height, C), half)],
        compiler_params=params(8),
        name="x_modes",
    )(*blocks, table_x)
    arrived = lax.all_to_all(partial, ("dp", "half", "quad"), 0, 0, tiled=True)

    mode_rows = rows * owners
    sent, inputs, pairs = pl.pallas_call(
        modes_kernel,
        out_shape=[
            pltpu.VMEM((owners, QUAD, rows, C), half),
            pltpu.VMEM((QUAD, mode_rows, C), half),
            pltpu.VMEM((QUAD, mode_rows, 2 * C), half),
        ],
        in_specs=[VMEM] * 4,
        out_specs=[VMEM] * 3,
        compiler_params=params(8),
        name="mode_grads",
    )(arrived.reshape(owners, halves, QUAD, 2, rows, C), rounded, gather, scatter)
    back = lax.all_to_all(sent.reshape(per_half), ("dp", "quad"), 0, 0, tiled=True)
    back_come = swap_halves(back)

    count = 4
    total = modes * QUAD * pencils // count
    first_steps = total * 12 // 16

    def adam(begin, end, after, *before):
        steps = end - begin
        return pl.pallas_call(
            functools.partial(adam_kernel, begin),
            out_shape=[pltpu.HBM(split, f32)] * 3 + [pltpu.VMEM((8, C), f32)],
            in_specs=[VMEM] * 5 + [ANY] + [HBM] * len(before),
            out_specs=[HBM] * 3 + [VMEM],
            scratch_shapes=[
                pltpu.VMEM((3, steps, count, 2, C, C), f32),
                pltpu.SemaphoreType.DMA((steps, 3)),
            ],
            input_output_aliases={6 + k: k for k in range(len(before))},
            compiler_params=params(22),
            cost_estimate=cost(16 * weights.size * steps // total),
            name="adam",
        )(inputs, pairs, weights_held, first, second, after, *before)

    *updated, token = adam(0, first_steps, back)
    blocks = pl.pallas_call(
        back_x_kernel,
        out_shape=[pltpu.VMEM((cells, owners, height, C), half)] * QUAD,
        in_specs=[VMEM] * 3 + [ANY],
        out_specs=[VMEM] * QUAD,
        scratch_shapes=[
            pltpu.VMEM((halves,) + per_half, half),
            pltpu.VMEM((QUAD, cells, owners, height, C), half),
        ],
        compiler_params=params(8),
        name="back_x",
    )(back, back_come, back_table_x, token)
    *updated, token = adam(first_steps, total, blocks[1], *updated)
    blocks = exchange(blocks)
    field_grad = pl.pallas_call(
        back_yz_kernel,
        out_shape=jax.ShapeDtypeStruct((cells, NY * NZ, C), half),
        in_specs=[VMEM] * (QUAD + 1) + [ANY],
        out_specs=VMEM,
        scratch_shapes=[pltpu.VMEM((QUAD, cells, owners, height, C), half)],
        compiler_params=params(8),
        name="back_yz",
    )(*blocks, back_table_yz, token)
    return (field_grad.reshape(field.shape), *[values.reshape(weights.shape) for values in updated])


def trig_tables(length, modes_kept, signed):
    cosine, sine_part = np_tables(length, modes_kept, signed)
    return jnp.asarray(cosine, half), jnp.asarray(sine_part, half)


def forward_table(cosine, sine_part):
    real_row = jnp.stack([cosine, -sine_part], axis=-1)
    imag_row = jnp.stack([sine_part, cosine], axis=-1)
    return jnp.stack([real_row, imag_row], axis=1)


def inverse_table(cosine, sine_part):
    real_row = jnp.stack([cosine.T, sine_part.T], axis=-1)
    imag_row = jnp.stack([-sine_part.T, cosine.T], axis=-1)
    return jnp.stack([real_row, imag_row], axis=1)


def adam_update(weights, first_moment, second_moment, weight_grads):
    new_first = decay_first * first_moment + (1.0 - decay_first) * weight_grads
    new_second = decay_second * second_moment + (1.0 - decay_second) * weight_grads * weight_grads
    first_hat = new_first / (1.0 - decay_first**STEP)
    second_hat = new_second / (1.0 - decay_second**STEP)
    new_weights = weights - learn_rate * first_hat / (jnp.sqrt(second_hat) + adam_floor)
    return (new_weights, new_first, new_second)


def general(field, cotangent, weights, first_moment, second_moment):
    slab_count = lax.axis_size("space")
    batch_local = field.shape[0]
    cells_x = field.shape[1]
    total_x = cells_x * slab_count
    cos_z, sin_z = trig_tables(NZ, MZ, False)
    cos_y, sin_y = trig_tables(NY, MY, True)
    cos_x, sin_x = trig_tables(total_x, MX, True)
    table_z = jnp.stack([cos_z, -sin_z], axis=1)
    table_y = forward_table(cos_y, sin_y)
    table_x = forward_table(cos_x, sin_x)
    back_table_x = inverse_table(cos_x, sin_x)
    back_table_y = inverse_table(cos_y, sin_y)
    back_table_z = jnp.stack([cos_z.T, -sin_z.T], axis=0)
    product = functools.partial(jnp.einsum, preferred_element_type=f32)

    def swap(values, axis, split, concat):
        return lax.all_to_all(values, axis, split_axis=split, concat_axis=concat, tiled=True)

    def to_modes(slab_field):
        first_pass = product("bxyzc,zpk->bxypkc", slab_field, table_z).astype(half)
        second = product("bxypkc,ypmq->bxmkqc", first_pass, table_y).astype(half)
        second = second.reshape(batch_local, cells_x, MYZ, 2, C)
        along = product("bxpjc,xjmq->bmpqc", swap(second, "space", 2, 1), table_x).astype(half)
        return swap(swap(along, "space", 1, 2), "dp", 2, 0)

    field_hat = to_modes(field)
    cot_hat = to_modes(cotangent)
    rotated = jnp.stack([cot_hat[:, :, :, 1], -cot_hat[:, :, :, 0]], axis=3)
    form_in = "bmpjc,bmpjo->mpco"
    weight_grads = jnp.stack([product(form_in, field_hat, cot_hat), product(form_in, field_hat, rotated)], axis=2)
    half_weights = weights.astype(half)
    form_back = "mpjio,bmpjo->bmpi"
    mode_grads = jnp.stack(
        [product(form_back, half_weights, cot_hat), product(form_back, half_weights, rotated)], axis=3
    ).astype(half)
    updated = adam_update(weights, first_moment, second_moment, weight_grads)
    pencils = swap(swap(mode_grads, "dp", 0, 2), "space", 2, 1)
    back_x = product("bmpjc,mjxq->bxpqc", pencils, back_table_x).astype(half)
    unpacked = swap(back_x, "space", 1, 2).reshape(batch_local, cells_x, MY, MZ, 2, C)
    back_y = product("bxmkjc,mjyq->bxyqkc", unpacked, back_table_y).astype(half)
    field_grad = product("bxyqkc,qkz->bxyzc", back_y, back_table_z).astype(half)
    return (field_grad, *updated)


def solution(mesh):
    owners, spaces = mesh.shape["dp"], mesh.shape["space"]
    pencils = MYZ // (owners * QUAD)
    if spaces == 2 * QUAD and MX == 2 * spaces and MYZ % (owners * QUAD * 8) == 0 and pencils * owners % 2 == 0:
        mesh = jax.sharding.Mesh(mesh.devices.reshape(owners, 2, QUAD), ("dp", "half", "quad"))
        space, on_device = ("half", "quad"), fast
    else:
        space, on_device = "space", general
    grid = P("dp", space, None, None, None)
    held = P(space, "dp", None, None, None)
    return jax.shard_map(
        on_device,
        mesh=mesh,
        in_specs=(grid, grid, held, held, held),
        out_specs=(grid, held, held, held),
        check_vma=False,
    )
```

```python
import functools
import math

import jax
import jax.numpy as jnp
import ml_dtypes
import numpy as np
from jax import lax
from jax.experimental import pallas as pl
from jax.experimental.pallas import tpu as pltpu
from jax.sharding import PartitionSpec as P

C = 128
MX = 16
MY = 16
MZ = 8
NY = 32
NZ = 16
STEP = 100
MYZ = 128
QUAD = 4
PARTNERS = (0, 3, 1, 2)


decay_first = 0.9
decay_second = 0.999
learn_rate = 0.001
adam_floor = 1e-08

f32 = jnp.float32
half = jnp.bfloat16


def np_tables(length, modes_kept, signed):
    points = np.arange(length)
    frequency = np.arange(modes_kept) - (modes_kept // 2 if signed else 0)
    angles = np.mod(points[:, None] * frequency[None, :], length) * (2.0 * math.pi / length)
    factor = np.float32(1.0 / math.sqrt(length))
    cosine = (np.cos(angles).astype(np.float32) * factor).astype(ml_dtypes.bfloat16)
    sine = (np.sin(angles).astype(np.float32) * factor).astype(ml_dtypes.bfloat16)
    return cosine.astype(np.float64), sine.astype(np.float64)


def yz_table(dp_count):
    cos_z, sin_z = np_tables(NZ, MZ, False)
    cos_y, sin_y = np_tables(NY, MY, True)
    cy, sy = cos_y.T[:, None, :, None], sin_y.T[:, None, :, None]
    cz, sz = cos_z.T[None, :, None, :], sin_z.T[None, :, None, :]
    real = cy * cz - sy * sz
    imag = -(sy * cz + cy * sz)
    table = np.stack([real, imag], axis=2).reshape(MYZ, 2, NY * NZ)
    pencils = MYZ // dp_count // QUAD
    table = table.reshape(dp_count, QUAD, pencils, 2, NY * NZ).transpose(1, 0, 2, 3, 4)
    return table.reshape(QUAD, dp_count * pencils * 2, NY * NZ).astype(ml_dtypes.bfloat16)


def x_tables(total_x, halves, pencils):
    cos_x, sin_x = np_tables(total_x, MX, True)
    same = np.eye(pencils)
    span = total_x // halves
    forward, backward = [], []
    for part in range(halves):
        c, s = cos_x[part * span : (part + 1) * span], sin_x[part * span : (part + 1) * span]
        fwd = np.zeros((MX, pencils, 2, span, pencils, 2))
        fwd[:, :, 0, :, :, 0] = np.einsum("xm,pr->mpxr", c, same)
        fwd[:, :, 0, :, :, 1] = np.einsum("xm,pr->mpxr", s, same)
        fwd[:, :, 1, :, :, 0] = np.einsum("xm,pr->mpxr", -s, same)
        fwd[:, :, 1, :, :, 1] = np.einsum("xm,pr->mpxr", c, same)
        bwd = np.zeros((span, pencils, 2, MX, pencils, 2))
        bwd[:, :, 0, :, :, 0] = np.einsum("xm,pr->xpmr", c, same)
        bwd[:, :, 0, :, :, 1] = np.einsum("xm,pr->xpmr", -s, same)
        bwd[:, :, 1, :, :, 0] = np.einsum("xm,pr->xpmr", s, same)
        bwd[:, :, 1, :, :, 1] = np.einsum("xm,pr->xpmr", c, same)
        forward.append(fwd.reshape(MX * pencils * 2, span * pencils * 2))
        backward.append(bwd.reshape(span * pencils * 2, MX * pencils * 2))
    return np.stack(forward).astype(ml_dtypes.bfloat16), np.stack(backward).astype(ml_dtypes.bfloat16)


def gather_tables(batch, halves, modes, pencils):
    plain = np.zeros((modes, pencils, batch, 2, batch, halves, modes, pencils, 2))
    turned = np.zeros_like(plain)
    for m in range(modes):
        for p in range(pencils):
            for b in range(batch):
                plain[m, p, b, 0, b, :, m, p, 0] = 1.0
                plain[m, p, b, 1, b, :, m, p, 1] = 1.0
                turned[m, p, b, 0, b, :, m, p, 1] = 1.0
                turned[m, p, b, 1, b, :, m, p, 0] = -1.0
    rows = modes * pencils * batch * 2
    both = np.concatenate([plain.reshape(rows, -1), turned.reshape(rows, -1)])
    return both.astype(ml_dtypes.bfloat16)


def scatter_table(batch, modes, pencils):
    order = np.arange(modes * pencils * batch * 2).reshape(modes * pencils, batch, 2).transpose(1, 0, 2).reshape(-1)
    return np.eye(order.size)[order].astype(ml_dtypes.bfloat16)


def dot(a, b, dims=((1,), (0,))):
    return lax.dot_general(a, b, (dims, ((), ())), preferred_element_type=f32)


def yz_kernel(field, cotangent, table, *refs):
    blocks, (table_in, cells_in, sems) = refs[:QUAD], refs[QUAD:]
    rows = table.shape[1]
    cells = field.shape[0]
    loads = [
        pltpu.make_async_copy(table, table_in, sems.at[0]),
        pltpu.make_async_copy(field, cells_in.at[0], sems.at[1]),
        pltpu.make_async_copy(cotangent, cells_in.at[1], sems.at[2]),
    ]
    for load in loads:
        load.start()
    for load in loads:
        load.wait()
    matrix = jnp.concatenate([table_in[lax.axis_index("quad") ^ r] for r in range(QUAD)], axis=0)
    for which in range(2):
        for x in range(0, cells, 2):
            pair = jnp.concatenate([cells_in[which, x], cells_in[which, x + 1]], axis=1)
            result = dot(matrix, pair).astype(half)
            for r in range(QUAD):
                piece = result[r * rows : (r + 1) * rows]
                blocks[r][which, x] = piece[:, :C]
                blocks[r][which, x + 1] = piece[:, C:]


def x_kernel(*refs):
    pieces, (table, out, held) = refs[:QUAD], refs[QUAD:]
    for r, piece in zip(PARTNERS, pieces):
        held[lax.axis_index("quad") ^ r] = piece[...]
    matrix = table[lax.axis_index("half")]
    fields, cells, rows = held.shape[1:4]
    height = matrix.shape[1] // QUAD // cells
    spaces = out.shape[0] // (rows // height)
    for d in range(rows // height):
        columns = [
            jnp.concatenate(
                [held[q, f, x, d * height : (d + 1) * height, :] for q in range(QUAD) for x in range(cells)], axis=0
            )
            for f in range(fields)
        ]
        result = dot(matrix, jnp.concatenate(columns, axis=1)).astype(half)
        for f in range(fields):
            out[d * spaces : (d + 1) * spaces, f] = result[:, f * C : (f + 1) * C].reshape(spaces, -1, C)


def stage_kernel(after, weights, *refs):
    count = (len(refs) - 3) // 2
    sources, weights_held, held = refs[:count], refs[count], refs[count + 1 : 2 * count + 1]
    rounded, sems = refs[2 * count + 1 :]
    del after
    modes, pencils = weights.shape[:2]
    each = pencils // 4
    spans = [(m, p) for m in range(modes) for p in range(0, pencils, each)]
    loads = []

    def add(source, target):
        loads.append(pltpu.make_async_copy(source, target, sems.at[len(loads)]))

    for m, p in spans:
        add(weights.at[m, p : p + each], weights_held.at[m, p : p + each])
    for source, target in zip(sources, held):
        if len(source.shape) < 5:
            add(source, target)
        else:
            for m, p in spans:
                add(source.at[m, p : p + each], target.at[m, p : p + each])
    for load in loads:
        load.start()
    for k, (m, p) in enumerate(spans):
        loads[k].wait()

        def body(i, carry):
            for part in range(2):
                rounded[m, p + i, :, part * C : (part + 1) * C] = weights_held[m, p + i, part].astype(half)
            return carry

        lax.fori_loop(0, each, body, 0)
    for load in loads[len(spans) :]:
        load.wait()


def modes_kernel(arrived, weights, gather, scatter, sent, inputs, pairs):
    batch, halves, quad, _, rows, _ = arrived.shape
    modes, pencils = weights.shape[0], weights.shape[1] // quad
    height = batch * 2
    columns_out = []
    all_pairs = []
    for q in range(quad):
        field = arrived[:, :, q, 0].reshape(-1, C)
        cot = arrived[:, :, q, 1].reshape(-1, C)
        both = dot(gather[...], jnp.concatenate([field, cot], axis=1)).astype(half)
        count = both.shape[0] // 2
        inputs[q] = both[:count, :C]
        pair = jnp.concatenate([both[:count, C:], both[count:, C:]], axis=1)
        pairs[q] = pair
        all_pairs.append(pair)
    for q in range(quad):
        pair = all_pairs[q]
        results = []
        for m in range(modes):
            for p in range(0, pencils, 2):
                at = (m * pencils + p) * height
                first = q * pencils + p
                columns = weights[m, first : first + 2].reshape(2 * C, 2 * C)
                result = dot(pair[at : at + 2 * height], columns, ((1,), (1,)))
                results += [result[:height, :C], result[height:, C:]]
        columns_out.append(jnp.concatenate(results, axis=0).astype(half))
    spread = dot(scatter[...], jnp.concatenate(columns_out, axis=1)).astype(half)
    for q in range(quad):
        sent[:, q] = spread[:, q * C : (q + 1) * C].reshape(batch, rows, C)


def adam_kernel(begin, inputs, pairs, weights, first, second, *refs):
    new_weights, new_first, new_second, token, held, sems = refs[-6:]
    new = (new_weights, new_first, new_second)
    modes, pencils = weights.shape[:2]
    steps, count = held.shape[1:3]
    height = inputs.shape[1] // (modes * (pencils // QUAD))
    per_mode = pencils // count
    per_quad = per_mode // QUAD
    scale_first = learn_rate / (1.0 - decay_first**STEP)
    scale_second = 1.0 / (1.0 - decay_second**STEP)

    def copies(i):
        mode, at = (i + begin) // per_mode, (i + begin) % per_mode
        return [
            pltpu.make_async_copy(held.at[o, i], new[o].at[mode, pl.ds(at * count, count)], sems.at[i, o])
            for o in range(3)
        ]

    def body(i, carry):
        mode, at = (i + begin) // per_mode, (i + begin) % per_mode
        rows = count * height
        row = pl.multiple_of((mode * per_quad + at % per_quad) * rows, rows)
        us = inputs[at // per_quad, pl.ds(row, rows), :]
        gs = pairs[at // per_quad, pl.ds(row, rows), :]
        for k in range(count):
            u = us[k * height : (k + 1) * height]
            g = gs[k * height : (k + 1) * height]
            grads = dot(u, g, ((0,), (0,)))
            p = at * count + k
            for part in range(2):
                grad = grads[:, part * C : (part + 1) * C]
                m = decay_first * first[mode, p, part] + (1.0 - decay_first) * grad
                v = decay_second * second[mode, p, part] + ((1.0 - decay_second) * grad) * grad
                held[1, i, k, part] = m
                held[2, i, k, part] = v
                level = v * scale_second
                inverse = lax.rsqrt(level)
                floored = level * inverse + adam_floor
                inverse = inverse * (2.0 - floored * inverse)
                held[0, i, k, part] = weights[mode, p, part] - (scale_first * m) * inverse
        for copy in copies(i):
            copy.start()
        return carry

    def finish(i, carry):
        for copy in copies(i):
            copy.wait()
        return carry

    lax.fori_loop(0, steps, body, 0)
    lax.fori_loop(0, steps, finish, 0)
    token[...] = jnp.zeros_like(token)


def back_x_kernel(own, come, table, after, *refs):
    blocks, (arrived, held) = refs[:QUAD], refs[QUAD:]
    arrived[lax.axis_index("half")] = own[...]
    arrived[1 - lax.axis_index("half")] = come[...]
    matrix = table[lax.axis_index("half")]
    cells, owners, height, _ = blocks[0].shape
    halves = arrived.shape[0]
    span = cells * height
    for d in range(0, owners, 2):
        columns = [
            jnp.concatenate([arrived[h, k * QUAD : (k + 1) * QUAD].reshape(-1, C) for h in range(halves)], axis=0)
            for k in (d, d + 1)
        ]
        result = dot(matrix, jnp.concatenate(columns, axis=1)).astype(half)
        for q in range(QUAD):
            piece = result[q * span : (q + 1) * span].reshape(cells, height, 2 * C)
            held[q, :, d] = piece[:, :, :C]
            held[q, :, d + 1] = piece[:, :, C:]
    for r in range(QUAD):
        blocks[r][...] = held[lax.axis_index("quad") ^ r]


def back_yz_kernel(*refs):
    pieces, (table, after, out, held) = refs[:QUAD], refs[QUAD:]
    for r, piece in zip(PARTNERS, pieces):
        held[lax.axis_index("quad") ^ r] = piece[...]
    matrix = table[...]
    for x in range(0, out.shape[0], 2):
        columns = jnp.concatenate([held[:, k].reshape(-1, C) for k in (x, x + 1)], axis=1)
        result = dot(matrix, columns).astype(half)
        out[x] = result[:, :C]
        out[x + 1] = result[:, C:]


VMEM = pl.BlockSpec(memory_space=pltpu.VMEM)
HBM = pl.BlockSpec(memory_space=pltpu.HBM)
ANY = pl.BlockSpec(memory_space=pl.ANY)
MIB = 1 << 20


def params(mib, **more):
    return pltpu.CompilerParams(vmem_limit_bytes=mib * MIB, **more)


def cost(size):
    return pl.CostEstimate(flops=0, bytes_accessed=size, transcendentals=0)


def in_hbm(values):
    return pltpu.with_memory_space_constraint(values, pltpu.HBM)


def exchange(blocks):
    moved = [lax.ppermute(blocks[r], "quad", [(q, q ^ r) for q in range(QUAD)]) for r in PARTNERS[1:]]
    return [blocks[0]] + moved


def swap_halves(values):
    return lax.ppermute(values, "half", [(0, 1), (1, 0)])


def fast(field, cotangent, weights, first_moment, second_moment):
    halves = lax.axis_size("half")
    spaces = halves * QUAD
    owners = lax.axis_size("dp")
    cells = field.shape[1]
    total_x = cells * spaces
    pencils = MYZ // owners // QUAD
    modes = MX // spaces
    height = pencils * 2
    table_yz = yz_table(owners)
    table_x, back_table_x = x_tables(total_x, halves, pencils)
    back_table_yz = np.ascontiguousarray(table_yz.reshape(MYZ * 2, NY * NZ).T)
    gather = gather_tables(owners, halves, modes, pencils)
    scatter = scatter_table(owners, modes, pencils)
    vmem = lambda values: pltpu.VMEM(values.shape, values.dtype)

    flat = (cells, NY * NZ, C)
    blocks = pl.pallas_call(
        yz_kernel,
        out_shape=[pltpu.VMEM((2, cells, owners * height, C), half)] * QUAD,
        in_specs=[HBM] * 3,
        out_specs=[VMEM] * QUAD,
        scratch_shapes=[
            pltpu.VMEM(table_yz.shape, half),
            pltpu.VMEM((2,) + flat, half),
            pltpu.SemaphoreType.DMA((3,)),
        ],
        compiler_params=params(8),
        name="yz_modes",
    )(in_hbm(field.reshape(flat)), in_hbm(cotangent.reshape(flat)), in_hbm(jnp.asarray(table_yz)))

    split = (modes, QUAD * pencils, 2, C, C)
    big, first, second = weights.reshape(split), first_moment.reshape(split), second_moment.reshape(split)
    staged = [jnp.asarray(t) for t in (table_x, gather, scatter, back_table_x, back_table_yz)]
    weights_held, table_x, gather, scatter, back_table_x, back_table_yz, rounded = pl.pallas_call(
        stage_kernel,
        out_shape=[vmem(big)] + [vmem(t) for t in staged] + [pltpu.VMEM((modes, QUAD * pencils, C, 2 * C), half)],
        in_specs=[ANY] + [HBM] * (1 + len(staged)),
        out_specs=[VMEM] * (2 + len(staged)),
        scratch_shapes=[pltpu.SemaphoreType.DMA((4 * modes + len(staged),))],
        compiler_params=params(8),
        cost_estimate=cost(0),
        name="stage",
    )(blocks[0], in_hbm(big), *[in_hbm(t) for t in staged])
    blocks = exchange(blocks)

    rows = modes * height
    per_half = (owners * QUAD, rows, C)
    partial = pl.pallas_call(
        x_kernel,
        out_shape=pltpu.VMEM((owners * spaces, 2, rows, C), half),
        in_specs=[VMEM] * (QUAD + 1),
        out_specs=VMEM,
        scratch_shapes=[pltpu.VMEM((QUAD, 2, cells, owners * height, C), half)],
        compiler_params=params(8),
        name="x_modes",
    )(*blocks, table_x)
    arrived = lax.all_to_all(partial, ("dp", "half", "quad"), 0, 0, tiled=True)

    mode_rows = rows * owners
    sent, inputs, pairs = pl.pallas_call(
        modes_kernel,
        out_shape=[
            pltpu.VMEM((owners, QUAD, rows, C), half),
            pltpu.VMEM((QUAD, mode_rows, C), half),
            pltpu.VMEM((QUAD, mode_rows, 2 * C), half),
        ],
        in_specs=[VMEM] * 4,
        out_specs=[VMEM] * 3,
        compiler_params=params(8),
        name="mode_grads",
    )(arrived.reshape(owners, halves, QUAD, 2, rows, C), rounded, gather, scatter)
    back = lax.all_to_all(sent.reshape(per_half), ("dp", "quad"), 0, 0, tiled=True)
    back_come = swap_halves(back)

    count = 4
    total = modes * QUAD * pencils // count
    first_steps = total * 13 // 16

    def adam(begin, end, after, *before):
        steps = end - begin
        return pl.pallas_call(
            functools.partial(adam_kernel, begin),
            out_shape=[pltpu.HBM(split, f32)] * 3 + [pltpu.VMEM((8, C), f32)],
            in_specs=[VMEM] * 5 + [ANY] + [HBM] * len(before),
            out_specs=[HBM] * 3 + [VMEM],
            scratch_shapes=[
                pltpu.VMEM((3, steps, count, 2, C, C), f32),
                pltpu.SemaphoreType.DMA((steps, 3)),
            ],
            input_output_aliases={6 + k: k for k in range(len(before))},
            compiler_params=params(22),
            cost_estimate=cost(16 * weights.size * steps // total),
            name="adam",
        )(inputs, pairs, weights_held, first, second, after, *before)

    *updated, token = adam(0, first_steps, back)
    blocks = pl.pallas_call(
        back_x_kernel,
        out_shape=[pltpu.VMEM((cells, owners, height, C), half)] * QUAD,
        in_specs=[VMEM] * 3 + [ANY],
        out_specs=[VMEM] * QUAD,
        scratch_shapes=[
            pltpu.VMEM((halves,) + per_half, half),
            pltpu.VMEM((QUAD, cells, owners, height, C), half),
        ],
        compiler_params=params(8),
        name="back_x",
    )(back, back_come, back_table_x, token)
    *updated, token = adam(first_steps, total, blocks[1], *updated)
    blocks = exchange(blocks)
    field_grad = pl.pallas_call(
        back_yz_kernel,
        out_shape=jax.ShapeDtypeStruct((cells, NY * NZ, C), half),
        in_specs=[VMEM] * (QUAD + 1) + [ANY],
        out_specs=VMEM,
        scratch_shapes=[pltpu.VMEM((QUAD, cells, owners, height, C), half)],
        compiler_params=params(8),
        name="back_yz",
    )(*blocks, back_table_yz, token)
    return (field_grad.reshape(field.shape), *[values.reshape(weights.shape) for values in updated])


def trig_tables(length, modes_kept, signed):
    cosine, sine_part = np_tables(length, modes_kept, signed)
    return jnp.asarray(cosine, half), jnp.asarray(sine_part, half)


def forward_table(cosine, sine_part):
    real_row = jnp.stack([cosine, -sine_part], axis=-1)
    imag_row = jnp.stack([sine_part, cosine], axis=-1)
    return jnp.stack([real_row, imag_row], axis=1)


def inverse_table(cosine, sine_part):
    real_row = jnp.stack([cosine.T, sine_part.T], axis=-1)
    imag_row = jnp.stack([-sine_part.T, cosine.T], axis=-1)
    return jnp.stack([real_row, imag_row], axis=1)


def adam_update(weights, first_moment, second_moment, weight_grads):
    new_first = decay_first * first_moment + (1.0 - decay_first) * weight_grads
    new_second = decay_second * second_moment + (1.0 - decay_second) * weight_grads * weight_grads
    first_hat = new_first / (1.0 - decay_first**STEP)
    second_hat = new_second / (1.0 - decay_second**STEP)
    new_weights = weights - learn_rate * first_hat / (jnp.sqrt(second_hat) + adam_floor)
    return (new_weights, new_first, new_second)


def general(field, cotangent, weights, first_moment, second_moment):
    slab_count = lax.axis_size("space")
    batch_local = field.shape[0]
    cells_x = field.shape[1]
    total_x = cells_x * slab_count
    cos_z, sin_z = trig_tables(NZ, MZ, False)
    cos_y, sin_y = trig_tables(NY, MY, True)
    cos_x, sin_x = trig_tables(total_x, MX, True)
    table_z = jnp.stack([cos_z, -sin_z], axis=1)
    table_y = forward_table(cos_y, sin_y)
    table_x = forward_table(cos_x, sin_x)
    back_table_x = inverse_table(cos_x, sin_x)
    back_table_y = inverse_table(cos_y, sin_y)
    back_table_z = jnp.stack([cos_z.T, -sin_z.T], axis=0)
    product = functools.partial(jnp.einsum, preferred_element_type=f32)

    def swap(values, axis, split, concat):
        return lax.all_to_all(values, axis, split_axis=split, concat_axis=concat, tiled=True)

    def to_modes(slab_field):
        first_pass = product("bxyzc,zpk->bxypkc", slab_field, table_z).astype(half)
        second = product("bxypkc,ypmq->bxmkqc", first_pass, table_y).astype(half)
        second = second.reshape(batch_local, cells_x, MYZ, 2, C)
        along = product("bxpjc,xjmq->bmpqc", swap(second, "space", 2, 1), table_x).astype(half)
        return swap(swap(along, "space", 1, 2), "dp", 2, 0)

    field_hat = to_modes(field)
    cot_hat = to_modes(cotangent)
    rotated = jnp.stack([cot_hat[:, :, :, 1], -cot_hat[:, :, :, 0]], axis=3)
    form_in = "bmpjc,bmpjo->mpco"
    weight_grads = jnp.stack([product(form_in, field_hat, cot_hat), product(form_in, field_hat, rotated)], axis=2)
    half_weights = weights.astype(half)
    form_back = "mpjio,bmpjo->bmpi"
    mode_grads = jnp.stack(
        [product(form_back, half_weights, cot_hat), product(form_back, half_weights, rotated)], axis=3
    ).astype(half)
    updated = adam_update(weights, first_moment, second_moment, weight_grads)
    pencils = swap(swap(mode_grads, "dp", 0, 2), "space", 2, 1)
    back_x = product("bmpjc,mjxq->bxpqc", pencils, back_table_x).astype(half)
    unpacked = swap(back_x, "space", 1, 2).reshape(batch_local, cells_x, MY, MZ, 2, C)
    back_y = product("bxmkjc,mjyq->bxyqkc", unpacked, back_table_y).astype(half)
    field_grad = product("bxyqkc,qkz->bxyzc", back_y, back_table_z).astype(half)
    return (field_grad, *updated)


def solution(mesh):
    owners, spaces = mesh.shape["dp"], mesh.shape["space"]
    pencils = MYZ // (owners * QUAD)
    if spaces == 2 * QUAD and MX == 2 * spaces and MYZ % (owners * QUAD * 8) == 0 and pencils * owners % 2 == 0:
        mesh = jax.sharding.Mesh(mesh.devices.reshape(owners, 2, QUAD), ("dp", "half", "quad"))
        space, on_device = ("half", "quad"), fast
    else:
        space, on_device = "space", general
    grid = P("dp", space, None, None, None)
    held = P(space, "dp", None, None, None)
    return jax.shard_map(
        on_device,
        mesh=mesh,
        in_specs=(grid, grid, held, held, held),
        out_specs=(grid, held, held, held),
        check_vma=False,
    )
```

```python
import functools
import math

import jax
import jax.numpy as jnp
import ml_dtypes
import numpy as np
from jax import lax
from jax.experimental import pallas as pl
from jax.experimental.pallas import tpu as pltpu
from jax.sharding import PartitionSpec as P

C = 128
MX = 16
MY = 16
MZ = 8
NY = 32
NZ = 16
STEP = 100
MYZ = 128
QUAD = 4
PARTNERS = (0, 3, 1, 2)


decay_first = 0.9
decay_second = 0.999
learn_rate = 0.001
adam_floor = 1e-08

f32 = jnp.float32
half = jnp.bfloat16


def np_tables(length, modes_kept, signed):
    points = np.arange(length)
    frequency = np.arange(modes_kept) - (modes_kept // 2 if signed else 0)
    angles = np.mod(points[:, None] * frequency[None, :], length) * (2.0 * math.pi / length)
    factor = np.float32(1.0 / math.sqrt(length))
    cosine = (np.cos(angles).astype(np.float32) * factor).astype(ml_dtypes.bfloat16)
    sine = (np.sin(angles).astype(np.float32) * factor).astype(ml_dtypes.bfloat16)
    return cosine.astype(np.float64), sine.astype(np.float64)


def yz_table(dp_count):
    cos_z, sin_z = np_tables(NZ, MZ, False)
    cos_y, sin_y = np_tables(NY, MY, True)
    cy, sy = cos_y.T[:, None, :, None], sin_y.T[:, None, :, None]
    cz, sz = cos_z.T[None, :, None, :], sin_z.T[None, :, None, :]
    real = cy * cz - sy * sz
    imag = -(sy * cz + cy * sz)
    table = np.stack([real, imag], axis=2).reshape(MYZ, 2, NY * NZ)
    pencils = MYZ // dp_count // QUAD
    table = table.reshape(dp_count, QUAD, pencils, 2, NY * NZ).transpose(1, 0, 2, 3, 4)
    return table.reshape(QUAD, dp_count * pencils * 2, NY * NZ).astype(ml_dtypes.bfloat16)


def x_tables(total_x, halves, pencils):
    cos_x, sin_x = np_tables(total_x, MX, True)
    same = np.eye(pencils)
    span = total_x // halves
    forward, backward = [], []
    for part in range(halves):
        c, s = cos_x[part * span : (part + 1) * span], sin_x[part * span : (part + 1) * span]
        fwd = np.zeros((MX, pencils, 2, span, pencils, 2))
        fwd[:, :, 0, :, :, 0] = np.einsum("xm,pr->mpxr", c, same)
        fwd[:, :, 0, :, :, 1] = np.einsum("xm,pr->mpxr", s, same)
        fwd[:, :, 1, :, :, 0] = np.einsum("xm,pr->mpxr", -s, same)
        fwd[:, :, 1, :, :, 1] = np.einsum("xm,pr->mpxr", c, same)
        bwd = np.zeros((span, pencils, 2, MX, pencils, 2))
        bwd[:, :, 0, :, :, 0] = np.einsum("xm,pr->xpmr", c, same)
        bwd[:, :, 0, :, :, 1] = np.einsum("xm,pr->xpmr", -s, same)
        bwd[:, :, 1, :, :, 0] = np.einsum("xm,pr->xpmr", s, same)
        bwd[:, :, 1, :, :, 1] = np.einsum("xm,pr->xpmr", c, same)
        forward.append(fwd.reshape(MX * pencils * 2, span * pencils * 2))
        backward.append(bwd.reshape(span * pencils * 2, MX * pencils * 2))
    return np.stack(forward).astype(ml_dtypes.bfloat16), np.stack(backward).astype(ml_dtypes.bfloat16)


def gather_tables(batch, halves, modes, pencils):
    plain = np.zeros((modes, pencils, batch, 2, batch, halves, modes, pencils, 2))
    turned = np.zeros_like(plain)
    for m in range(modes):
        for p in range(pencils):
            for b in range(batch):
                plain[m, p, b, 0, b, :, m, p, 0] = 1.0
                plain[m, p, b, 1, b, :, m, p, 1] = 1.0
                turned[m, p, b, 0, b, :, m, p, 1] = 1.0
                turned[m, p, b, 1, b, :, m, p, 0] = -1.0
    rows = modes * pencils * batch * 2
    both = np.concatenate([plain.reshape(rows, -1), turned.reshape(rows, -1)])
    return both.astype(ml_dtypes.bfloat16)


def scatter_table(batch, modes, pencils):
    order = np.arange(modes * pencils * batch * 2).reshape(modes * pencils, batch, 2).transpose(1, 0, 2).reshape(-1)
    return np.eye(order.size)[order].astype(ml_dtypes.bfloat16)


def dot(a, b, dims=((1,), (0,))):
    return lax.dot_general(a, b, (dims, ((), ())), preferred_element_type=f32)


def yz_kernel(field, cotangent, table, *refs):
    blocks, (table_in, cells_in, sems) = refs[:QUAD], refs[QUAD:]
    rows = table.shape[1]
    cells = field.shape[0]
    loads = [
        pltpu.make_async_copy(table, table_in, sems.at[0]),
        pltpu.make_async_copy(field, cells_in.at[0], sems.at[1]),
        pltpu.make_async_copy(cotangent, cells_in.at[1], sems.at[2]),
    ]
    for load in loads:
        load.start()
    for load in loads:
        load.wait()
    matrix = jnp.concatenate([table_in[lax.axis_index("quad") ^ r] for r in range(QUAD)], axis=0)
    for which in range(2):
        for x in range(0, cells, 2):
            pair = jnp.concatenate([cells_in[which, x], cells_in[which, x + 1]], axis=1)
            result = dot(matrix, pair).astype(half)
            for r in range(QUAD):
                piece = result[r * rows : (r + 1) * rows]
                blocks[r][which, x] = piece[:, :C]
                blocks[r][which, x + 1] = piece[:, C:]


def x_kernel(*refs):
    pieces, (table, out, held) = refs[:QUAD], refs[QUAD:]
    for r, piece in zip(PARTNERS, pieces):
        held[lax.axis_index("quad") ^ r] = piece[...]
    matrix = table[lax.axis_index("half")]
    fields, cells, rows = held.shape[1:4]
    height = matrix.shape[1] // QUAD // cells
    spaces = out.shape[0] // (rows // height)
    for d in range(rows // height):
        columns = [
            jnp.concatenate(
                [held[q, f, x, d * height : (d + 1) * height, :] for q in range(QUAD) for x in range(cells)], axis=0
            )
            for f in range(fields)
        ]
        result = dot(matrix, jnp.concatenate(columns, axis=1)).astype(half)
        for f in range(fields):
            out[d * spaces : (d + 1) * spaces, f] = result[:, f * C : (f + 1) * C].reshape(spaces, -1, C)


def stage_kernel(after, weights, *refs):
    count = (len(refs) - 3) // 2
    sources, weights_held, held = refs[:count], refs[count], refs[count + 1 : 2 * count + 1]
    rounded, sems = refs[2 * count + 1 :]
    del after
    modes, pencils = weights.shape[:2]
    each = pencils // 4
    spans = [(m, p) for m in range(modes) for p in range(0, pencils, each)]
    loads = []

    def add(source, target):
        loads.append(pltpu.make_async_copy(source, target, sems.at[len(loads)]))

    for m, p in spans:
        add(weights.at[m, p : p + each], weights_held.at[m, p : p + each])
    for source, target in zip(sources, held):
        if len(source.shape) < 5:
            add(source, target)
        else:
            for m, p in spans:
                add(source.at[m, p : p + each], target.at[m, p : p + each])
    for load in loads:
        load.start()
    for k, (m, p) in enumerate(spans):
        loads[k].wait()

        def body(i, carry):
            for part in range(2):
                rounded[m, p + i, :, part * C : (part + 1) * C] = weights_held[m, p + i, part].astype(half)
            return carry

        lax.fori_loop(0, each, body, 0)
    for load in loads[len(spans) :]:
        load.wait()


def modes_kernel(arrived, weights, gather, scatter, sent, inputs, pairs):
    batch, halves, quad, _, rows, _ = arrived.shape
    modes, pencils = weights.shape[0], weights.shape[1] // quad
    height = batch * 2
    columns_out = []
    wide = [arrived[:, :, q, f].reshape(-1, C) for q in range(quad) for f in range(2)]
    gathered = dot(gather[...], jnp.concatenate(wide, axis=1)).astype(half)
    count = gathered.shape[0] // 2
    all_pairs = []
    for q in range(quad):
        both = gathered[:, q * 2 * C : (q + 1) * 2 * C]
        inputs[q] = both[:count, :C]
        pair = jnp.concatenate([both[:count, C:], both[count:, C:]], axis=1)
        pairs[q] = pair
        all_pairs.append(pair)
    for q in range(quad):
        pair = all_pairs[q]
        results = []
        for m in range(modes):
            for p in range(0, pencils, 2):
                at = (m * pencils + p) * height
                first = q * pencils + p
                columns = weights[m, first : first + 2].reshape(2 * C, 2 * C)
                result = dot(pair[at : at + 2 * height], columns, ((1,), (1,)))
                results += [result[:height, :C], result[height:, C:]]
        columns_out.append(jnp.concatenate(results, axis=0).astype(half))
    spread = dot(scatter[...], jnp.concatenate(columns_out, axis=1)).astype(half)
    for q in range(quad):
        sent[:, q] = spread[:, q * C : (q + 1) * C].reshape(batch, rows, C)


def adam_kernel(begin, inputs, pairs, weights, first, second, *refs):
    new_weights, new_first, new_second, token, held, sems = refs[-6:]
    new = (new_weights, new_first, new_second)
    modes, pencils = weights.shape[:2]
    steps, count = held.shape[1:3]
    height = inputs.shape[1] // (modes * (pencils // QUAD))
    per_mode = pencils // count
    per_quad = per_mode // QUAD
    scale_first = learn_rate / (1.0 - decay_first**STEP)
    scale_second = 1.0 / (1.0 - decay_second**STEP)

    def copies(i):
        mode, at = (i + begin) // per_mode, (i + begin) % per_mode
        return [
            pltpu.make_async_copy(held.at[o, i], new[o].at[mode, pl.ds(at * count, count)], sems.at[i, o])
            for o in range(3)
        ]

    def body(i, carry):
        mode, at = (i + begin) // per_mode, (i + begin) % per_mode
        rows = count * height
        row = pl.multiple_of((mode * per_quad + at % per_quad) * rows, rows)
        us = inputs[at // per_quad, pl.ds(row, rows), :]
        gs = pairs[at // per_quad, pl.ds(row, rows), :]
        for k in range(count):
            u = us[k * height : (k + 1) * height]
            g = gs[k * height : (k + 1) * height]
            grads = dot(u, g, ((0,), (0,)))
            p = at * count + k
            for part in range(2):
                grad = grads[:, part * C : (part + 1) * C]
                m = decay_first * first[mode, p, part] + (1.0 - decay_first) * grad
                v = decay_second * second[mode, p, part] + ((1.0 - decay_second) * grad) * grad
                held[1, i, k, part] = m
                held[2, i, k, part] = v
                level = v * scale_second
                inverse = lax.rsqrt(level)
                floored = level * inverse + adam_floor
                inverse = inverse * (2.0 - floored * inverse)
                held[0, i, k, part] = weights[mode, p, part] - (scale_first * m) * inverse
        for copy in copies(i):
            copy.start()
        return carry

    def finish(i, carry):
        for copy in copies(i):
            copy.wait()
        return carry

    lax.fori_loop(0, steps, body, 0)
    lax.fori_loop(0, steps, finish, 0)
    token[...] = jnp.zeros_like(token)


def back_x_kernel(own, come, table, after, *refs):
    blocks, (arrived, held) = refs[:QUAD], refs[QUAD:]
    arrived[lax.axis_index("half")] = own[...]
    arrived[1 - lax.axis_index("half")] = come[...]
    matrix = table[lax.axis_index("half")]
    cells, owners, height, _ = blocks[0].shape
    halves = arrived.shape[0]
    span = cells * height
    for d in range(0, owners, 2):
        columns = [
            jnp.concatenate([arrived[h, k * QUAD : (k + 1) * QUAD].reshape(-1, C) for h in range(halves)], axis=0)
            for k in (d, d + 1)
        ]
        result = dot(matrix, jnp.concatenate(columns, axis=1)).astype(half)
        for q in range(QUAD):
            piece = result[q * span : (q + 1) * span].reshape(cells, height, 2 * C)
            held[q, :, d] = piece[:, :, :C]
            held[q, :, d + 1] = piece[:, :, C:]
    for r in range(QUAD):
        blocks[r][...] = held[lax.axis_index("quad") ^ r]


def back_yz_kernel(*refs):
    pieces, (table, after, out, held) = refs[:QUAD], refs[QUAD:]
    for r, piece in zip(PARTNERS, pieces):
        held[lax.axis_index("quad") ^ r] = piece[...]
    matrix = table[...]
    for x in range(0, out.shape[0], 2):
        columns = jnp.concatenate([held[:, k].reshape(-1, C) for k in (x, x + 1)], axis=1)
        result = dot(matrix, columns).astype(half)
        out[x] = result[:, :C]
        out[x + 1] = result[:, C:]


VMEM = pl.BlockSpec(memory_space=pltpu.VMEM)
HBM = pl.BlockSpec(memory_space=pltpu.HBM)
ANY = pl.BlockSpec(memory_space=pl.ANY)
MIB = 1 << 20


def params(mib, **more):
    return pltpu.CompilerParams(vmem_limit_bytes=mib * MIB, **more)


def cost(size):
    return pl.CostEstimate(flops=0, bytes_accessed=size, transcendentals=0)


def in_hbm(values):
    return pltpu.with_memory_space_constraint(values, pltpu.HBM)


def exchange(blocks):
    moved = [lax.ppermute(blocks[r], "quad", [(q, q ^ r) for q in range(QUAD)]) for r in PARTNERS[1:]]
    return [blocks[0]] + moved


def swap_halves(values):
    return lax.ppermute(values, "half", [(0, 1), (1, 0)])


def fast(field, cotangent, weights, first_moment, second_moment):
    halves = lax.axis_size("half")
    spaces = halves * QUAD
    owners = lax.axis_size("dp")
    cells = field.shape[1]
    total_x = cells * spaces
    pencils = MYZ // owners // QUAD
    modes = MX // spaces
    height = pencils * 2
    table_yz = yz_table(owners)
    table_x, back_table_x = x_tables(total_x, halves, pencils)
    back_table_yz = np.ascontiguousarray(table_yz.reshape(MYZ * 2, NY * NZ).T)
    gather = gather_tables(owners, halves, modes, pencils)
    scatter = scatter_table(owners, modes, pencils)
    vmem = lambda values: pltpu.VMEM(values.shape, values.dtype)

    flat = (cells, NY * NZ, C)
    blocks = pl.pallas_call(
        yz_kernel,
        out_shape=[pltpu.VMEM((2, cells, owners * height, C), half)] * QUAD,
        in_specs=[HBM] * 3,
        out_specs=[VMEM] * QUAD,
        scratch_shapes=[
            pltpu.VMEM(table_yz.shape, half),
            pltpu.VMEM((2,) + flat, half),
            pltpu.SemaphoreType.DMA((3,)),
        ],
        compiler_params=params(8),
        name="yz_modes",
    )(in_hbm(field.reshape(flat)), in_hbm(cotangent.reshape(flat)), in_hbm(jnp.asarray(table_yz)))

    split = (modes, QUAD * pencils, 2, C, C)
    big, first, second = weights.reshape(split), first_moment.reshape(split), second_moment.reshape(split)
    staged = [jnp.asarray(t) for t in (table_x, gather, scatter, back_table_x, back_table_yz)]
    weights_held, table_x, gather, scatter, back_table_x, back_table_yz, rounded = pl.pallas_call(
        stage_kernel,
        out_shape=[vmem(big)] + [vmem(t) for t in staged] + [pltpu.VMEM((modes, QUAD * pencils, C, 2 * C), half)],
        in_specs=[ANY] + [HBM] * (1 + len(staged)),
        out_specs=[VMEM] * (2 + len(staged)),
        scratch_shapes=[pltpu.SemaphoreType.DMA((4 * modes + len(staged),))],
        compiler_params=params(8),
        cost_estimate=cost(0),
        name="stage",
    )(blocks[0], in_hbm(big), *[in_hbm(t) for t in staged])
    blocks = exchange(blocks)

    rows = modes * height
    per_half = (owners * QUAD, rows, C)
    partial = pl.pallas_call(
        x_kernel,
        out_shape=pltpu.VMEM((owners * spaces, 2, rows, C), half),
        in_specs=[VMEM] * (QUAD + 1),
        out_specs=VMEM,
        scratch_shapes=[pltpu.VMEM((QUAD, 2, cells, owners * height, C), half)],
        compiler_params=params(8),
        name="x_modes",
    )(*blocks, table_x)
    arrived = lax.all_to_all(partial, ("dp", "half", "quad"), 0, 0, tiled=True)

    mode_rows = rows * owners
    sent, inputs, pairs = pl.pallas_call(
        modes_kernel,
        out_shape=[
            pltpu.VMEM((owners, QUAD, rows, C), half),
            pltpu.VMEM((QUAD, mode_rows, C), half),
            pltpu.VMEM((QUAD, mode_rows, 2 * C), half),
        ],
        in_specs=[VMEM] * 4,
        out_specs=[VMEM] * 3,
        compiler_params=params(8),
        name="mode_grads",
    )(arrived.reshape(owners, halves, QUAD, 2, rows, C), rounded, gather, scatter)
    back = lax.all_to_all(sent.reshape(per_half), ("dp", "quad"), 0, 0, tiled=True)
    back_come = swap_halves(back)

    count = 4
    total = modes * QUAD * pencils // count
    first_steps = total * 13 // 16

    def adam(begin, end, after, *before):
        steps = end - begin
        return pl.pallas_call(
            functools.partial(adam_kernel, begin),
            out_shape=[pltpu.HBM(split, f32)] * 3 + [pltpu.VMEM((8, C), f32)],
            in_specs=[VMEM] * 5 + [ANY] + [HBM] * len(before),
            out_specs=[HBM] * 3 + [VMEM],
            scratch_shapes=[
                pltpu.VMEM((3, steps, count, 2, C, C), f32),
                pltpu.SemaphoreType.DMA((steps, 3)),
            ],
            input_output_aliases={6 + k: k for k in range(len(before))},
            compiler_params=params(22),
            cost_estimate=cost(16 * weights.size * steps // total),
            name="adam",
        )(inputs, pairs, weights_held, first, second, after, *before)

    *updated, token = adam(0, first_steps, back)
    blocks = pl.pallas_call(
        back_x_kernel,
        out_shape=[pltpu.VMEM((cells, owners, height, C), half)] * QUAD,
        in_specs=[VMEM] * 3 + [ANY],
        out_specs=[VMEM] * QUAD,
        scratch_shapes=[
            pltpu.VMEM((halves,) + per_half, half),
            pltpu.VMEM((QUAD, cells, owners, height, C), half),
        ],
        compiler_params=params(8),
        name="back_x",
    )(back, back_come, back_table_x, token)
    *updated, token = adam(first_steps, total, blocks[1], *updated)
    blocks = exchange(blocks)
    field_grad = pl.pallas_call(
        back_yz_kernel,
        out_shape=jax.ShapeDtypeStruct((cells, NY * NZ, C), half),
        in_specs=[VMEM] * (QUAD + 1) + [ANY],
        out_specs=VMEM,
        scratch_shapes=[pltpu.VMEM((QUAD, cells, owners, height, C), half)],
        compiler_params=params(8),
        name="back_yz",
    )(*blocks, back_table_yz, token)
    return (field_grad.reshape(field.shape), *[values.reshape(weights.shape) for values in updated])


def trig_tables(length, modes_kept, signed):
    cosine, sine_part = np_tables(length, modes_kept, signed)
    return jnp.asarray(cosine, half), jnp.asarray(sine_part, half)


def forward_table(cosine, sine_part):
    real_row = jnp.stack([cosine, -sine_part], axis=-1)
    imag_row = jnp.stack([sine_part, cosine], axis=-1)
    return jnp.stack([real_row, imag_row], axis=1)


def inverse_table(cosine, sine_part):
    real_row = jnp.stack([cosine.T, sine_part.T], axis=-1)
    imag_row = jnp.stack([-sine_part.T, cosine.T], axis=-1)
    return jnp.stack([real_row, imag_row], axis=1)


def adam_update(weights, first_moment, second_moment, weight_grads):
    new_first = decay_first * first_moment + (1.0 - decay_first) * weight_grads
    new_second = decay_second * second_moment + (1.0 - decay_second) * weight_grads * weight_grads
    first_hat = new_first / (1.0 - decay_first**STEP)
    second_hat = new_second / (1.0 - decay_second**STEP)
    new_weights = weights - learn_rate * first_hat / (jnp.sqrt(second_hat) + adam_floor)
    return (new_weights, new_first, new_second)


def general(field, cotangent, weights, first_moment, second_moment):
    slab_count = lax.axis_size("space")
    batch_local = field.shape[0]
    cells_x = field.shape[1]
    total_x = cells_x * slab_count
    cos_z, sin_z = trig_tables(NZ, MZ, False)
    cos_y, sin_y = trig_tables(NY, MY, True)
    cos_x, sin_x = trig_tables(total_x, MX, True)
    table_z = jnp.stack([cos_z, -sin_z], axis=1)
    table_y = forward_table(cos_y, sin_y)
    table_x = forward_table(cos_x, sin_x)
    back_table_x = inverse_table(cos_x, sin_x)
    back_table_y = inverse_table(cos_y, sin_y)
    back_table_z = jnp.stack([cos_z.T, -sin_z.T], axis=0)
    product = functools.partial(jnp.einsum, preferred_element_type=f32)

    def swap(values, axis, split, concat):
        return lax.all_to_all(values, axis, split_axis=split, concat_axis=concat, tiled=True)

    def to_modes(slab_field):
        first_pass = product("bxyzc,zpk->bxypkc", slab_field, table_z).astype(half)
        second = product("bxypkc,ypmq->bxmkqc", first_pass, table_y).astype(half)
        second = second.reshape(batch_local, cells_x, MYZ, 2, C)
        along = product("bxpjc,xjmq->bmpqc", swap(second, "space", 2, 1), table_x).astype(half)
        return swap(swap(along, "space", 1, 2), "dp", 2, 0)

    field_hat = to_modes(field)
    cot_hat = to_modes(cotangent)
    rotated = jnp.stack([cot_hat[:, :, :, 1], -cot_hat[:, :, :, 0]], axis=3)
    form_in = "bmpjc,bmpjo->mpco"
    weight_grads = jnp.stack([product(form_in, field_hat, cot_hat), product(form_in, field_hat, rotated)], axis=2)
    half_weights = weights.astype(half)
    form_back = "mpjio,bmpjo->bmpi"
    mode_grads = jnp.stack(
        [product(form_back, half_weights, cot_hat), product(form_back, half_weights, rotated)], axis=3
    ).astype(half)
    updated = adam_update(weights, first_moment, second_moment, weight_grads)
    pencils = swap(swap(mode_grads, "dp", 0, 2), "space", 2, 1)
    back_x = product("bmpjc,mjxq->bxpqc", pencils, back_table_x).astype(half)
    unpacked = swap(back_x, "space", 1, 2).reshape(batch_local, cells_x, MY, MZ, 2, C)
    back_y = product("bxmkjc,mjyq->bxyqkc", unpacked, back_table_y).astype(half)
    field_grad = product("bxyqkc,qkz->bxyzc", back_y, back_table_z).astype(half)
    return (field_grad, *updated)


def solution(mesh):
    owners, spaces = mesh.shape["dp"], mesh.shape["space"]
    pencils = MYZ // (owners * QUAD)
    if spaces == 2 * QUAD and MX == 2 * spaces and MYZ % (owners * QUAD * 8) == 0 and pencils * owners % 2 == 0:
        mesh = jax.sharding.Mesh(mesh.devices.reshape(owners, 2, QUAD), ("dp", "half", "quad"))
        space, on_device = ("half", "quad"), fast
    else:
        space, on_device = "space", general
    grid = P("dp", space, None, None, None)
    held = P(space, "dp", None, None, None)
    return jax.shard_map(
        on_device,
        mesh=mesh,
        in_specs=(grid, grid, held, held, held),
        out_specs=(grid, held, held, held),
        check_vma=False,
    )
```
